512 devices in a mesh: dp: 8 (over y, core), expert: 64 (over x, z).
Axes of the slice: x: 4, y: 4, z: 16, core: 2. Of those that a mesh axis runs over, the one named last changes fastest.
Arguments:
- tokens: bfloat16 [32768, 4096], P(('dp', 'expert')), parts along dimension 0, may hold values from -6 to 6
- routes: int32 [32768, 2], P(('dp', 'expert')), parts along dimension 0, may hold values from 0 to 7, all different within a row; in each aligned block of 64 rows (0 to 63, 64 to 127, ...) at most 20 rows name the same one
- numerators: int32 [32768, 2], P(('dp', 'expert')), parts along dimension 0, may hold values from 1 to 256
- counts: int32 [512], P(('dp', 'expert')), parts along dimension 0, may hold values from 32 to 64, as said below
- w_gate: bfloat16 [32768, 1024], P('expert'), may hold values from -0.09375 to 0.09375
- w_up: bfloat16 [32768, 1024], P('expert'), may hold values from -0.09375 to 0.09375
- w_down: bfloat16 [1024, 32768], P(None, 'expert'), may hold values from -0.1875 to 0.1875
Outputs:
- mixed: bfloat16 [32768, 4096], P(('dp', 'expert')), parts along dimension 0
The draws below stay inside these ranges and needn't reach their ends.
There are 8 independent parts, one for each index of `dp`. The reference program is written for one: setup_inputs(seed, part) draws one part's arguments, and reference() takes and returns one part's arrays. A program takes and returns all parts, laid end to end along the dimension named above; an argument that names none is the same for every part. Nothing has to cross between parts.
Inputs may be any that keep to these rules, and one draw needn't show every extreme that they name: `routes`: each row names 2 different experts. Among the 64 rows of one device no expert is named more than 20 times, and in every draw some device has an expert named exactly 20 times. Rows 0 to counts - 1 of a device are live, the others are ignored; some device is full in every draw.
All inputs are finite; a program needn't handle non-finite values.
Results may differ from the reference program's by a relative error of at most 0.027.
Values may be sent and summed in bfloat16 or wider, within the bound.
No kernel may reach another device: no remote copies, remote signals or barrier semaphores. Data moves between devices by JAX's collectives and lax.ppermute only.
A program may use at most 128 MiB of HBM per device.

```python
import math
import jax
import jax.numpy as jnp
import numpy as np
from jax import lax

D = 4096
F = 1024
BLOCK = 128
TOPK = 2
TOK_DEV = 64
E_IN = 8
CAP = 20
TOKENS = 4096
N_EXPERT = 64


def draw_counts(key, part):
    key = jax.random.fold_in(key, 7)
    first_key, second_key = jax.random.split(key)
    base_counts = jax.random.randint(first_key, (N_EXPERT,), TOK_DEV // 2, TOK_DEV + 1)
    full_device = jax.random.randint(second_key, (), 0, N_EXPERT)
    return jnp.where(jnp.arange(N_EXPERT) == full_device, TOK_DEV, base_counts).astype(jnp.int32)


def with_ends(drawn, rng, smallest, largest):
    longest = drawn.shape.index(max(drawn.shape))
    spots = []
    for shift in (0, 1):
        where = [jax.random.randint(jax.random.fold_in(rng, axis), (), 0, length) for axis, length in enumerate(drawn.shape)]
        where[longest] = (where[longest] + shift) % drawn.shape[longest]
        spots.append(tuple(where))
    return drawn.at[spots[0]].set(smallest).at[spots[1]].set(largest)


def block_levels(rng, extent, shards, least, high):
    def one(position, parts):
        steps = jax.random.uniform(jax.random.fold_in(jax.random.fold_in(rng, 6), position), (parts,), jnp.float32, least / len(shards), high / len(shards))
        return jnp.repeat(jnp.exp(steps), extent[position] // parts).reshape((-1,) + (1,) * (len(extent) - position - 1))

    factor_of = one(*shards[0])
    for cut in shards[1:]:
        factor_of = factor_of * one(*cut)
    return factor_of


def deal_out(rng, own, number, rows, number_of, top, limit, slope):
    order = jax.random.permutation(rng, number_of)
    crowded, ordinary = load_shares(number_of, rows * top, limit, slope, True), load_shares(number_of, rows * top, limit, slope, False)
    places = jnp.arange(number_of)

    def named(tallies, turn):
        used = int((tallies > 0).sum())
        fixed = max(1, used // 4)
        passed = fixed + (places - fixed + turn * (used - fixed)) % max(1, number_of - fixed)
        return jnp.zeros((number_of,), jnp.int32).at[order[jnp.where(places < fixed, places, passed)]].set(jnp.asarray(tallies, jnp.int32))

    tallies = jnp.where(number % 4 == 0, named(crowded, number // 4), named(ordinary, number - number // 4 - 1))
    mixed = jax.random.permutation(jax.random.fold_in(own, 3), number_of)
    source_of, receiver = mixed[0:number_of // 2 * 2:2], mixed[1:number_of // 2 * 2:2]
    room = jnp.minimum(tallies[source_of] - 1, limit - tallies[receiver]) // 2
    room = jnp.where((source_of == order[0]) | (receiver == order[0]) | (tallies[receiver] == 0), 0, jnp.maximum(room, 0))
    passed = jax.random.randint(jax.random.fold_in(own, 4), (number_of // 2,), 0, 1 << 20) % (room + 1)
    tallies = tallies.at[source_of].add(-passed).at[receiver].add(passed)
    labels = jnp.searchsorted(jnp.cumsum(tallies), jnp.arange(rows * top), side="right").astype(jnp.int32)
    table = labels.reshape(top, rows).T
    table = table[jax.random.permutation(jax.random.fold_in(own, 1), rows)]
    turn = jax.random.randint(jax.random.fold_in(own, 2), (rows, 1), 0, top)
    return jnp.take_along_axis(table, (jnp.arange(top)[None, :] + turn) % top, axis=1)


def load_shares(count, total, limit, lean, full):
    weights = [(1 << 20) // math.isqrt(standing ** lean) + 1 for standing in range(1, count + 1)]
    largest = limit if full else min(limit, max(-(-total // count), total * weights[0] // sum(weights)))
    least = 1 if total - largest >= count - 1 else 0
    given, rest = [largest] + [least] * (count - 1), total - largest - least * (count - 1)
    while rest > 0:
        candidates = [i for i in range(1, count) if given[i] < largest] or [i for i in range(1, count) if given[i] < limit]
        pool, left = sum([weights[i] for i in candidates]), rest
        for i in candidates:
            addition = min(limit - given[i], max(1, left * weights[i] // pool), rest)
            given[i] = given[i] + addition
            rest = rest - addition
    return np.array(given)


def scatter_about(key, shape, spread, bound, shards=(), kind=jnp.bfloat16):
    drawn = jax.random.normal(key, shape, jnp.float32) * spread
    if len(shards) > 0:
        drawn = block_levels(key, shape, shards, -0.22, 0.18) * drawn
    return jnp.clip(drawn, min=-bound, max=bound).astype(kind)


def setup_inputs(seed: int = 0, part: int = 0) -> dict:
    streams_of = jax.random.split(jax.random.key(seed), 8)
    part_keys = jax.random.split(jax.random.fold_in(streams_of[7], part), 8)
    tokens = scatter_about(part_keys[0], (TOKENS, D), 1.0, 6.0, ((0, 64),))
    routes_keys = jax.random.split(jax.random.fold_in(part_keys[1], 1), TOKENS // TOK_DEV)
    routes_turns = jax.random.permutation(jax.random.fold_in(part_keys[1], 3), TOKENS // TOK_DEV)
    routes = jax.vmap(lambda own, number: deal_out(jax.random.fold_in(part_keys[1], 2), own, number, TOK_DEV, E_IN, TOPK, CAP, 1))(routes_keys, routes_turns).reshape((TOKENS, TOPK))
    numerators = with_ends(jax.random.randint(part_keys[2], (TOKENS, TOPK), 1, 257), jax.random.fold_in(part_keys[2], 1), 1, 256).astype(jnp.int32)
    counts = draw_counts(jax.random.fold_in(jax.random.fold_in(streams_of[7], part), 71), part)
    w_gate = scatter_about(streams_of[4], (E_IN * D, F), D ** -0.5, 0.09375, ((0, 64),))
    w_up = scatter_about(streams_of[5], (E_IN * D, F), D ** -0.5, 0.09375, ((0, 64),))
    w_down = scatter_about(streams_of[6], (F, E_IN * D), F ** -0.5, 0.1875, ((1, 64),))
    return dict(tokens=tokens, routes=routes, numerators=numerators, counts=counts, w_gate=w_gate, w_up=w_up, w_down=w_down)


def snap_scaled(scaled):
    magnitude = jnp.abs(scaled)
    spacing = jnp.full_like(magnitude, 2.0 ** -9)
    for exponent in range(-5, 9):
        spacing = jnp.where(magnitude >= 2.0 ** exponent, 2.0 ** (exponent - 3), spacing)
    snapped = jnp.floor(magnitude / spacing + 0.5) * spacing
    return jnp.where(scaled < 0.0, -snapped, snapped)


def reference(tokens, routes, numerators, counts, w_gate, w_up, w_down):
    values = tokens.astype(jnp.float32).reshape(TOKENS, D // BLOCK, BLOCK)
    block_amax = jnp.max(jnp.abs(values), axis=2)
    block_scale = (block_amax + 1e-6) / 448.0
    coded = snap_scaled(values / block_scale[:, :, None]).astype(jnp.bfloat16)
    restored = (coded.astype(jnp.float32) * block_scale[:, :, None]).reshape(TOKENS, D).astype(jnp.bfloat16)
    row_place = jnp.arange(TOKENS, dtype=jnp.int32) % TOK_DEV
    row_owner = jnp.arange(TOKENS, dtype=jnp.int32) // TOK_DEV
    live_rows = row_place < counts[row_owner]
    slot_share = numerators.astype(jnp.float32) / 256.0
    gate_stack = w_gate.reshape(E_IN, D, F)
    up_stack = w_up.reshape(E_IN, D, F)
    down_stack = w_down.reshape(F, E_IN, D).transpose(1, 0, 2)
    most_rows = N_EXPERT * CAP

    def expert_step(running_sum, expert_item):
        number, gate_w, up_w, down_w = expert_item
        chosen = jnp.sum(jnp.where(routes == number, slot_share, jnp.zeros_like(slot_share)), axis=1)
        chosen = jnp.where(live_rows, chosen, jnp.zeros_like(chosen))
        used = jnp.sum((chosen > 0.0).astype(jnp.int32))
        picked = jnp.nonzero(chosen > 0.0, size=most_rows, fill_value=0)[0].astype(jnp.int32)
        valid = jnp.arange(most_rows, dtype=jnp.int32) < used
        picked_share = jnp.where(valid, chosen[picked], jnp.zeros_like(chosen[picked]))
        rows_in = restored[picked]
        gate_sum = jnp.dot(rows_in, gate_w, preferred_element_type=jnp.float32)
        up_sum = jnp.dot(rows_in, up_w, preferred_element_type=jnp.float32)
        hidden = (jax.nn.silu(gate_sum) * up_sum).astype(jnp.bfloat16)
        result = jnp.dot(hidden, down_w, preferred_element_type=jnp.float32)
        weighted = (result * picked_share[:, None]).astype(jnp.bfloat16)
        return running_sum.at[picked].add(weighted.astype(jnp.float32)), None

    numbers = jnp.arange(E_IN, dtype=jnp.int32)
    running_sum, _ = lax.scan(expert_step, jnp.zeros((TOKENS, D), jnp.float32), (numbers, gate_stack, up_stack, down_stack))
    return running_sum.astype(jnp.bfloat16)
```

```python
import functools

import jax
import jax.numpy as jnp
from jax import lax
from jax.experimental import pallas as pl
from jax.experimental.pallas import tpu as pltpu
from jax.sharding import Mesh
from jax.sharding import PartitionSpec as P

Y, C, X, Z = 4, 2, 4, 16
D, F, TOK = 4096, 1024, 64
SHARD = 512
MEMBERS = 8
CAP = 20
SLOTS = 2 * CAP
MAIN = 16
REST = SLOTS - 2 * MAIN
SRC = Y * X
ROWS = SRC * SLOTS
ALL_SLOTS = X * SLOTS
FQ = F // Y
HALF = SHARD // 2
VMEM = 100 * 1024 * 1024 // 2


def slot_layout(place):
    column = (place * 1639) >> 16
    at = place - column * SLOTS
    second = ((at >= MAIN) & (at < 2 * MAIN)) | (at >= 2 * MAIN + REST // 2)
    slot = jnp.where(at < MAIN, at, jnp.where(at < 2 * MAIN + REST // 2, at - MAIN, at - MAIN - REST // 2))
    return 2 * column + second.astype(jnp.int32), slot


def encode_kernel(core_ref, count_ref, routes_ref, tokens_ref, out_ref):
    core = core_ref[0]
    place = lax.broadcasted_iota(jnp.int32, (ALL_SLOTS, TOK), 0)
    row = lax.broadcasted_iota(jnp.int32, (ALL_SLOTS, TOK), 1)
    expert, slot = slot_layout(place)
    named = (routes_ref[0:1, :] == expert) | (routes_ref[1:2, :] == expert)
    named = named & (row < count_ref[0])
    earlier = lax.broadcasted_iota(jnp.int32, (TOK, TOK), 0) < lax.broadcasted_iota(jnp.int32, (TOK, TOK), 1)
    rank = jnp.dot(
        named.astype(jnp.float32).astype(jnp.bfloat16),
        earlier.astype(jnp.float32).astype(jnp.bfloat16),
        preferred_element_type=jnp.float32,
    )
    chosen = named & (rank.astype(jnp.int32) == slot)
    chosen = chosen.astype(jnp.float32).astype(jnp.bfloat16)

    def step(i, carry):
        half = i // MEMBERS
        member = i - half * MEMBERS
        side = jnp.where(half == 0, core, 1 - core)
        start = pl.multiple_of(member * SHARD + side * HALF, HALF)
        parts = []
        values = tokens_ref[:, pl.ds(start, HALF)].astype(jnp.float32)
        for block in range(HALF // 128):
            v = values[:, block * 128 : (block + 1) * 128]
            size = jnp.abs(v)
            scale = (jnp.max(size, axis=1, keepdims=True) + 1e-06) / 448.0
            scaled = v / scale
            x = jnp.abs(scaled)
            spacing = jnp.full_like(x, 2.0**-9)
            for shift, least in ((8, 2.0**2), (4, 2.0**-2), (2, 2.0**-4), (1, 2.0**-5)):
                big = x >= least
                x = jnp.where(big, x * 2.0**-shift, x)
                spacing = jnp.where(big, spacing * 2.0**shift, spacing)
            snapped = jnp.floor(x * 512.0 + 0.5) * spacing
            coded = jnp.where(scaled < 0.0, -snapped, snapped)
            parts.append((coded * scale).astype(jnp.bfloat16))
        restored = jnp.concatenate(parts, axis=1)
        rows = jnp.dot(chosen, restored, preferred_element_type=jnp.float32)
        out_ref[:, pl.ds(pl.multiple_of(i * HALF, HALF), HALF)] = rows.astype(jnp.bfloat16)
        return carry

    lax.fori_loop(0, 2 * MEMBERS, step, 0)


def shares_kernel(count_ref, routes_ref, numerators_ref, out_ref):
    place = lax.broadcasted_iota(jnp.int32, (TOK, ALL_SLOTS), 1)
    row = lax.broadcasted_iota(jnp.int32, (TOK, ALL_SLOTS), 0)
    expert, slot = slot_layout(place)
    live = row < count_ref[0]
    first = (routes_ref[:, 0:1] == expert) & live
    second = (routes_ref[:, 1:2] == expert) & live
    earlier = lax.broadcasted_iota(jnp.int32, (TOK, TOK), 1) < lax.broadcasted_iota(jnp.int32, (TOK, TOK), 0)
    rank = jnp.dot(
        earlier.astype(jnp.float32).astype(jnp.bfloat16),
        (first | second).astype(jnp.float32).astype(jnp.bfloat16),
        preferred_element_type=jnp.float32,
    )
    here = rank.astype(jnp.int32) == slot
    share = numerators_ref[...].astype(jnp.float32) / 256.0
    out = jnp.where(first & here, share[:, 0:1], 0.0) + jnp.where(second & here, share[:, 1:2], 0.0)
    out_ref[...] = out.astype(jnp.bfloat16)


def split_rows(block):
    wide = block.astype(jnp.float32)
    n = wide.shape[-1]
    mixed = wide[:, 2 * MAIN :].reshape(SRC * REST, n)
    return [
        jnp.concatenate([wide[:, e * MAIN : (e + 1) * MAIN].reshape(SRC * MAIN, n), mixed], axis=0).astype(jnp.bfloat16)
        for e in range(2)
    ]


def join_rows(first, second):
    n = first.shape[-1]
    main = SRC * MAIN
    place = lax.broadcasted_iota(jnp.int32, (SRC * REST, n), 0)
    mixed = jnp.where((place & (REST - 1)) < REST // 2, first[main:], second[main:])
    return jnp.concatenate(
        [first[:main].reshape(SRC, MAIN, n), second[:main].reshape(SRC, MAIN, n), mixed.reshape(SRC, REST, n)], axis=1
    )


def hidden_kernel(rows_ref, own_ref, other_ref, out_ref, first_sum, second_sum):
    step = pl.program_id(0)

    @pl.when(step == 0)
    def _():
        first_sum[...] = jnp.zeros_like(first_sum)
        second_sum[...] = jnp.zeros_like(second_sum)

    first, second = split_rows(rows_ref[...])

    def add(weights_ref):
        first_sum[...] += jnp.dot(first, weights_ref[0, 0], preferred_element_type=jnp.float32)
        second_sum[...] += jnp.dot(second, weights_ref[1, 0], preferred_element_type=jnp.float32)

    @pl.when(step < MEMBERS)
    def _():
        add(own_ref)

    @pl.when(step >= MEMBERS)
    def _():
        add(other_ref)

    @pl.when(step == 2 * MEMBERS - 1)
    def _():
        def hidden(total):
            gate = total[:, :FQ]
            return gate / (1.0 + jnp.exp(-gate)) * total[:, FQ:]

        out_ref[...] = join_rows(hidden(first_sum[...]), hidden(second_sum[...])).astype(jnp.bfloat16)


def down_kernel(core_ref, hidden_ref, own_ref, other_ref, out_ref, first_rows, second_rows):
    @pl.when(pl.program_id(0) == 0)
    def _():
        core = core_ref[0]
        for half in range(2):
            side = core if half == 0 else 1 - core
            for quarter in range(Y):
                first, second = split_rows(hidden_ref[quarter, :, :, pl.ds(pl.multiple_of(side * 128, 128), 128)])
                at = (half * Y + quarter) * 128
                first_rows[:, at : at + 128] = first
                second_rows[:, at : at + 128] = second

    def result(expert, rows):
        weights = jnp.concatenate(
            [
                jnp.concatenate([ref[expert, 0], ref[expert, 1]], axis=1)
                for ref in (own_ref, other_ref)
            ],
            axis=0,
        )
        return jnp.dot(rows[...], weights, preferred_element_type=jnp.float32)

    out_ref[...] = join_rows(result(0, first_rows), result(1, second_rows)).astype(jnp.bfloat16)


def mix_kernel(shares_ref, rows_ref, out_ref):
    for quarter in range(Y):
        rows = rows_ref[quarter * X : (quarter + 1) * X].reshape(ALL_SLOTS, MEMBERS * 128)
        mixed = jnp.dot(shares_ref[...], rows, preferred_element_type=jnp.float32).astype(jnp.bfloat16)
        for member in range(MEMBERS):
            at = member * SHARD + quarter * 128
            out_ref[:, at : at + 128] = mixed[:, member * 128 : (member + 1) * 128]


SCALAR = pl.BlockSpec(memory_space=pltpu.SMEM)
WHOLE = pl.BlockSpec(memory_space=pltpu.VMEM)


def shape(dims):
    return jax.ShapeDtypeStruct(dims, jnp.bfloat16)


def params(**extra):
    return pltpu.CompilerParams(vmem_limit_bytes=VMEM, **extra)


def encode(core, counts, routes, tokens):
    return pl.pallas_call(
        encode_kernel,
        out_shape=shape((ALL_SLOTS, D)),
        in_specs=[SCALAR, SCALAR, WHOLE, WHOLE],
        out_specs=WHOLE,
        compiler_params=params(),
        cost_estimate=pl.CostEstimate(flops=2 * ALL_SLOTS * TOK * D, bytes_accessed=2 * (TOK + ALL_SLOTS) * D, transcendentals=0),
    )(core, counts, routes.T, tokens)


def share_table(counts, routes, numerators):
    return pl.pallas_call(
        shares_kernel,
        out_shape=shape((TOK, ALL_SLOTS)),
        in_specs=[SCALAR, WHOLE, WHOLE],
        out_specs=WHOLE,
    )(counts, routes, numerators)


def hidden_rows(rows, own, other):
    last = MEMBERS - 1
    return pl.pallas_call(
        hidden_kernel,
        grid=(2 * MEMBERS,),
        out_shape=shape((SRC, SLOTS, FQ)),
        in_specs=[
            pl.BlockSpec((SRC, SLOTS, HALF), lambda k: (0, 0, k)),
            pl.BlockSpec((2, 1, HALF, 2 * FQ), lambda k: (0, jnp.minimum(k, last), 0, 0)),
            pl.BlockSpec((2, 1, HALF, 2 * FQ), lambda k: (0, jnp.maximum(k - MEMBERS, 0), 0, 0)),
        ],
        out_specs=pl.BlockSpec((SRC, SLOTS, FQ), lambda k: (0, 0, 0)),
        scratch_shapes=[pltpu.VMEM((SRC * (MAIN + REST), 2 * FQ), jnp.float32)] * 2,
        compiler_params=params(),
        cost_estimate=pl.CostEstimate(flops=2 * ROWS * D * 2 * FQ, bytes_accessed=2 * ROWS * D + 8 * D * FQ, transcendentals=0),
    )(rows, own, other)


def down_rows(core, hidden, own, other):
    weights = pl.BlockSpec((2, 2, F // 2, 128), lambda n: (0, n, 0, 0))
    return pl.pallas_call(
        down_kernel,
        grid=(MEMBERS // 2,),
        out_shape=shape((SRC, SLOTS, MEMBERS * 128)),
        in_specs=[
            SCALAR,
            pl.BlockSpec((Y, SRC, SLOTS, FQ), lambda n: (0, 0, 0, 0)),
            weights,
            weights,
        ],
        out_specs=pl.BlockSpec((SRC, SLOTS, 256), lambda n: (0, 0, n)),
        scratch_shapes=[pltpu.VMEM((SRC * (MAIN + REST), F), jnp.bfloat16)] * 2,
        compiler_params=params(),
        cost_estimate=pl.CostEstimate(flops=2 * ROWS * F * F, bytes_accessed=2 * ROWS * F * 2 + 4 * F * F, transcendentals=0),
    )(core, hidden, own, other)


def mix(shares, rows):
    return pl.pallas_call(
        mix_kernel,
        out_shape=shape((TOK, D)),
        in_specs=[WHOLE, WHOLE],
        out_specs=WHOLE,
        compiler_params=params(),
    )(shares, rows)


def swap_cores(block):
    return lax.ppermute(block, "c", [(0, 1), (1, 0)])


def local(tokens, routes, numerators, counts, w_gate, w_up, w_down):
    y, c = lax.axis_index("y"), lax.axis_index("c")
    core = c.astype(jnp.int32).reshape(1)
    gate = lax.dynamic_slice(w_gate, (c * HALF, y * FQ), (HALF, FQ))
    up = lax.dynamic_slice(w_up, (c * HALF, y * FQ), (HALF, FQ))
    down = lax.dynamic_slice(w_down.reshape(Y, 2, 128, SHARD), (0, c, 0, y * 128), (Y, 1, 128, 128))
    own_in = lax.all_gather(jnp.concatenate([gate, up], axis=1), "z").reshape(2, MEMBERS, HALF, 2 * FQ)
    other_in = swap_cores(own_in)
    own_out = lax.all_gather(down.reshape(F // 2, 128), "z").reshape(2, MEMBERS, F // 2, 128)
    other_out = swap_cores(own_out)
    shares = share_table(counts, routes, numerators)
    rows = encode(core, counts, routes, tokens).reshape(X, SLOTS, D)
    rows = lax.all_to_all(rows, "x", 0, 0, tiled=True)
    rows = lax.all_gather(rows, "y").reshape(SRC, SLOTS, D)
    hidden = hidden_rows(rows, own_in, other_in)
    hidden = lax.all_gather(hidden, "y")
    result = down_rows(core, hidden, own_out, other_out)
    result = lax.all_to_all(result, ("y", "x"), 0, 0, tiled=True)
    return mix(shares, result)


def solution(mesh):
    grid = Mesh(mesh.devices.reshape(Y, C, X, Z), ("y", "c", "x", "z"))
    tokens = ("y", "c", "x", "z")
    group = ("x", "z")
    placed = (
        P(tokens, None),
        P(tokens, None),
        P(tokens, None),
        P(tokens),
        P(group, None),
        P(group, None),
        P(None, group),
    )
    return jax.shard_map(local, mesh=grid, in_specs=placed, out_specs=P(tokens, None), check_vma=False)
```

```python
import functools

import jax
import jax.numpy as jnp
from jax import lax
from jax.experimental import pallas as pl
from jax.experimental.pallas import tpu as pltpu
from jax.sharding import Mesh
from jax.sharding import PartitionSpec as P

Y, C, X, Z = 4, 2, 4, 16
D, F, TOK = 4096, 1024, 64
SHARD = 512
MEMBERS = 8
CAP = 20
SLOTS = 2 * CAP
MAIN = 16
REST = SLOTS - 2 * MAIN
SRC = Y * X
ROWS = SRC * SLOTS
ALL_SLOTS = X * SLOTS
FQ = F // Y
HALF = SHARD // 2
DEEP = 2
OFFSETS = (0, 1, 2, 3)
VMEM = 100 * 1024 * 1024 // 2


def slot_layout(place):
    column = (place * 1639) >> 16
    at = place - column * SLOTS
    second = ((at >= MAIN) & (at < 2 * MAIN)) | (at >= 2 * MAIN + REST // 2)
    slot = jnp.where(at < MAIN, at, jnp.where(at < 2 * MAIN + REST // 2, at - MAIN, at - MAIN - REST // 2))
    return 2 * column + second.astype(jnp.int32), slot


def restore(v):
    scale = (jnp.max(jnp.abs(v), axis=1, keepdims=True) + 1e-06) / 448.0
    scaled = v / scale
    x = jnp.abs(scaled)
    spacing = jnp.full_like(x, 2.0**-9)
    for shift, least in ((8, 2.0**2), (4, 2.0**-2), (2, 2.0**-4), (1, 2.0**-5)):
        big = x >= least
        x = jnp.where(big, x * 2.0**-shift, x)
        spacing = jnp.where(big, spacing * 2.0**shift, spacing)
    snapped = jnp.floor(x * 512.0 + 0.5) * spacing
    coded = jnp.where(scaled < 0.0, -snapped, snapped)
    return (coded * scale).astype(jnp.bfloat16)


def encode_kernel(count_ref, routes_ref, tokens_ref, first_ref, second_ref):
    place = lax.broadcasted_iota(jnp.int32, (ALL_SLOTS, TOK), 0)
    row = lax.broadcasted_iota(jnp.int32, (ALL_SLOTS, TOK), 1)
    expert, slot = slot_layout(place)
    named = (routes_ref[0:1, :] == expert) | (routes_ref[1:2, :] == expert)
    named = named & (row < count_ref[0])
    earlier = lax.broadcasted_iota(jnp.int32, (TOK, TOK), 0) < lax.broadcasted_iota(jnp.int32, (TOK, TOK), 1)
    rank = jnp.dot(
        named.astype(jnp.float32).astype(jnp.bfloat16),
        earlier.astype(jnp.float32).astype(jnp.bfloat16),
        preferred_element_type=jnp.float32,
    )
    chosen = named & (rank.astype(jnp.int32) == slot)
    chosen = chosen.astype(jnp.float32).astype(jnp.bfloat16)

    def step(member, carry):
        for half, out_ref in enumerate((first_ref, second_ref)):
            start = pl.multiple_of(member * SHARD + half * HALF, HALF)
            values = tokens_ref[:, pl.ds(start, HALF)].astype(jnp.float32)
            restored = jnp.concatenate([restore(values[:, b * 128 : (b + 1) * 128]) for b in range(HALF // 128)], axis=1)
            rows = jnp.dot(chosen, restored, preferred_element_type=jnp.float32)
            out_ref[:, pl.ds(pl.multiple_of(member * HALF, HALF), HALF)] = rows.astype(jnp.bfloat16)
        return carry

    lax.fori_loop(0, MEMBERS, step, 0)


def shares_kernel(count_ref, routes_ref, numerators_ref, out_ref):
    place = lax.broadcasted_iota(jnp.int32, (TOK, ALL_SLOTS), 1)
    row = lax.broadcasted_iota(jnp.int32, (TOK, ALL_SLOTS), 0)
    expert, slot = slot_layout(place)
    live = row < count_ref[0]
    first = (routes_ref[:, 0:1] == expert) & live
    second = (routes_ref[:, 1:2] == expert) & live
    earlier = lax.broadcasted_iota(jnp.int32, (TOK, TOK), 1) < lax.broadcasted_iota(jnp.int32, (TOK, TOK), 0)
    rank = jnp.dot(
        earlier.astype(jnp.float32).astype(jnp.bfloat16),
        (first | second).astype(jnp.float32).astype(jnp.bfloat16),
        preferred_element_type=jnp.float32,
    )
    here = rank.astype(jnp.int32) == slot
    share = numerators_ref[...].astype(jnp.float32) / 256.0
    out = jnp.where(first & here, share[:, 0:1], 0.0) + jnp.where(second & here, share[:, 1:2], 0.0)
    out_ref[...] = out.astype(jnp.bfloat16)


def split_rows(block):
    wide = block.astype(jnp.float32)
    n = wide.shape[-1]
    mixed = wide[:, 2 * MAIN :].reshape(SRC * REST, n)
    return [
        jnp.concatenate([wide[:, e * MAIN : (e + 1) * MAIN].reshape(SRC * MAIN, n), mixed], axis=0).astype(jnp.bfloat16)
        for e in range(2)
    ]


def join_rows(first, second):
    n = first.shape[-1]
    main = SRC * MAIN
    place = lax.broadcasted_iota(jnp.int32, (SRC * REST, n), 0)
    mixed = jnp.where((place & (REST - 1)) < REST // 2, first[main:], second[main:])
    return jnp.concatenate(
        [first[:main].reshape(SRC, MAIN, n), second[:main].reshape(SRC, MAIN, n), mixed.reshape(SRC, REST, n)], axis=1
    )


def hidden_kernel(place_ref, *refs):
    rows, weights_ref, out_ref, first_sum, second_sum = refs[:8], refs[8], refs[9], refs[10], refs[11]
    step = pl.program_id(0)

    @pl.when(step == 0)
    def _():
        first_sum[...] = jnp.zeros_like(first_sum)
        second_sum[...] = jnp.zeros_like(second_sum)

    def add(parts):
        first, second = split_rows(jnp.concatenate([ref[...] for ref in parts], axis=0))
        for expert, (block, total) in enumerate(((first, first_sum), (second, second_sum))):
            weights = jnp.concatenate([weights_ref[expert, m, 0] for m in range(DEEP)], axis=0)
            total[...] += jnp.dot(block, weights, preferred_element_type=jnp.float32)

    @pl.when(step < MEMBERS // DEEP)
    def _():
        add(rows[0::2])

    @pl.when(step >= MEMBERS // DEEP)
    def _():
        add(rows[1::2])

    @pl.when(step == 2 * MEMBERS // DEEP - 1)
    def _():
        def hidden(total):
            gate = total[:, :FQ]
            return gate / (1.0 + jnp.exp(-gate)) * total[:, FQ:]

        joined = join_rows(hidden(first_sum[...]), hidden(second_sum[...])).astype(jnp.bfloat16)
        for i, offset in enumerate(OFFSETS):
            source = lax.rem(place_ref[0] + offset, Y)
            block = joined[i * X : (i + 1) * X]
            for copy in range(Y):
                out_ref[copy, pl.ds(source * X, X)] = block


def down_kernel(hidden_ref, weights_ref, out_ref, first_rows, second_rows):
    @pl.when(pl.program_id(0) == 0)
    def _():
        for quarter in range(Y):
            first, second = split_rows(hidden_ref[quarter])
            first_rows[:, quarter * FQ : (quarter + 1) * FQ] = first
            second_rows[:, quarter * FQ : (quarter + 1) * FQ] = second

    def result(expert, rows):
        weights = jnp.concatenate(
            [
                jnp.concatenate([weights_ref[expert, m, half, :, q * 128 : (q + 1) * 128] for m in range(2)], axis=1)
                for q in range(Y)
                for half in range(C)
            ],
            axis=0,
        )
        return jnp.dot(rows[...], weights, preferred_element_type=jnp.float32)

    out_ref[...] = join_rows(result(0, first_rows), result(1, second_rows)).astype(jnp.bfloat16)


def mix_kernel(shares_ref, rows_ref, out_ref):
    for quarter in range(Y):
        rows = rows_ref[quarter * X : (quarter + 1) * X].reshape(ALL_SLOTS, MEMBERS * 128)
        mixed = jnp.dot(shares_ref[...], rows, preferred_element_type=jnp.float32).astype(jnp.bfloat16)
        for member in range(MEMBERS):
            at = member * SHARD + quarter * 128
            out_ref[:, at : at + 128] = mixed[:, member * 128 : (member + 1) * 128]


SCALAR = pl.BlockSpec(memory_space=pltpu.SMEM)
WHOLE = pl.BlockSpec(memory_space=pltpu.VMEM)


def shape(dims):
    return jax.ShapeDtypeStruct(dims, jnp.bfloat16)


def params(**extra):
    return pltpu.CompilerParams(vmem_limit_bytes=VMEM, **extra)


def encode(counts, routes, tokens):
    return pl.pallas_call(
        encode_kernel,
        out_shape=[shape((ALL_SLOTS, D // 2))] * 2,
        in_specs=[SCALAR, WHOLE, WHOLE],
        out_specs=[WHOLE] * 2,
        compiler_params=params(),
        cost_estimate=pl.CostEstimate(flops=2 * ALL_SLOTS * TOK * D, bytes_accessed=2 * (TOK + ALL_SLOTS) * D, transcendentals=0),
    )(counts, routes.T, tokens)


def share_table(counts, routes, numerators):
    return pl.pallas_call(
        shares_kernel,
        out_shape=shape((TOK, ALL_SLOTS)),
        in_specs=[SCALAR, WHOLE, WHOLE],
        out_specs=WHOLE,
    )(counts, routes, numerators)


def hidden_rows(place, rows, weights):
    steps = MEMBERS // DEEP
    first = pl.BlockSpec((X, SLOTS, DEEP * HALF), lambda k: (0, 0, jnp.minimum(k, steps - 1)))
    second = pl.BlockSpec((X, SLOTS, DEEP * HALF), lambda k: (0, 0, jnp.maximum(k - steps, 0)))
    return pl.pallas_call(
        hidden_kernel,
        grid=(2 * steps,),
        out_shape=shape((Y, SRC, SLOTS, FQ)),
        in_specs=[
            SCALAR,
            *[first, second] * Y,
            pl.BlockSpec((2, DEEP, 1, HALF, 2 * FQ), lambda k: (0, lax.rem(k, steps), k // steps, 0, 0)),
        ],
        out_specs=pl.BlockSpec((Y, SRC, SLOTS, FQ), lambda k: (0, 0, 0, 0)),
        scratch_shapes=[pltpu.VMEM((SRC * (MAIN + REST), 2 * FQ), jnp.float32)] * 2,
        compiler_params=params(),
        cost_estimate=pl.CostEstimate(flops=2 * ROWS * D * 2 * FQ, bytes_accessed=2 * ROWS * D + 8 * D * FQ, transcendentals=0),
    )(place, *rows, weights)


def down_rows(hidden, weights):
    return pl.pallas_call(
        down_kernel,
        grid=(MEMBERS // 2,),
        out_shape=shape((SRC, SLOTS, MEMBERS * 128)),
        in_specs=[
            pl.BlockSpec((Y, SRC, SLOTS, FQ), lambda n: (0, 0, 0, 0)),
            pl.BlockSpec((2, 2, C, 128, SHARD), lambda n: (0, n, 0, HALF // 128, 0)),
        ],
        out_specs=pl.BlockSpec((SRC, SLOTS, 256), lambda n: (0, 0, n)),
        scratch_shapes=[pltpu.VMEM((SRC * (MAIN + REST), F), jnp.bfloat16)] * 2,
        compiler_params=params(),
        cost_estimate=pl.CostEstimate(flops=2 * ROWS * F * F, bytes_accessed=2 * ROWS * F * 2 + 4 * F * F, transcendentals=0),
    )(hidden, weights)


def mix(shares, rows):
    return pl.pallas_call(
        mix_kernel,
        out_shape=shape((TOK, D)),
        in_specs=[WHOLE, WHOLE],
        out_specs=WHOLE,
        compiler_params=params(),
    )(shares, rows)


def shift(block, by):
    return lax.ppermute(block, "y", [(i, (i + by) % Y) for i in range(Y)])


def local(tokens, routes, numerators, counts, w_gate, w_up, w_down):
    y, c = lax.axis_index("y"), lax.axis_index("c")
    gate = lax.dynamic_slice(w_gate, (c * HALF, y * FQ), (HALF, FQ))
    up = lax.dynamic_slice(w_up, (c * HALF, y * FQ), (HALF, FQ))
    down = lax.dynamic_slice(w_down.reshape(Y, C, 128, SHARD), (0, c, 0, y * 128), (Y, 1, 128, 128))
    down = jnp.concatenate([down[q, 0] for q in range(Y)], axis=1)
    weights = jnp.concatenate([jnp.concatenate([gate, up], axis=1), down], axis=0)
    weights = lax.all_gather(weights, ("z", "c")).reshape(2, MEMBERS, C, HALF + 128, SHARD)
    shares = share_table(counts, routes, numerators)
    first, second = encode(counts, routes, tokens)
    first = lax.all_to_all(first.reshape(X, SLOTS, D // 2), "x", 0, 0, tiled=True)
    second = lax.all_to_all(second.reshape(X, SLOTS, D // 2), "x", 0, 0, tiled=True)
    first_3, second_1 = shift(first, 1), shift(second, -1)
    second_3, first_1 = shift(second, 1), shift(first, -1)
    first_2, second_2 = shift(first_3, 1), shift(second_1, -1)
    rows = (first, second, first_1, second_1, first_2, second_2, first_3, second_3)
    place = y.astype(jnp.int32).reshape(1)
    hidden = hidden_rows(place, rows, weights)
    hidden = lax.all_to_all(hidden, "y", 0, 0, tiled=True)
    result = down_rows(hidden, weights)
    result = lax.all_to_all(result, ("y", "x"), 0, 0, tiled=True)
    return mix(shares, result)


def solution(mesh):
    grid = Mesh(mesh.devices.reshape(Y, C, X, Z), ("y", "c", "x", "z"))
    tokens = ("y", "c", "x", "z")
    group = ("x", "z")
    placed = (
        P(tokens, None),
        P(tokens, None),
        P(tokens, None),
        P(tokens),
        P(group, None),
        P(group, None),
        P(None, group),
    )
    return jax.shard_map(local, mesh=grid, in_specs=placed, out_specs=P(tokens, None), check_vma=False)
```

```python
import functools

import jax
import jax.numpy as jnp
from jax import lax
from jax.experimental import pallas as pl
from jax.experimental.pallas import tpu as pltpu
from jax.sharding import Mesh
from jax.sharding import PartitionSpec as P

Y, C, X, Z = 4, 2, 4, 16
D, F, TOK = 4096, 1024, 64
SHARD = 512
MEMBERS = 8
CAP = 20
SLOTS = 2 * CAP
MAIN = 16
REST = SLOTS - 2 * MAIN
LEAD = MAIN + REST
SRC = Y * X
ROWS = SRC * SLOTS
ALL_SLOTS = X * SLOTS
FQ = F // Y
HALF = SHARD // 2
DEEP = 4
VMEM = 100 * 1024 * 1024 // 2


def slot_at(at):
    second = (at >= MAIN + REST // 2).astype(jnp.int32)
    slot = jnp.where(at < MAIN + REST // 2, at, jnp.where(at < LEAD, at - REST // 2, at - LEAD))
    return second, slot


def pack_kernel(place_ref, gate_ref, up_ref, *refs):
    out_ref = refs[Y]
    out_ref[:HALF, :FQ] = gate_ref[...]
    out_ref[:HALF, FQ:] = up_ref[...]
    for quarter in range(Y):
        out_ref[HALF:, quarter * 128 : (quarter + 1) * 128] = refs[quarter][...]


def restore(v):
    scale = (jnp.max(jnp.abs(v), axis=1, keepdims=True) + 1e-06) / 448.0
    scaled = v / scale
    x = jnp.abs(scaled)
    spacing = jnp.full_like(x, 2.0**-9)
    for shift, least in ((8, 2.0**2), (4, 2.0**-2), (2, 2.0**-4), (1, 2.0**-5)):
        big = x >= least
        x = jnp.where(big, x * 2.0**-shift, x)
        spacing = jnp.where(big, spacing * 2.0**shift, spacing)
    snapped = jnp.floor(x * 512.0 + 0.5) * spacing
    coded = jnp.where(scaled < 0.0, -snapped, snapped)
    return (coded * scale).astype(jnp.bfloat16)


def encode_kernel(count_ref, routes_ref, tokens_ref, first_ref, second_ref):
    place = lax.broadcasted_iota(jnp.int32, (ALL_SLOTS, TOK), 0)
    row = lax.broadcasted_iota(jnp.int32, (ALL_SLOTS, TOK), 1)
    column = (place * 1639) >> 16
    second, slot = slot_at(place - column * SLOTS)
    expert = 2 * column + second
    named = (routes_ref[0:1, :] == expert) | (routes_ref[1:2, :] == expert)
    named = named & (row < count_ref[0])
    earlier = lax.broadcasted_iota(jnp.int32, (TOK, TOK), 0) < lax.broadcasted_iota(jnp.int32, (TOK, TOK), 1)
    rank = jnp.dot(
        named.astype(jnp.float32).astype(jnp.bfloat16),
        earlier.astype(jnp.float32).astype(jnp.bfloat16),
        preferred_element_type=jnp.float32,
    )
    chosen = named & (rank.astype(jnp.int32) == slot)
    chosen = chosen.astype(jnp.float32).astype(jnp.bfloat16)

    def step(member, carry):
        for half, out_ref in enumerate((first_ref, second_ref)):
            start = pl.multiple_of(member * SHARD + half * HALF, HALF)
            values = tokens_ref[:, pl.ds(start, HALF)].astype(jnp.float32)
            restored = jnp.concatenate([restore(values[:, b * 128 : (b + 1) * 128]) for b in range(HALF // 128)], axis=1)
            rows = jnp.dot(chosen, restored, preferred_element_type=jnp.float32)
            out_ref[:, pl.ds(pl.multiple_of(member * HALF, HALF), HALF)] = rows.astype(jnp.bfloat16)
        return carry

    lax.fori_loop(0, MEMBERS, step, 0)


def shares_kernel(count_ref, routes_ref, numerators_ref, lead_ref, last_ref):
    share = numerators_ref[...].astype(jnp.float32) / 256.0
    earlier = lax.broadcasted_iota(jnp.int32, (TOK, TOK), 1) < lax.broadcasted_iota(jnp.int32, (TOK, TOK), 0)
    earlier = earlier.astype(jnp.float32).astype(jnp.bfloat16)
    for out_ref, start, length in ((lead_ref, 0, LEAD), (last_ref, LEAD, MAIN)):
        dims = (TOK, X * length)
        place = lax.broadcasted_iota(jnp.int32, dims, 1)
        column = sum((place >= i * length).astype(jnp.int32) for i in range(1, X))
        second, slot = slot_at(place - column * length + start)
        expert = 2 * column + second
        live = lax.broadcasted_iota(jnp.int32, dims, 0) < count_ref[0]
        by_first = (routes_ref[:, 0:1] == expert) & live
        by_second = (routes_ref[:, 1:2] == expert) & live
        named = (by_first | by_second).astype(jnp.float32).astype(jnp.bfloat16)
        rank = jnp.dot(earlier, named, preferred_element_type=jnp.float32)
        here = rank.astype(jnp.int32) == slot
        out = jnp.where(by_first & here, share[:, 0:1], 0.0) + jnp.where(by_second & here, share[:, 1:2], 0.0)
        out_ref[...] = out.astype(jnp.bfloat16)


def run_of(block, start, length):
    n = block.shape[-1]
    return block[:, start : start + length].astype(jnp.float32).reshape(-1, n).astype(jnp.bfloat16)


def mixed_rows(first, second):
    place = lax.broadcasted_iota(jnp.int32, first.shape, 0)
    return jnp.where((place & (REST - 1)) < REST // 2, first, second)


def sources(rows, length):
    return rows.reshape(-1, length, rows.shape[-1])


def swish(total):
    gate = total[:, :FQ]
    return gate / (1.0 + jnp.exp(-gate)) * total[:, FQ:]


def hidden_kernel(lead, place_ref, *refs):
    rows, weights_ref, out_ref, sums = refs[: 2 * Y], refs[2 * Y], refs[2 * Y + 1], refs[2 * Y + 2 :]
    steps = MEMBERS // DEEP
    step = pl.program_id(0)

    def add(parts, start):
        blocks = [ref[...] for ref in parts]
        if lead:
            mixed = [run_of(b, MAIN, REST) for b in blocks]
            groups = [[run_of(b, 0, MAIN) for b in blocks] + mixed, mixed]
        else:
            groups = [[run_of(b, LEAD, MAIN) for b in blocks]]
        for expert, (group, total) in enumerate(zip(groups, sums)):
            weights = jnp.concatenate([weights_ref[expert, m, 0] for m in range(DEEP)], axis=0)
            product = jnp.dot(jnp.concatenate(group, axis=0), weights, preferred_element_type=jnp.float32)
            total[...] = product if start else total[...] + product

    @pl.when(step == 0)
    def _():
        add(rows[0::2], True)

    @pl.when((step > 0) & (step < steps))
    def _():
        add(rows[0::2], False)

    @pl.when(step >= steps)
    def _():
        add(rows[1::2], False)

    @pl.when(step == 2 * steps - 1)
    def _():
        first = swish(sums[0][...])
        if lead:
            main = SRC * MAIN
            mixed = mixed_rows(first[main:], swish(sums[1][...]))
            joined = jnp.concatenate([sources(first[:main], MAIN), sources(mixed, REST)], axis=1)
        else:
            joined = sources(first, MAIN)
        joined = joined.astype(jnp.bfloat16)
        for offset in range(Y):
            source = lax.rem(place_ref[0] + offset, Y)
            block = joined[offset * X : (offset + 1) * X]
            for copy in range(Y):
                out_ref[copy, pl.ds(source * X, X)] = block


def down_kernel(lead, hidden_ref, weights_ref, out_ref, rows):
    main = SRC * MAIN

    @pl.when(pl.program_id(0) == 0)
    def _():
        for quarter in range(Y):
            block = hidden_ref[quarter]
            at = slice(quarter * FQ, (quarter + 1) * FQ)
            rows[:main, at] = run_of(block, 0, MAIN)
            if lead:
                rows[main:, at] = run_of(block, MAIN, REST)

    def result(expert, part):
        weights = jnp.concatenate(
            [
                jnp.concatenate([weights_ref[expert, m, half, :, q * 128 : (q + 1) * 128] for m in range(2)], axis=1)
                for q in range(Y)
                for half in range(C)
            ],
            axis=0,
        )
        return jnp.dot(part, weights, preferred_element_type=jnp.float32)

    first = result(0, rows[...])
    if lead:
        mixed = mixed_rows(first[main:], result(1, rows[main:]))
        first = jnp.concatenate([sources(first[:main], MAIN), sources(mixed, REST)], axis=1)
    else:
        first = sources(first, MAIN)
    out_ref[...] = first.astype(jnp.bfloat16)


def mix_kernel(lead_shares_ref, last_shares_ref, lead_ref, last_ref, out_ref):
    for quarter in range(Y):
        mixed = 0.0
        for shares_ref, ref in ((lead_shares_ref, lead_ref), (last_shares_ref, last_ref)):
            block = ref[quarter * X : (quarter + 1) * X]
            rows = block.reshape(-1, block.shape[-1])
            mixed += jnp.dot(shares_ref[...], rows, preferred_element_type=jnp.float32)
        mixed = mixed.astype(jnp.bfloat16)
        for member in range(MEMBERS):
            at = member * SHARD + quarter * 128
            out_ref[:, at : at + 128] = mixed[:, member * 128 : (member + 1) * 128]


SCALAR = pl.BlockSpec(memory_space=pltpu.SMEM)
WHOLE = pl.BlockSpec(memory_space=pltpu.VMEM)


def shape(dims):
    return jax.ShapeDtypeStruct(dims, jnp.bfloat16)


def params(**extra):
    return pltpu.CompilerParams(vmem_limit_bytes=VMEM, **extra)


def encode(counts, routes, tokens):
    return pl.pallas_call(
        encode_kernel,
        out_shape=[shape((ALL_SLOTS, D // 2))] * 2,
        in_specs=[SCALAR, WHOLE, WHOLE],
        out_specs=[WHOLE] * 2,
        compiler_params=params(),
        cost_estimate=pl.CostEstimate(flops=2 * ALL_SLOTS * TOK * D, bytes_accessed=2 * (TOK + ALL_SLOTS) * D, transcendentals=0),
    )(counts, routes.T, tokens)


def pack(place, w_gate, w_up, w_down):
    quarters = [pl.BlockSpec((128, 128), lambda i, p, q=q: (C * q + p[1], p[0])) for q in range(Y)]
    return pl.pallas_call(
        pack_kernel,
        out_shape=shape((HALF + 128, SHARD)),
        grid_spec=pltpu.PrefetchScalarGridSpec(
            num_scalar_prefetch=1,
            grid=(1,),
            in_specs=[pl.BlockSpec((HALF, FQ), lambda i, p: (p[1], p[0]))] * 2 + quarters,
            out_specs=pl.BlockSpec((HALF + 128, SHARD), lambda i, p: (0, 0)),
        ),
    )(place, w_gate, w_up, *[w_down] * Y)


def share_tables(counts, routes, numerators):
    return pl.pallas_call(
        shares_kernel,
        out_shape=[shape((TOK, X * LEAD)), shape((TOK, X * MAIN))],
        in_specs=[SCALAR, WHOLE, WHOLE],
        out_specs=[WHOLE] * 2,
    )(counts, routes, numerators)


def hidden_rows(lead, place, rows, weights):
    steps = MEMBERS // DEEP
    length = LEAD if lead else MAIN
    experts = 2 if lead else 1
    first = pl.BlockSpec((X, SLOTS, DEEP * HALF), lambda k: (0, 0, jnp.minimum(k, steps - 1)))
    second = pl.BlockSpec((X, SLOTS, DEEP * HALF), lambda k: (0, 0, jnp.maximum(k - steps, 0)))
    sums = [pltpu.VMEM((SRC * length, 2 * FQ), jnp.float32)]
    if lead:
        sums += [pltpu.VMEM((SRC * REST, 2 * FQ), jnp.float32)]
    return pl.pallas_call(
        functools.partial(hidden_kernel, lead),
        grid=(2 * steps,),
        out_shape=shape((Y, SRC, length, FQ)),
        in_specs=[
            SCALAR,
            *[first, second] * Y,
            pl.BlockSpec((experts, DEEP, 1, HALF, 2 * FQ), lambda k: (2 - experts, lax.rem(k, steps), k // steps, 0, 0)),
        ],
        out_specs=pl.BlockSpec((Y, SRC, length, FQ), lambda k: (0, 0, 0, 0)),
        scratch_shapes=sums,
        compiler_params=params(),
        cost_estimate=pl.CostEstimate(flops=2 * SRC * length * D * 2 * FQ, bytes_accessed=2 * ROWS * D + 4 * experts * D * FQ, transcendentals=0),
    )(place, *rows, weights)


def down_rows(lead, hidden, weights):
    length = LEAD if lead else MAIN
    experts = 2 if lead else 1
    return pl.pallas_call(
        functools.partial(down_kernel, lead),
        grid=(MEMBERS // 2,),
        out_shape=shape((SRC, length, MEMBERS * 128)),
        in_specs=[
            pl.BlockSpec((Y, SRC, length, FQ), lambda n: (0, 0, 0, 0)),
            pl.BlockSpec((experts, 2, C, 128, SHARD), lambda n: (2 - experts, n, 0, HALF // 128, 0)),
        ],
        out_specs=pl.BlockSpec((SRC, length, 256), lambda n: (0, 0, n)),
        scratch_shapes=[pltpu.VMEM((SRC * length, F), jnp.bfloat16)],
        compiler_params=params(),
        cost_estimate=pl.CostEstimate(flops=2 * SRC * length * F * F, bytes_accessed=4 * SRC * length * F + 2 * experts * F * F, transcendentals=0),
    )(hidden, weights)


def mix(shares, rows):
    return pl.pallas_call(
        mix_kernel,
        out_shape=shape((TOK, D)),
        in_specs=[WHOLE] * 4,
        out_specs=WHOLE,
        compiler_params=params(),
    )(*shares, *rows)


def shift(block, by):
    return lax.ppermute(block, "y", [(i, (i + by) % Y) for i in range(Y)])


def local(tokens, routes, numerators, counts, w_gate, w_up, w_down):
    place = jnp.stack([lax.axis_index("y"), lax.axis_index("c")]).astype(jnp.int32)
    weights = pack(place, w_gate, w_up, w_down)
    weights = lax.all_gather(weights, ("z", "c")).reshape(2, MEMBERS, C, HALF + 128, SHARD)
    shares = share_tables(counts, routes, numerators)
    first, second = encode(counts, routes, tokens)
    first = lax.all_to_all(first.reshape(X, SLOTS, D // 2), "x", 0, 0, tiled=True)
    second = lax.all_to_all(second.reshape(X, SLOTS, D // 2), "x", 0, 0, tiled=True)
    first_3, second_1 = shift(first, 1), shift(second, -1)
    second_3, first_1 = shift(second, 1), shift(first, -1)
    first_2, second_2 = shift(first_3, 1), shift(second_1, -1)
    rows = (first, second, first_1, second_1, first_2, second_2, first_3, second_3)
    results = []
    for lead in (True, False):
        hidden = hidden_rows(lead, place, rows, weights)
        hidden = lax.all_to_all(hidden, "y", 0, 0, tiled=True)
        results.append(lax.all_to_all(down_rows(lead, hidden, weights), ("y", "x"), 0, 0, tiled=True))
    return mix(shares, results)


def solution(mesh):
    grid = Mesh(mesh.devices.reshape(Y, C, X, Z), ("y", "c", "x", "z"))
    tokens = ("y", "c", "x", "z")
    group = ("x", "z")
    placed = (
        P(tokens, None),
        P(tokens, None),
        P(tokens, None),
        P(tokens),
        P(group, None),
        P(group, None),
        P(None, group),
    )
    return jax.shard_map(local, mesh=grid, in_specs=placed, out_specs=P(tokens, None), check_vma=False)
```

```python
import jax
import jax.numpy as jnp
from jax import lax
from jax.experimental import pallas as pl
from jax.experimental.pallas import tpu as pltpu
from jax.sharding import Mesh
from jax.sharding import PartitionSpec as P

Y, C, X, Z = 4, 2, 4, 16
D, F, TOK = 4096, 1024, 64
SHARD = 512
MEMBERS = 8
CAP = 20
SLOTS = 2 * CAP
MAIN = 16
REST = SLOTS - 2 * MAIN
LEAD = MAIN + REST
SRC = Y * X
ROWS = SRC * SLOTS
ALL_SLOTS = X * SLOTS
FQ = F // Y
HALF = SHARD // 2
WIDE = 4


def slot_at(at):
    second = (at >= MAIN + REST // 2).astype(jnp.int32)
    slot = jnp.where(at < MAIN + REST // 2, at, jnp.where(at < LEAD, at - REST // 2, at - LEAD))
    return second, slot


def pack_kernel(gate_ref, up_ref, down_ref, out_ref, packed, sems):
    y, c = lax.axis_index("y"), lax.axis_index("c")
    rows = pl.ds(pl.multiple_of(c * HALF, HALF), HALF)
    columns = pl.ds(pl.multiple_of(y * FQ, FQ), FQ)
    copies = [
        pltpu.make_async_copy(gate_ref.at[rows, columns], packed.at[:HALF, :FQ], sems.at[0]),
        pltpu.make_async_copy(up_ref.at[rows, columns], packed.at[:HALF, FQ:], sems.at[1]),
    ]
    columns = pl.ds(pl.multiple_of(y * 128, 128), 128)
    for quarter in range(Y):
        rows = pl.ds(pl.multiple_of(quarter * FQ + c * 128, 128), 128)
        to = packed.at[HALF:, quarter * 128 : (quarter + 1) * 128]
        copies.append(pltpu.make_async_copy(down_ref.at[rows, columns], to, sems.at[2 + quarter]))
    for copy in copies:
        copy.start()
    for copy in copies:
        copy.wait()
    copy = pltpu.make_async_copy(packed, out_ref, sems.at[2 + Y])
    copy.start()
    copy.wait()


def restore(v):
    scale = (jnp.max(jnp.abs(v), axis=1, keepdims=True) + 1e-06) / 448.0
    scaled = v / scale
    x = jnp.abs(scaled)
    spacing = jnp.full_like(x, 2.0**-9)
    for shift, least in ((8, 2.0**2), (4, 2.0**-2), (2, 2.0**-4), (1, 2.0**-5)):
        big = x >= least
        x = jnp.where(big, x * 2.0**-shift, x)
        spacing = jnp.where(big, spacing * 2.0**shift, spacing)
    snapped = jnp.floor(x * 512.0 + 0.5) * spacing
    coded = jnp.where(scaled < 0.0, -snapped, snapped)
    return (coded * scale).astype(jnp.bfloat16)


def places(dims, axis):
    place = lax.broadcasted_iota(jnp.int32, dims, axis)
    column = (place * 1639) >> 16
    second, slot = slot_at(place - column * SLOTS)
    return 2 * column + second, slot


def earlier_rows(axis):
    first, second = (lax.broadcasted_iota(jnp.int32, (TOK, TOK), a) for a in (axis, 1 - axis))
    return (first < second).astype(jnp.float32).astype(jnp.bfloat16)


def encode_kernel(count_ref, columns_ref, tokens_ref, first_ref, second_ref):
    dims = (ALL_SLOTS, TOK)
    expert, slot = places(dims, 0)
    named = (columns_ref[0:1, :] == expert) | (columns_ref[1:2, :] == expert)
    named = named & (lax.broadcasted_iota(jnp.int32, dims, 1) < count_ref[0])
    one = named.astype(jnp.float32).astype(jnp.bfloat16)
    rank = jnp.dot(one, earlier_rows(0), preferred_element_type=jnp.float32)
    chosen = named & (rank.astype(jnp.int32) == slot)
    chosen = chosen.astype(jnp.float32).astype(jnp.bfloat16)

    def step(member, carry):
        for half, out_ref in enumerate((first_ref, second_ref)):
            start = pl.multiple_of(member * SHARD + half * HALF, HALF)
            values = tokens_ref[:, pl.ds(start, HALF)].astype(jnp.float32)
            restored = jnp.concatenate([restore(values[:, b * 128 : (b + 1) * 128]) for b in range(HALF // 128)], axis=1)
            rows = jnp.dot(chosen, restored, preferred_element_type=jnp.float32)
            out_ref[:, pl.ds(pl.multiple_of(member * HALF, HALF), HALF)] = rows.astype(jnp.bfloat16)
        return carry

    lax.fori_loop(0, MEMBERS, step, 0)


def mix_kernel(count_ref, routes_ref, numerators_ref, rows_ref, out_ref):
    dims = (TOK, ALL_SLOTS)
    expert, slot = places(dims, 1)
    live = lax.broadcasted_iota(jnp.int32, dims, 0) < count_ref[0]
    by_first = (routes_ref[:, 0:1] == expert) & live
    by_second = (routes_ref[:, 1:2] == expert) & live
    one = (by_first | by_second).astype(jnp.float32).astype(jnp.bfloat16)
    rank = jnp.dot(earlier_rows(1), one, preferred_element_type=jnp.float32)
    here = rank.astype(jnp.int32) == slot
    share = numerators_ref[...].astype(jnp.float32) / 256.0
    shares = jnp.where(by_first & here, share[:, 0:1], 0.0) + jnp.where(by_second & here, share[:, 1:2], 0.0)
    shares = shares.astype(jnp.bfloat16)
    for quarter in range(Y):
        rows = rows_ref[quarter * X : (quarter + 1) * X].reshape(ALL_SLOTS, MEMBERS * 128)
        mixed = jnp.dot(shares, rows, preferred_element_type=jnp.float32).astype(jnp.bfloat16)
        for member in range(MEMBERS):
            at = member * SHARD + quarter * 128
            out_ref[:, at : at + 128] = mixed[:, member * 128 : (member + 1) * 128]


def run_of(block, start, length):
    n = block.shape[-1]
    return block[:, start : start + length].astype(jnp.float32).reshape(-1, n).astype(jnp.bfloat16)


def mixed_rows(first, second):
    place = lax.broadcasted_iota(jnp.int32, first.shape, 0)
    return jnp.where((place & (REST - 1)) < REST // 2, first, second)


def sources(rows, length):
    return rows.reshape(-1, length, rows.shape[-1])


def swish(total):
    gate = total[:, :FQ]
    return gate / (1.0 + jnp.exp(-gate)) * total[:, FQ:]


def hidden_kernel(place_ref, *refs):
    rows, weights_ref, out_ref, sums = refs[: 2 * Y], refs[2 * Y], refs[2 * Y + 1], refs[2 * Y + 2 :]
    main = SRC * MAIN

    def add(parts, start):
        blocks = [ref[...] for ref in parts]
        mixed = [run_of(b, MAIN, REST) for b in blocks]
        for expert, total in enumerate(sums):
            group = [run_of(b, expert * LEAD, MAIN) for b in blocks] + mixed
            weights = weights_ref[expert, :, 0].reshape(MEMBERS * HALF, 2 * FQ)
            product = jnp.dot(jnp.concatenate(group, axis=0), weights, preferred_element_type=jnp.float32)
            total[...] = product if start else total[...] + product

    @pl.when(pl.program_id(0) == 0)
    def _():
        add(rows[0::2], True)

    @pl.when(pl.program_id(0) == 1)
    def _():
        add(rows[1::2], False)
        first, second = (swish(total[...]) for total in sums)
        mixed = mixed_rows(first[main:], second[main:])
        joined = [sources(first[:main], MAIN), sources(mixed, REST), sources(second[:main], MAIN)]
        joined = jnp.concatenate(joined, axis=1).astype(jnp.bfloat16)
        for offset in range(Y):
            source = lax.rem(place_ref[0] + offset, Y)
            block = joined[offset * X : (offset + 1) * X]
            for copy in range(Y):
                out_ref[copy, pl.ds(source * X, X)] = block


def down_kernel(hidden_ref, weights_ref, out_ref, *rows):
    main = SRC * MAIN

    @pl.when(pl.program_id(0) == 0)
    def _():
        for quarter in range(Y):
            block = hidden_ref[quarter]
            at = slice(quarter * FQ, (quarter + 1) * FQ)
            mixed = run_of(block, MAIN, REST)
            for expert in range(2):
                rows[expert][:main, at] = run_of(block, expert * LEAD, MAIN)
                rows[expert][main:, at] = mixed

    def result(expert):
        weights = jnp.concatenate(
            [
                jnp.concatenate([weights_ref[expert, m, half, :, q * 128 : (q + 1) * 128] for m in range(WIDE)], axis=1)
                for q in range(Y)
                for half in range(C)
            ],
            axis=0,
        )
        return jnp.dot(rows[expert][...], weights, preferred_element_type=jnp.float32)

    first, second = result(0), result(1)
    mixed = mixed_rows(first[main:], second[main:])
    joined = [sources(first[:main], MAIN), sources(mixed, REST), sources(second[:main], MAIN)]
    out_ref[...] = jnp.concatenate(joined, axis=1).astype(jnp.bfloat16)


SCALAR = pl.BlockSpec(memory_space=pltpu.SMEM)
WHOLE = pl.BlockSpec(memory_space=pltpu.VMEM)
ANY = pl.BlockSpec(memory_space=pl.ANY)


def shape(dims):
    return jax.ShapeDtypeStruct(dims, jnp.bfloat16)


def params(mebibytes):
    return pltpu.CompilerParams(vmem_limit_bytes=mebibytes << 20)


def encode(counts, routes, tokens):
    return pl.pallas_call(
        encode_kernel,
        out_shape=[shape((ALL_SLOTS, D // 2))] * 2,
        in_specs=[SCALAR, WHOLE, WHOLE],
        out_specs=[WHOLE] * 2,
        compiler_params=params(8),
        cost_estimate=pl.CostEstimate(flops=2 * ALL_SLOTS * TOK * D, bytes_accessed=2 * (TOK + ALL_SLOTS) * D, transcendentals=0),
    )(counts, routes.T, tokens)


def pack(w_gate, w_up, w_down):
    return pl.pallas_call(
        pack_kernel,
        out_shape=shape((HALF + 128, SHARD)),
        in_specs=[ANY] * 3,
        out_specs=ANY,
        scratch_shapes=[pltpu.VMEM((HALF + 128, SHARD), jnp.bfloat16), pltpu.SemaphoreType.DMA((3 + Y,))],
    )(w_gate, w_up, w_down)


def hidden_rows(place, rows, weights):
    return pl.pallas_call(
        hidden_kernel,
        grid=(2,),
        out_shape=shape((Y, SRC, SLOTS, FQ)),
        in_specs=[SCALAR, *[WHOLE] * (2 * Y), pl.BlockSpec((2, MEMBERS, 1, HALF, 2 * FQ), lambda k: (0, 0, k, 0, 0))],
        out_specs=pl.BlockSpec((Y, SRC, SLOTS, FQ), lambda k: (0, 0, 0, 0)),
        scratch_shapes=[pltpu.VMEM((SRC * (MAIN + REST), 2 * FQ), jnp.float32)] * 2,
        compiler_params=params(36),
        cost_estimate=pl.CostEstimate(flops=2 * ROWS * D * 2 * FQ, bytes_accessed=2 * ROWS * D + 8 * D * FQ, transcendentals=0),
    )(place, *rows, weights)


def down_rows(hidden, weights):
    return pl.pallas_call(
        down_kernel,
        grid=(MEMBERS // WIDE,),
        out_shape=shape((SRC, SLOTS, MEMBERS * 128)),
        in_specs=[WHOLE, pl.BlockSpec((2, WIDE, C, 128, SHARD), lambda n: (0, n, 0, HALF // 128, 0))],
        out_specs=pl.BlockSpec((SRC, SLOTS, WIDE * 128), lambda n: (0, 0, n)),
        scratch_shapes=[pltpu.VMEM((SRC * (MAIN + REST), F), jnp.bfloat16)] * 2,
        compiler_params=params(24),
        cost_estimate=pl.CostEstimate(flops=2 * ROWS * F * F, bytes_accessed=4 * ROWS * F + 4 * F * F, transcendentals=0),
    )(hidden, weights)


def mix(counts, routes, numerators, rows):
    return pl.pallas_call(
        mix_kernel,
        out_shape=shape((TOK, D)),
        in_specs=[SCALAR] + [WHOLE] * 3,
        out_specs=WHOLE,
        compiler_params=params(8),
    )(counts, routes, numerators, rows)


def shift(block, by):
    return lax.ppermute(block, "y", [(i, (i + by) % Y) for i in range(Y)])


def local(tokens, routes, numerators, counts, w_gate, w_up, w_down):
    place = lax.axis_index("y").astype(jnp.int32).reshape(1)
    weights = pack(w_gate, w_up, w_down)
    weights = lax.all_gather(weights, ("z", "c")).reshape(2, MEMBERS, C, HALF + 128, SHARD)
    first, second = encode(counts, routes, tokens)
    first = lax.all_to_all(first.reshape(X, SLOTS, D // 2), "x", 0, 0, tiled=True)
    second = lax.all_to_all(second.reshape(X, SLOTS, D // 2), "x", 0, 0, tiled=True)
    first_3, second_1 = shift(first, 1), shift(second, -1)
    second_3, first_1 = shift(second, 1), shift(first, -1)
    first_2, second_2 = shift(first_3, 1), shift(second_1, -1)
    rows = (first, second, first_1, second_1, first_2, second_2, first_3, second_3)
    hidden = lax.all_to_all(hidden_rows(place, rows, weights), "y", 0, 0, tiled=True)
    result = lax.all_to_all(down_rows(hidden, weights), ("y", "x"), 0, 0, tiled=True)
    return mix(counts, routes, numerators, result)


def solution(mesh):
    grid = Mesh(mesh.devices.reshape(Y, C, X, Z), ("y", "c", "x", "z"))
    tokens = ("y", "c", "x", "z")
    group = ("x", "z")
    placed = (
        P(tokens, None),
        P(tokens, None),
        P(tokens, None),
        P(tokens),
        P(group, None),
        P(group, None),
        P(None, group),
    )
    return jax.shard_map(local, mesh=grid, in_specs=placed, out_specs=P(tokens, None), check_vma=False)
```

```python
import jax
import jax.numpy as jnp
from jax import lax
from jax.experimental import pallas as pl
from jax.experimental.pallas import tpu as pltpu
from jax.sharding import Mesh
from jax.sharding import PartitionSpec as P

Y, C, X, Z = 4, 2, 4, 16
D, F, TOK = 4096, 1024, 64
SHARD = 512
MEMBERS = 8
CAP = 20
SLOTS = 2 * CAP
MAIN = 16
REST = SLOTS - 2 * MAIN
LEAD = MAIN + REST
SRC = Y * X
ROWS = SRC * SLOTS
ALL_SLOTS = X * SLOTS
FQ = F // Y
HALF = SHARD // 2
DEEP = 4
WIDE = 4


def slot_at(at):
    second = (at >= MAIN + REST // 2).astype(jnp.int32)
    slot = jnp.where(at < MAIN + REST // 2, at, jnp.where(at < LEAD, at - REST // 2, at - LEAD))
    return second, slot


def pack_kernel(gate_ref, up_ref, down_ref, out_ref, packed, sems):
    y, c = lax.axis_index("y"), lax.axis_index("c")
    rows = pl.ds(pl.multiple_of(c * HALF, HALF), HALF)
    columns = pl.ds(pl.multiple_of(y * FQ, FQ), FQ)
    copies = [
        pltpu.make_async_copy(gate_ref.at[rows, columns], packed.at[:HALF, :FQ], sems.at[0]),
        pltpu.make_async_copy(up_ref.at[rows, columns], packed.at[:HALF, FQ:], sems.at[1]),
    ]
    columns = pl.ds(pl.multiple_of(y * 128, 128), 128)
    for quarter in range(Y):
        rows = pl.ds(pl.multiple_of(quarter * FQ + c * 128, 128), 128)
        to = packed.at[HALF:, quarter * 128 : (quarter + 1) * 128]
        copies.append(pltpu.make_async_copy(down_ref.at[rows, columns], to, sems.at[2 + quarter]))
    for copy in copies:
        copy.start()
    for copy in copies:
        copy.wait()
    copy = pltpu.make_async_copy(packed, out_ref, sems.at[2 + Y])
    copy.start()
    copy.wait()


def restore(v):
    scale = (jnp.max(jnp.abs(v), axis=1, keepdims=True) + 1e-06) / 448.0
    scaled = v / scale
    x = jnp.abs(scaled)
    spacing = jnp.full_like(x, 2.0**-9)
    for shift, least in ((8, 2.0**2), (4, 2.0**-2), (2, 2.0**-4), (1, 2.0**-5)):
        big = x >= least
        x = jnp.where(big, x * 2.0**-shift, x)
        spacing = jnp.where(big, spacing * 2.0**shift, spacing)
    snapped = jnp.floor(x * 512.0 + 0.5) * spacing
    coded = jnp.where(scaled < 0.0, -snapped, snapped)
    return (coded * scale).astype(jnp.bfloat16)


def places(dims, axis):
    place = lax.broadcasted_iota(jnp.int32, dims, axis)
    column = (place * 1639) >> 16
    second, slot = slot_at(place - column * SLOTS)
    return 2 * column + second, slot


def earlier_rows(axis):
    first, second = (lax.broadcasted_iota(jnp.int32, (TOK, TOK), a) for a in (axis, 1 - axis))
    return (first < second).astype(jnp.float32).astype(jnp.bfloat16)


def encode_kernel(count_ref, columns_ref, tokens_ref, first_ref, second_ref):
    dims = (ALL_SLOTS, TOK)
    expert, slot = places(dims, 0)
    named = (columns_ref[0:1, :] == expert) | (columns_ref[1:2, :] == expert)
    named = named & (lax.broadcasted_iota(jnp.int32, dims, 1) < count_ref[0])
    one = named.astype(jnp.float32).astype(jnp.bfloat16)
    rank = jnp.dot(one, earlier_rows(0), preferred_element_type=jnp.float32)
    chosen = named & (rank.astype(jnp.int32) == slot)
    chosen = chosen.astype(jnp.float32).astype(jnp.bfloat16)

    def step(member, carry):
        for half, out_ref in enumerate((first_ref, second_ref)):
            start = pl.multiple_of(member * SHARD + half * HALF, HALF)
            values = tokens_ref[:, pl.ds(start, HALF)].astype(jnp.float32)
            restored = jnp.concatenate([restore(values[:, b * 128 : (b + 1) * 128]) for b in range(HALF // 128)], axis=1)
            rows = jnp.dot(chosen, restored, preferred_element_type=jnp.float32)
            out_ref[:, pl.ds(pl.multiple_of(member * HALF, HALF), HALF)] = rows.astype(jnp.bfloat16)
        return carry

    lax.fori_loop(0, MEMBERS, step, 0)


def mix_kernel(count_ref, routes_ref, numerators_ref, rows_ref, out_ref):
    dims = (TOK, ALL_SLOTS)
    expert, slot = places(dims, 1)
    live = lax.broadcasted_iota(jnp.int32, dims, 0) < count_ref[0]
    by_first = (routes_ref[:, 0:1] == expert) & live
    by_second = (routes_ref[:, 1:2] == expert) & live
    one = (by_first | by_second).astype(jnp.float32).astype(jnp.bfloat16)
    rank = jnp.dot(earlier_rows(1), one, preferred_element_type=jnp.float32)
    here = rank.astype(jnp.int32) == slot
    share = numerators_ref[...].astype(jnp.float32) / 256.0
    shares = jnp.where(by_first & here, share[:, 0:1], 0.0) + jnp.where(by_second & here, share[:, 1:2], 0.0)
    shares = shares.astype(jnp.bfloat16)
    for quarter in range(Y):
        rows = rows_ref[quarter * X : (quarter + 1) * X].reshape(ALL_SLOTS, MEMBERS * 128)
        mixed = jnp.dot(shares, rows, preferred_element_type=jnp.float32).astype(jnp.bfloat16)
        for member in range(MEMBERS):
            at = member * SHARD + quarter * 128
            out_ref[:, at : at + 128] = mixed[:, member * 128 : (member + 1) * 128]


def split_rows(block):
    wide = block.astype(jnp.float32)
    n = wide.shape[-1]
    mixed = wide[:, MAIN:LEAD].reshape(-1, 2, REST, n)
    even, odd = mixed[:, 0], mixed[:, 1]
    low = lax.broadcasted_iota(jnp.int32, even.shape, 1) < REST // 2
    rest = (jnp.where(low, even, swap_halves(odd)), jnp.where(low, swap_halves(even), odd))
    return [
        (wide[:, e * LEAD : e * LEAD + MAIN].reshape(-1, n).astype(jnp.bfloat16), rest[e].reshape(-1, n).astype(jnp.bfloat16))
        for e in range(2)
    ]


def swap_halves(rows):
    return jnp.concatenate([rows[:, REST // 2 :], rows[:, : REST // 2]], axis=1)


def join_rows(first, second):
    main = SRC * MAIN
    n = first.shape[-1]
    one, two = (rows[main:].reshape(-1, REST, n) for rows in (first, second))
    low = lax.broadcasted_iota(jnp.int32, one.shape, 1) < REST // 2
    even, odd = jnp.where(low, one, swap_halves(two)), jnp.where(low, swap_halves(one), two)
    mixed = jnp.stack([even, odd], axis=1).reshape(SRC, REST, n)
    runs = [rows[:main].reshape(SRC, MAIN, n) for rows in (first, second)]
    return jnp.concatenate([runs[0], mixed, runs[1]], axis=1).astype(jnp.bfloat16)


def swish(total):
    gate = total[:, :FQ]
    return gate / (1.0 + jnp.exp(-gate)) * total[:, FQ:]


def hidden_kernel(place_ref, *refs):
    rows, weights_ref, out_ref, held, sems = refs[: 2 * Y], *refs[2 * Y : 2 * Y + 4]
    sums = refs[2 * Y + 4 :]
    groups = MEMBERS // DEEP
    copies = [
        pltpu.make_async_copy(
            weights_ref.at[:, (i % groups) * DEEP : (i % groups + 1) * DEEP, i // groups, :HALF], held.at[i], sems.at[i]
        )
        for i in range(C * groups)
    ]
    copies[0].start()
    copies[1].start()
    for i, copy in enumerate(copies):
        half, group = i // groups, i % groups
        at = slice(group * DEEP * HALF, (group + 1) * DEEP * HALF)
        blocks = [split_rows(ref[:, :, at]) for ref in rows[half::2]]
        copy.wait()
        if i + 2 < len(copies):
            copies[i + 2].start()
        for expert, total in enumerate(sums):
            block = jnp.concatenate([b[expert][part] for part in range(2) for b in blocks], axis=0)
            weights = held[i, expert].reshape(DEEP * HALF, 2 * FQ)
            product = jnp.dot(block, weights, preferred_element_type=jnp.float32)
            total[...] = product if i == 0 else total[...] + product
    joined = join_rows(*(swish(total[...]) for total in sums))
    for offset in range(Y):
        source = lax.rem(place_ref[0] + offset, Y)
        block = joined[offset * X : (offset + 1) * X]
        for copy in range(Y):
            out_ref[copy, pl.ds(source * X, X)] = block


def down_kernel(hidden_ref, weights_ref, out_ref, *rows):
    main = SRC * MAIN

    @pl.when(pl.program_id(0) == 0)
    def _():
        for quarter in range(Y):
            at = slice(quarter * FQ, (quarter + 1) * FQ)
            for ref, (run, rest) in zip(rows, split_rows(hidden_ref[quarter])):
                ref[:main, at] = run
                ref[main:, at] = rest

    def result(expert):
        weights = jnp.concatenate(
            [
                jnp.concatenate([weights_ref[expert, m, half, :, q * 128 : (q + 1) * 128] for m in range(WIDE)], axis=1)
                for q in range(Y)
                for half in range(C)
            ],
            axis=0,
        )
        return jnp.dot(rows[expert][...], weights, preferred_element_type=jnp.float32)

    out_ref[...] = join_rows(result(0), result(1))


SCALAR = pl.BlockSpec(memory_space=pltpu.SMEM)
WHOLE = pl.BlockSpec(memory_space=pltpu.VMEM)
ANY = pl.BlockSpec(memory_space=pl.ANY)


def shape(dims):
    return jax.ShapeDtypeStruct(dims, jnp.bfloat16)


def params(mebibytes):
    return pltpu.CompilerParams(vmem_limit_bytes=mebibytes << 20)


def encode(counts, routes, tokens):
    return pl.pallas_call(
        encode_kernel,
        out_shape=[shape((ALL_SLOTS, D // 2))] * 2,
        in_specs=[SCALAR, WHOLE, WHOLE],
        out_specs=[WHOLE] * 2,
        compiler_params=params(8),
        cost_estimate=pl.CostEstimate(flops=2 * ALL_SLOTS * TOK * D, bytes_accessed=2 * (TOK + ALL_SLOTS) * D, transcendentals=0),
    )(counts, routes.T, tokens)


def pack(w_gate, w_up, w_down):
    return pl.pallas_call(
        pack_kernel,
        out_shape=shape((HALF + 128, SHARD)),
        in_specs=[ANY] * 3,
        out_specs=ANY,
        scratch_shapes=[pltpu.VMEM((HALF + 128, SHARD), jnp.bfloat16), pltpu.SemaphoreType.DMA((3 + Y,))],
    )(w_gate, w_up, w_down)


def hidden_rows(place, rows, weights):
    pieces = C * MEMBERS // DEEP
    return pl.pallas_call(
        hidden_kernel,
        out_shape=shape((Y, SRC, SLOTS, FQ)),
        in_specs=[SCALAR, *[WHOLE] * (2 * Y), ANY],
        out_specs=WHOLE,
        scratch_shapes=[
            pltpu.VMEM((pieces, 2, DEEP, HALF, 2 * FQ), jnp.bfloat16),
            pltpu.SemaphoreType.DMA((pieces,)),
            *[pltpu.VMEM((SRC * SLOTS // 2, 2 * FQ), jnp.float32)] * 2,
        ],
        compiler_params=params(36),
        cost_estimate=pl.CostEstimate(flops=2 * ROWS * D * 2 * FQ, bytes_accessed=2 * ROWS * D + 8 * D * FQ, transcendentals=0),
    )(place, *rows, weights)


def down_rows(hidden, weights):
    return pl.pallas_call(
        down_kernel,
        grid=(MEMBERS // WIDE,),
        out_shape=shape((SRC, SLOTS, MEMBERS * 128)),
        in_specs=[WHOLE, pl.BlockSpec((2, WIDE, C, 128, SHARD), lambda n: (0, n, 0, HALF // 128, 0))],
        out_specs=pl.BlockSpec((SRC, SLOTS, WIDE * 128), lambda n: (0, 0, n)),
        scratch_shapes=[pltpu.VMEM((SRC * SLOTS // 2, F), jnp.bfloat16)] * 2,
        compiler_params=params(24),
        cost_estimate=pl.CostEstimate(flops=2 * ROWS * F * F, bytes_accessed=4 * ROWS * F + 4 * F * F, transcendentals=0),
    )(hidden, weights)


def mix(counts, routes, numerators, rows):
    return pl.pallas_call(
        mix_kernel,
        out_shape=shape((TOK, D)),
        in_specs=[SCALAR] + [WHOLE] * 3,
        out_specs=WHOLE,
        compiler_params=params(8),
    )(counts, routes, numerators, rows)


def shift(block, by):
    return lax.ppermute(block, "y", [(i, (i + by) % Y) for i in range(Y)])


def local(tokens, routes, numerators, counts, w_gate, w_up, w_down):
    place = lax.axis_index("y").astype(jnp.int32).reshape(1)
    weights = pack(w_gate, w_up, w_down)
    weights = lax.all_gather(weights, ("z", "c")).reshape(2, MEMBERS, C, HALF + 128, SHARD)
    first, second = encode(counts, routes, tokens)
    first = lax.all_to_all(first.reshape(X, SLOTS, D // 2), "x", 0, 0, tiled=True)
    second = lax.all_to_all(second.reshape(X, SLOTS, D // 2), "x", 0, 0, tiled=True)
    first_3, second_1 = shift(first, 1), shift(second, -1)
    second_3, first_1 = shift(second, 1), shift(first, -1)
    first_2, second_2 = shift(first_3, 1), shift(second_1, -1)
    rows = (first, second, first_1, second_1, first_2, second_2, first_3, second_3)
    hidden = lax.all_to_all(hidden_rows(place, rows, weights), "y", 0, 0, tiled=True)
    result = lax.all_to_all(down_rows(hidden, weights), ("y", "x"), 0, 0, tiled=True)
    return mix(counts, routes, numerators, result)


def solution(mesh):
    grid = Mesh(mesh.devices.reshape(Y, C, X, Z), ("y", "c", "x", "z"))
    tokens = ("y", "c", "x", "z")
    group = ("x", "z")
    placed = (
        P(tokens, None),
        P(tokens, None),
        P(tokens, None),
        P(tokens),
        P(group, None),
        P(group, None),
        P(None, group),
    )
    return jax.shard_map(local, mesh=grid, in_specs=placed, out_specs=P(tokens, None), check_vma=False)
```

```python
import jax
import jax.numpy as jnp
from jax import lax
from jax.experimental import pallas as pl
from jax.experimental.pallas import tpu as pltpu
from jax.sharding import Mesh
from jax.sharding import PartitionSpec as P

Y, C, X, Z = 4, 2, 4, 16
D, F, TOK = 4096, 1024, 64
SHARD = 512
MEMBERS = 8
CAP = 20
SLOTS = 2 * CAP
MAIN = 16
REST = SLOTS - 2 * MAIN
LEAD = MAIN + REST
SRC = Y * X
ROWS = SRC * SLOTS
ALL_SLOTS = X * SLOTS
FQ = F // Y
HALF = SHARD // 2
DEEP = 4
WIDE = 4


def slot_at(at):
    second = (at >= MAIN + REST // 2).astype(jnp.int32)
    slot = jnp.where(at < MAIN + REST // 2, at, jnp.where(at < LEAD, at - REST // 2, at - LEAD))
    return second, slot


def pack_kernel(gate_ref, up_ref, down_ref, out_ref, packed, sems):
    y, c = lax.axis_index("y"), lax.axis_index("c")
    rows = pl.ds(pl.multiple_of(c * HALF, HALF), HALF)
    columns = pl.ds(pl.multiple_of(y * FQ, FQ), FQ)
    copies = [
        pltpu.make_async_copy(gate_ref.at[rows, columns], packed.at[:HALF, :FQ], sems.at[0]),
        pltpu.make_async_copy(up_ref.at[rows, columns], packed.at[:HALF, FQ:], sems.at[1]),
    ]
    columns = pl.ds(pl.multiple_of(y * 128, 128), 128)
    for quarter in range(Y):
        rows = pl.ds(pl.multiple_of(quarter * FQ + c * 128, 128), 128)
        to = packed.at[HALF:, quarter * 128 : (quarter + 1) * 128]
        copies.append(pltpu.make_async_copy(down_ref.at[rows, columns], to, sems.at[2 + quarter]))
    for copy in copies:
        copy.start()
    for copy in copies:
        copy.wait()
    copy = pltpu.make_async_copy(packed, out_ref, sems.at[2 + Y])
    copy.start()
    copy.wait()


def restore(v):
    scale = (jnp.max(jnp.abs(v), axis=1, keepdims=True) + 1e-06) / 448.0
    scaled = v / scale
    x = jnp.abs(scaled)
    spacing = jnp.full_like(x, 2.0**-9)
    for shift, least in ((8, 2.0**2), (4, 2.0**-2), (2, 2.0**-4), (1, 2.0**-5)):
        big = x >= least
        x = jnp.where(big, x * 2.0**-shift, x)
        spacing = jnp.where(big, spacing * 2.0**shift, spacing)
    snapped = jnp.floor(x * 512.0 + 0.5) * spacing
    coded = jnp.where(scaled < 0.0, -snapped, snapped)
    return (coded * scale).astype(jnp.bfloat16)


def places(dims, axis):
    place = lax.broadcasted_iota(jnp.int32, dims, axis)
    column = (place * 1639) >> 16
    second, slot = slot_at(place - column * SLOTS)
    return 2 * column + second, slot


def earlier_rows(axis):
    first, second = (lax.broadcasted_iota(jnp.int32, (TOK, TOK), a) for a in (axis, 1 - axis))
    return (first < second).astype(jnp.float32).astype(jnp.bfloat16)


def encode_kernel(count_ref, columns_ref, tokens_ref, first_ref, second_ref):
    dims = (ALL_SLOTS, TOK)
    expert, slot = places(dims, 0)
    named = (columns_ref[0:1, :] == expert) | (columns_ref[1:2, :] == expert)
    named = named & (lax.broadcasted_iota(jnp.int32, dims, 1) < count_ref[0])
    one = named.astype(jnp.float32).astype(jnp.bfloat16)
    rank = jnp.dot(one, earlier_rows(0), preferred_element_type=jnp.float32)
    chosen = named & (rank.astype(jnp.int32) == slot)
    chosen = chosen.astype(jnp.float32).astype(jnp.bfloat16)

    def step(member, carry):
        for half, out_ref in enumerate((first_ref, second_ref)):
            start = pl.multiple_of(member * SHARD + half * HALF, HALF)
            values = tokens_ref[:, pl.ds(start, HALF)].astype(jnp.float32)
            restored = jnp.concatenate([restore(values[:, b * 128 : (b + 1) * 128]) for b in range(HALF // 128)], axis=1)
            rows = jnp.dot(chosen, restored, preferred_element_type=jnp.float32)
            out_ref[:, pl.ds(pl.multiple_of(member * HALF, HALF), HALF)] = rows.astype(jnp.bfloat16)
        return carry

    lax.fori_loop(0, MEMBERS, step, 0)


def mix_kernel(count_ref, routes_ref, numerators_ref, rows_ref, out_ref):
    dims = (TOK, ALL_SLOTS)
    expert, slot = places(dims, 1)
    live = lax.broadcasted_iota(jnp.int32, dims, 0) < count_ref[0]
    by_first = (routes_ref[:, 0:1] == expert) & live
    by_second = (routes_ref[:, 1:2] == expert) & live
    one = (by_first | by_second).astype(jnp.float32).astype(jnp.bfloat16)
    rank = jnp.dot(earlier_rows(1), one, preferred_element_type=jnp.float32)
    here = rank.astype(jnp.int32) == slot
    share = numerators_ref[...].astype(jnp.float32) / 256.0
    shares = jnp.where(by_first & here, share[:, 0:1], 0.0) + jnp.where(by_second & here, share[:, 1:2], 0.0)
    shares = shares.astype(jnp.bfloat16)
    for quarter in range(Y):
        rows = rows_ref[quarter * X : (quarter + 1) * X].reshape(ALL_SLOTS, MEMBERS * 128)
        mixed = jnp.dot(shares, rows, preferred_element_type=jnp.float32).astype(jnp.bfloat16)
        for member in range(MEMBERS):
            at = member * SHARD + quarter * 128
            out_ref[:, at : at + 128] = mixed[:, member * 128 : (member + 1) * 128]


def split_rows(block):
    wide = block.astype(jnp.float32)
    n = wide.shape[-1]
    mixed = wide[:, MAIN:LEAD].reshape(-1, 2, REST, n)
    even, odd = mixed[:, 0], mixed[:, 1]
    low = lax.broadcasted_iota(jnp.int32, even.shape, 1) < REST // 2
    rest = (jnp.where(low, even, swap_halves(odd)), jnp.where(low, swap_halves(even), odd))
    return [
        (wide[:, e * LEAD : e * LEAD + MAIN].reshape(-1, n).astype(jnp.bfloat16), rest[e].reshape(-1, n).astype(jnp.bfloat16))
        for e in range(2)
    ]


def swap_halves(rows):
    return jnp.concatenate([rows[:, REST // 2 :], rows[:, : REST // 2]], axis=1)


def join_rows(first, second):
    main = SRC * MAIN
    n = first.shape[-1]
    one, two = (rows[main:].reshape(-1, REST, n) for rows in (first, second))
    low = lax.broadcasted_iota(jnp.int32, one.shape, 1) < REST // 2
    even, odd = jnp.where(low, one, swap_halves(two)), jnp.where(low, swap_halves(one), two)
    mixed = jnp.stack([even, odd], axis=1).reshape(SRC, REST, n)
    runs = [rows[:main].reshape(SRC, MAIN, n) for rows in (first, second)]
    return jnp.concatenate([runs[0], mixed, runs[1]], axis=1).astype(jnp.bfloat16)


def swish(total):
    gate = total[:, :FQ]
    return gate / (1.0 + jnp.exp(-gate)) * total[:, FQ:]


def hidden_kernel(place_ref, *refs):
    rows, weights_ref, out_ref, down_ref, held, sems = refs[: 2 * Y], *refs[2 * Y : 2 * Y + 5]
    sums = refs[2 * Y + 5 :]
    groups = MEMBERS // DEEP
    copies = [
        pltpu.make_async_copy(
            weights_ref.at[:, (i % groups) * DEEP : (i % groups + 1) * DEEP, i // groups, :HALF], held.at[i], sems.at[i]
        )
        for i in range(C * groups)
    ]
    copies.append(pltpu.make_async_copy(weights_ref.at[:, :, :, HALF:], down_ref, sems.at[C * groups]))
    copies[0].start()
    copies[1].start()
    for i, copy in enumerate(copies[:-1]):
        half, group = i // groups, i % groups
        at = slice(group * DEEP * HALF, (group + 1) * DEEP * HALF)
        blocks = [split_rows(ref[:, :, at]) for ref in rows[half::2]]
        copy.wait()
        if i + 2 < len(copies):
            copies[i + 2].start()
        for expert, total in enumerate(sums):
            block = jnp.concatenate([b[expert][part] for part in range(2) for b in blocks], axis=0)
            weights = held[i, expert].reshape(DEEP * HALF, 2 * FQ)
            product = jnp.dot(block, weights, preferred_element_type=jnp.float32)
            total[...] = product if i == 0 else total[...] + product
    joined = join_rows(*(swish(total[...]) for total in sums))
    for offset in range(Y):
        source = lax.rem(place_ref[0] + offset, Y)
        block = joined[offset * X : (offset + 1) * X]
        for copy in range(Y):
            out_ref[copy, pl.ds(source * X, X)] = block
    copies[-1].wait()


def down_kernel(hidden_ref, weights_ref, out_ref, *rows):
    main = SRC * MAIN
    for quarter in range(Y):
        at = slice(quarter * FQ, (quarter + 1) * FQ)
        for ref, (run, rest) in zip(rows, split_rows(hidden_ref[quarter])):
            ref[:main, at] = run
            ref[main:, at] = rest

    def result(expert, members):
        weights = jnp.concatenate(
            [
                jnp.concatenate([weights_ref[expert, m, half, :, q * 128 : (q + 1) * 128] for m in members], axis=1)
                for q in range(Y)
                for half in range(C)
            ],
            axis=0,
        )
        return jnp.dot(rows[expert][...], weights, preferred_element_type=jnp.float32)

    for start in range(0, MEMBERS, WIDE):
        members = range(start, start + WIDE)
        out_ref[:, :, start * 128 : (start + WIDE) * 128] = join_rows(result(0, members), result(1, members))


SCALAR = pl.BlockSpec(memory_space=pltpu.SMEM)
WHOLE = pl.BlockSpec(memory_space=pltpu.VMEM)
ANY = pl.BlockSpec(memory_space=pl.ANY)


def shape(dims):
    return jax.ShapeDtypeStruct(dims, jnp.bfloat16)


def params(mebibytes):
    return pltpu.CompilerParams(vmem_limit_bytes=mebibytes << 20)


def encode(counts, routes, tokens):
    return pl.pallas_call(
        encode_kernel,
        out_shape=[shape((ALL_SLOTS, D // 2))] * 2,
        in_specs=[SCALAR, WHOLE, WHOLE],
        out_specs=[WHOLE] * 2,
        compiler_params=params(8),
        cost_estimate=pl.CostEstimate(flops=2 * ALL_SLOTS * TOK * D, bytes_accessed=2 * (TOK + ALL_SLOTS) * D, transcendentals=0),
    )(counts, routes.T, tokens)


def pack(w_gate, w_up, w_down):
    return pl.pallas_call(
        pack_kernel,
        out_shape=shape((HALF + 128, SHARD)),
        in_specs=[ANY] * 3,
        out_specs=ANY,
        scratch_shapes=[pltpu.VMEM((HALF + 128, SHARD), jnp.bfloat16), pltpu.SemaphoreType.DMA((3 + Y,))],
    )(w_gate, w_up, w_down)


def hidden_rows(place, rows, weights):
    pieces = C * MEMBERS // DEEP
    return pl.pallas_call(
        hidden_kernel,
        out_shape=[shape((Y, SRC, SLOTS, FQ)), shape((2, MEMBERS, C, 128, SHARD))],
        in_specs=[SCALAR, *[WHOLE] * (2 * Y), ANY],
        out_specs=[WHOLE] * 2,
        scratch_shapes=[
            pltpu.VMEM((pieces, 2, DEEP, HALF, 2 * FQ), jnp.bfloat16),
            pltpu.SemaphoreType.DMA((pieces + 1,)),
            *[pltpu.VMEM((SRC * SLOTS // 2, 2 * FQ), jnp.float32)] * 2,
        ],
        compiler_params=params(36),
        cost_estimate=pl.CostEstimate(flops=2 * ROWS * D * 2 * FQ, bytes_accessed=2 * ROWS * D + 8 * D * FQ, transcendentals=0),
    )(place, *rows, weights)


def down_rows(hidden, weights):
    return pl.pallas_call(
        down_kernel,
        out_shape=shape((SRC, SLOTS, MEMBERS * 128)),
        in_specs=[WHOLE] * 2,
        out_specs=WHOLE,
        scratch_shapes=[pltpu.VMEM((SRC * SLOTS // 2, F), jnp.bfloat16)] * 2,
        compiler_params=params(24),
        cost_estimate=pl.CostEstimate(flops=2 * ROWS * F * F, bytes_accessed=4 * ROWS * F + 4 * F * F, transcendentals=0),
    )(hidden, weights)


def mix(counts, routes, numerators, rows):
    return pl.pallas_call(
        mix_kernel,
        out_shape=shape((TOK, D)),
        in_specs=[SCALAR] + [WHOLE] * 3,
        out_specs=WHOLE,
        compiler_params=params(8),
    )(counts, routes, numerators, rows)


def shift(block, by):
    return lax.ppermute(block, "y", [(i, (i + by) % Y) for i in range(Y)])


def local(tokens, routes, numerators, counts, w_gate, w_up, w_down):
    place = lax.axis_index("y").astype(jnp.int32).reshape(1)
    weights = pack(w_gate, w_up, w_down)
    weights = lax.all_gather(weights, ("z", "c")).reshape(2, MEMBERS, C, HALF + 128, SHARD)
    first, second = encode(counts, routes, tokens)
    first = lax.all_to_all(first.reshape(X, SLOTS, D // 2), "x", 0, 0, tiled=True)
    second = lax.all_to_all(second.reshape(X, SLOTS, D // 2), "x", 0, 0, tiled=True)
    first_3, second_1 = shift(first, 1), shift(second, -1)
    second_3, first_1 = shift(second, 1), shift(first, -1)
    first_2, second_2 = shift(first_3, 1), shift(second_1, -1)
    rows = (first, second, first_1, second_1, first_2, second_2, first_3, second_3)
    hidden, down = hidden_rows(place, rows, weights)
    hidden = lax.all_to_all(hidden, "y", 0, 0, tiled=True)
    result = lax.all_to_all(down_rows(hidden, down), ("y", "x"), 0, 0, tiled=True)
    return mix(counts, routes, numerators, result)


def solution(mesh):
    grid = Mesh(mesh.devices.reshape(Y, C, X, Z), ("y", "c", "x", "z"))
    tokens = ("y", "c", "x", "z")
    group = ("x", "z")
    placed = (
        P(tokens, None),
        P(tokens, None),
        P(tokens, None),
        P(tokens),
        P(group, None),
        P(group, None),
        P(None, group),
    )
    return jax.shard_map(local, mesh=grid, in_specs=placed, out_specs=P(tokens, None), check_vma=False)
```

```python
import jax
import jax.numpy as jnp
from jax import lax
from jax.experimental import pallas as pl
from jax.experimental.pallas import tpu as pltpu
from jax.sharding import Mesh
from jax.sharding import PartitionSpec as P

Y, C, X, Z = 4, 2, 4, 16
D, F, TOK = 4096, 1024, 64
SHARD = 512
MEMBERS = 8
CAP = 20
SLOTS = 2 * CAP
MAIN = 16
REST = SLOTS - 2 * MAIN
LEAD = MAIN + REST
SRC = Y * X
ROWS = SRC * SLOTS
ALL_SLOTS = X * SLOTS
FQ = F // Y
HALF = SHARD // 2
DEEP = 4
WIDE = 4


def slot_at(at):
    second = (at >= MAIN + REST // 2).astype(jnp.int32)
    slot = jnp.where(at < MAIN + REST // 2, at, jnp.where(at < LEAD, at - REST // 2, at - LEAD))
    return second, slot


def pack_kernel(gate_ref, up_ref, down_ref, out_ref, packed, sems):
    y, c = lax.axis_index("y"), lax.axis_index("c")
    rows = pl.ds(pl.multiple_of(c * HALF, HALF), HALF)
    columns = pl.ds(pl.multiple_of(y * FQ, FQ), FQ)
    copies = [
        pltpu.make_async_copy(gate_ref.at[rows, columns], packed.at[:HALF, :FQ], sems.at[0]),
        pltpu.make_async_copy(up_ref.at[rows, columns], packed.at[:HALF, FQ:], sems.at[1]),
    ]
    columns = pl.ds(pl.multiple_of(y * 128, 128), 128)
    for quarter in range(Y):
        rows = pl.ds(pl.multiple_of(quarter * FQ + c * 128, 128), 128)
        to = packed.at[HALF:, quarter * 128 : (quarter + 1) * 128]
        copies.append(pltpu.make_async_copy(down_ref.at[rows, columns], to, sems.at[2 + quarter]))
    for copy in copies:
        copy.start()
    for copy in copies:
        copy.wait()
    copy = pltpu.make_async_copy(packed, out_ref, sems.at[2 + Y])
    copy.start()
    copy.wait()


def restore(v):
    scale = (jnp.max(jnp.abs(v), axis=1, keepdims=True) + 1e-06) / 448.0
    scaled = v / scale
    x = jnp.abs(scaled)
    spacing = jnp.full_like(x, 2.0**-9)
    for shift, least in ((8, 2.0**2), (4, 2.0**-2), (2, 2.0**-4), (1, 2.0**-5)):
        big = x >= least
        x = jnp.where(big, x * 2.0**-shift, x)
        spacing = jnp.where(big, spacing * 2.0**shift, spacing)
    snapped = jnp.floor(x * 512.0 + 0.5) * spacing
    coded = jnp.where(scaled < 0.0, -snapped, snapped)
    return (coded * scale).astype(jnp.bfloat16)


def placements(count_ref, columns_ref):
    dims = (ALL_SLOTS, TOK)
    place = lax.broadcasted_iota(jnp.int32, dims, 0)
    row = lax.broadcasted_iota(jnp.int32, dims, 1)
    column = (place * 1639) >> 16
    second, slot = slot_at(place - column * SLOTS)
    expert = 2 * column + second
    live = row < count_ref[0]
    by_first, by_second = ((columns_ref[i : i + 1, :] == expert) & live for i in range(2))
    named = (by_first | by_second).astype(jnp.float32).astype(jnp.bfloat16)
    earlier = (lax.broadcasted_iota(jnp.int32, (TOK, TOK), 0) < lax.broadcasted_iota(jnp.int32, (TOK, TOK), 1))
    rank = jnp.dot(named, earlier.astype(jnp.float32).astype(jnp.bfloat16), preferred_element_type=jnp.float32)
    here = rank.astype(jnp.int32) == slot
    return by_first & here, by_second & here


def encode_kernel(count_ref, columns_ref, tokens_ref, first_ref, second_ref):
    by_first, by_second = placements(count_ref, columns_ref)
    chosen = (by_first | by_second).astype(jnp.float32).astype(jnp.bfloat16)

    def step(member, carry):
        for half, out_ref in enumerate((first_ref, second_ref)):
            start = pl.multiple_of(member * SHARD + half * HALF, HALF)
            values = tokens_ref[:, pl.ds(start, HALF)].astype(jnp.float32)
            restored = jnp.concatenate([restore(values[:, b * 128 : (b + 1) * 128]) for b in range(HALF // 128)], axis=1)
            rows = jnp.dot(chosen, restored, preferred_element_type=jnp.float32)
            out_ref[:, pl.ds(pl.multiple_of(member * HALF, HALF), HALF)] = rows.astype(jnp.bfloat16)
        return carry

    lax.fori_loop(0, MEMBERS, step, 0)


def mix_kernel(count_ref, columns_ref, numerators_ref, rows_ref, out_ref):
    by_first, by_second = placements(count_ref, columns_ref)
    share = numerators_ref[...].astype(jnp.float32) / 256.0
    shares = jnp.where(by_first, share[0:1], 0.0) + jnp.where(by_second, share[1:2], 0.0)
    shares = shares.astype(jnp.bfloat16)
    for quarter in range(Y):
        rows = rows_ref[quarter * X : (quarter + 1) * X].reshape(ALL_SLOTS, MEMBERS * 128)
        mixed = lax.dot_general(shares, rows, (((0,), (0,)), ((), ())), preferred_element_type=jnp.float32)
        mixed = mixed.astype(jnp.bfloat16)
        for member in range(MEMBERS):
            at = member * SHARD + quarter * 128
            out_ref[:, at : at + 128] = mixed[:, member * 128 : (member + 1) * 128]


def split_rows(block):
    wide = block.astype(jnp.float32)
    n = wide.shape[-1]
    mixed = wide[:, MAIN:LEAD].reshape(-1, 2, REST, n)
    even, odd = mixed[:, 0], mixed[:, 1]
    low = lax.broadcasted_iota(jnp.int32, even.shape, 1) < REST // 2
    rest = (jnp.where(low, even, swap_halves(odd)), jnp.where(low, swap_halves(even), odd))
    return [
        (wide[:, e * LEAD : e * LEAD + MAIN].reshape(-1, n).astype(jnp.bfloat16), rest[e].reshape(-1, n).astype(jnp.bfloat16))
        for e in range(2)
    ]


def swap_halves(rows):
    return jnp.concatenate([rows[:, REST // 2 :], rows[:, : REST // 2]], axis=1)


def join_rows(first, second):
    main = SRC * MAIN
    n = first.shape[-1]
    one, two = (rows[main:].reshape(-1, REST, n) for rows in (first, second))
    low = lax.broadcasted_iota(jnp.int32, one.shape, 1) < REST // 2
    even, odd = jnp.where(low, one, swap_halves(two)), jnp.where(low, swap_halves(one), two)
    mixed = jnp.stack([even, odd], axis=1).reshape(SRC, REST, n)
    runs = [rows[:main].reshape(SRC, MAIN, n) for rows in (first, second)]
    return jnp.concatenate([runs[0], mixed, runs[1]], axis=1).astype(jnp.bfloat16)


def swish(total):
    gate = total[:, :FQ]
    return gate / (1.0 + jnp.exp(-gate)) * total[:, FQ:]


def hidden_kernel(place_ref, *refs):
    rows, weights_ref, out_ref, held, here, sems, row_sems = refs[: 2 * Y], *refs[2 * Y : 2 * Y + 6]
    sums = refs[2 * Y + 6 :]
    groups = MEMBERS // DEEP
    copies = [
        pltpu.make_async_copy(
            weights_ref.at[:, (i % groups) * DEEP : (i % groups + 1) * DEEP, i // groups, :HALF], held.at[i], sems.at[i]
        )
        for i in range(C * groups)
    ]
    moves = [pltpu.make_async_copy(ref, here.at[i], row_sems.at[i]) for i, ref in enumerate(rows)]
    for move in moves[0::2]:
        move.start()
    copies[0].start()
    for move in moves[1::2]:
        move.start()
    copies[1].start()
    for i, copy in enumerate(copies):
        half, group = i // groups, i % groups
        at = slice(group * DEEP * HALF, (group + 1) * DEEP * HALF)
        if group == 0:
            for move in moves[half::2]:
                move.wait()
        blocks = [split_rows(here[2 * offset + half, :, :, at]) for offset in range(Y)]
        copy.wait()
        if i + 2 < len(copies):
            copies[i + 2].start()
        for expert, total in enumerate(sums):
            block = jnp.concatenate([b[expert][part] for part in range(2) for b in blocks], axis=0)
            weights = held[i, expert].reshape(DEEP * HALF, 2 * FQ)
            product = jnp.dot(block, weights, preferred_element_type=jnp.float32)
            total[...] = product if i == 0 else total[...] + product
    joined = join_rows(*(swish(total[...]) for total in sums))
    for offset in range(Y):
        source = lax.rem(place_ref[0] + offset, Y)
        block = joined[offset * X : (offset + 1) * X]
        for copy in range(Y):
            out_ref[copy, pl.ds(source * X, X)] = block


def down_kernel(hidden_ref, weights_ref, out_ref, held, sems, *rows):
    main = SRC * MAIN
    starts = range(0, MEMBERS, WIDE)
    copies = [
        pltpu.make_async_copy(weights_ref.at[:, start : start + WIDE, :, HALF:], held.at[i], sems.at[i])
        for i, start in enumerate(starts)
    ]
    for copy in copies:
        copy.start()
    for quarter in range(Y):
        at = slice(quarter * FQ, (quarter + 1) * FQ)
        for ref, (run, rest) in zip(rows, split_rows(hidden_ref[quarter])):
            ref[:main, at] = run
            ref[main:, at] = rest

    def result(i, expert):
        weights = jnp.concatenate(
            [
                jnp.concatenate([held[i, expert, m, half, :, q * 128 : (q + 1) * 128] for m in range(WIDE)], axis=1)
                for q in range(Y)
                for half in range(C)
            ],
            axis=0,
        )
        return jnp.dot(rows[expert][...], weights, preferred_element_type=jnp.float32)

    for i, start in enumerate(starts):
        copies[i].wait()
        out_ref[:, :, start * 128 : (start + WIDE) * 128] = join_rows(result(i, 0), result(i, 1))


SCALAR = pl.BlockSpec(memory_space=pltpu.SMEM)
WHOLE = pl.BlockSpec(memory_space=pltpu.VMEM)
ANY = pl.BlockSpec(memory_space=pl.ANY)


def shape(dims):
    return jax.ShapeDtypeStruct(dims, jnp.bfloat16)


def params(mebibytes):
    return pltpu.CompilerParams(vmem_limit_bytes=mebibytes << 20)


def encode(counts, routes, tokens):
    return pl.pallas_call(
        encode_kernel,
        out_shape=[shape((ALL_SLOTS, D // 2))] * 2,
        in_specs=[SCALAR, WHOLE, WHOLE],
        out_specs=[WHOLE] * 2,
        compiler_params=params(8),
        cost_estimate=pl.CostEstimate(flops=2 * ALL_SLOTS * TOK * D, bytes_accessed=2 * (TOK + ALL_SLOTS) * D, transcendentals=0),
    )(counts, routes.T, tokens)


def pack(w_gate, w_up, w_down):
    return pl.pallas_call(
        pack_kernel,
        out_shape=shape((HALF + 128, SHARD)),
        in_specs=[ANY] * 3,
        out_specs=ANY,
        scratch_shapes=[pltpu.VMEM((HALF + 128, SHARD), jnp.bfloat16), pltpu.SemaphoreType.DMA((3 + Y,))],
    )(w_gate, w_up, w_down)


def hidden_rows(place, rows, weights):
    pieces = C * MEMBERS // DEEP
    return pl.pallas_call(
        hidden_kernel,
        out_shape=shape((Y, SRC, SLOTS, FQ)),
        in_specs=[SCALAR, *[ANY] * (2 * Y), ANY],
        out_specs=WHOLE,
        scratch_shapes=[
            pltpu.VMEM((pieces, 2, DEEP, HALF, 2 * FQ), jnp.bfloat16),
            pltpu.VMEM((2 * Y, X, SLOTS, D // 2), jnp.bfloat16),
            pltpu.SemaphoreType.DMA((pieces,)),
            pltpu.SemaphoreType.DMA((2 * Y,)),
            *[pltpu.VMEM((SRC * SLOTS // 2, 2 * FQ), jnp.float32)] * 2,
        ],
        compiler_params=params(36),
        cost_estimate=pl.CostEstimate(flops=2 * ROWS * D * 2 * FQ, bytes_accessed=2 * ROWS * D + 8 * D * FQ, transcendentals=0),
    )(place, *rows, weights)


def down_rows(hidden, weights):
    pieces = MEMBERS // WIDE
    return pl.pallas_call(
        down_kernel,
        out_shape=shape((SRC, SLOTS, MEMBERS * 128)),
        in_specs=[WHOLE, ANY],
        out_specs=WHOLE,
        scratch_shapes=[
            pltpu.VMEM((pieces, 2, WIDE, C, 128, SHARD), jnp.bfloat16),
            pltpu.SemaphoreType.DMA((pieces,)),
            *[pltpu.VMEM((SRC * SLOTS // 2, F), jnp.bfloat16)] * 2,
        ],
        compiler_params=params(50),
        cost_estimate=pl.CostEstimate(flops=2 * ROWS * F * F, bytes_accessed=4 * ROWS * F + 4 * F * F, transcendentals=0),
    )(hidden, weights)


def mix(counts, routes, numerators, rows):
    return pl.pallas_call(
        mix_kernel,
        out_shape=shape((TOK, D)),
        in_specs=[SCALAR] + [WHOLE] * 3,
        out_specs=WHOLE,
        compiler_params=params(8),
    )(counts, routes.T, numerators.T, rows)


def shift(block, by):
    return lax.ppermute(block, "y", [(i, (i + by) % Y) for i in range(Y)])


def local(tokens, routes, numerators, counts, w_gate, w_up, w_down):
    place = lax.axis_index("y").astype(jnp.int32).reshape(1)
    weights = pack(w_gate, w_up, w_down)
    weights = lax.all_gather(weights, ("z", "c")).reshape(2, MEMBERS, C, HALF + 128, SHARD)
    first, second = encode(counts, routes, tokens)
    first = lax.all_to_all(first.reshape(X, SLOTS, D // 2), "x", 0, 0, tiled=True)
    second = lax.all_to_all(second.reshape(X, SLOTS, D // 2), "x", 0, 0, tiled=True)
    first_3, second_1 = shift(first, 1), shift(second, -1)
    second_3, first_1 = shift(second, 1), shift(first, -1)
    first_2, second_2 = shift(first_3, 1), shift(second_1, -1)
    rows = (first, second, first_1, second_1, first_2, second_2, first_3, second_3)
    hidden = lax.all_to_all(hidden_rows(place, rows, weights), "y", 0, 0, tiled=True)
    result = lax.all_to_all(down_rows(hidden, weights), ("y", "x"), 0, 0, tiled=True)
    return mix(counts, routes, numerators, result)


def solution(mesh):
    grid = Mesh(mesh.devices.reshape(Y, C, X, Z), ("y", "c", "x", "z"))
    tokens = ("y", "c", "x", "z")
    group = ("x", "z")
    placed = (
        P(tokens, None),
        P(tokens, None),
        P(tokens, None),
        P(tokens),
        P(group, None),
        P(group, None),
        P(None, group),
    )
    return jax.shard_map(local, mesh=grid, in_specs=placed, out_specs=P(tokens, None), check_vma=False)
```

```python
import jax
import jax.numpy as jnp
from jax import lax
from jax.experimental import pallas as pl
from jax.experimental.pallas import tpu as pltpu
from jax.sharding import Mesh
from jax.sharding import PartitionSpec as P

Y, C, X, Z = 4, 2, 4, 16
D, F, TOK = 4096, 1024, 64
SHARD = 512
MEMBERS = 8
CAP = 20
SLOTS = 2 * CAP
MAIN = 16
REST = SLOTS - 2 * MAIN
LEAD = MAIN + REST
SRC = Y * X
ROWS = SRC * SLOTS
ALL_SLOTS = X * SLOTS
FQ = F // Y
HALF = SHARD // 2
DEEP = 4
WIDE = 4


def slot_at(at):
    second = (at >= MAIN + REST // 2).astype(jnp.int32)
    slot = jnp.where(at < MAIN + REST // 2, at, jnp.where(at < LEAD, at - REST // 2, at - LEAD))
    return second, slot


def pack_kernel(gate_ref, up_ref, down_ref, out_ref, packed, sems):
    y, c = lax.axis_index("y"), lax.axis_index("c")
    rows = pl.ds(pl.multiple_of(c * HALF, HALF), HALF)
    columns = pl.ds(pl.multiple_of(y * FQ, FQ), FQ)
    copies = [
        pltpu.make_async_copy(gate_ref.at[rows, columns], packed.at[:HALF, :FQ], sems.at[0]),
        pltpu.make_async_copy(up_ref.at[rows, columns], packed.at[:HALF, FQ:], sems.at[1]),
    ]
    columns = pl.ds(pl.multiple_of(y * 128, 128), 128)
    for quarter in range(Y):
        rows = pl.ds(pl.multiple_of(quarter * FQ + c * 128, 128), 128)
        to = packed.at[HALF:, quarter * 128 : (quarter + 1) * 128]
        copies.append(pltpu.make_async_copy(down_ref.at[rows, columns], to, sems.at[2 + quarter]))
    for copy in copies:
        copy.start()
    for copy in copies:
        copy.wait()
    copy = pltpu.make_async_copy(packed, out_ref, sems.at[2 + Y])
    copy.start()
    copy.wait()


def restore(v):
    scale = (jnp.max(jnp.abs(v), axis=1, keepdims=True) + 1e-06) / 448.0
    scaled = v / scale
    x = jnp.abs(scaled)
    spacing = jnp.full_like(x, 2.0**-9)
    for shift, least in ((8, 2.0**2), (4, 2.0**-2), (2, 2.0**-4), (1, 2.0**-5)):
        big = x >= least
        x = jnp.where(big, x * 2.0**-shift, x)
        spacing = jnp.where(big, spacing * 2.0**shift, spacing)
    snapped = jnp.floor(x * 512.0 + 0.5) * spacing
    coded = jnp.where(scaled < 0.0, -snapped, snapped)
    return (coded * scale).astype(jnp.bfloat16)


def placements(count_ref, columns_ref):
    dims = (ALL_SLOTS, TOK)
    place = lax.broadcasted_iota(jnp.int32, dims, 0)
    row = lax.broadcasted_iota(jnp.int32, dims, 1)
    column = (place * 1639) >> 16
    second, slot = slot_at(place - column * SLOTS)
    expert = 2 * column + second
    live = row < count_ref[0]
    by_first, by_second = ((columns_ref[i : i + 1, :] == expert) & live for i in range(2))
    named = (by_first | by_second).astype(jnp.float32).astype(jnp.bfloat16)
    earlier = (lax.broadcasted_iota(jnp.int32, (TOK, TOK), 0) < lax.broadcasted_iota(jnp.int32, (TOK, TOK), 1))
    rank = jnp.dot(named, earlier.astype(jnp.float32).astype(jnp.bfloat16), preferred_element_type=jnp.float32)
    here = rank.astype(jnp.int32) == slot
    return by_first & here, by_second & here


def encode_kernel(count_ref, columns_ref, tokens_ref, first_ref, second_ref):
    by_first, by_second = placements(count_ref, columns_ref)
    chosen = (by_first | by_second).astype(jnp.float32).astype(jnp.bfloat16)

    def step(member, carry):
        for half, out_ref in enumerate((first_ref, second_ref)):
            start = pl.multiple_of(member * SHARD + half * HALF, HALF)
            values = tokens_ref[:, pl.ds(start, HALF)].astype(jnp.float32)
            restored = jnp.concatenate([restore(values[:, b * 128 : (b + 1) * 128]) for b in range(HALF // 128)], axis=1)
            rows = jnp.dot(chosen, restored, preferred_element_type=jnp.float32)
            out_ref[:, pl.ds(pl.multiple_of(member * HALF, HALF), HALF)] = rows.astype(jnp.bfloat16)
        return carry

    lax.fori_loop(0, MEMBERS, step, 0)


def mix_kernel(count_ref, columns_ref, numerators_ref, rows_ref, out_ref):
    by_first, by_second = placements(count_ref, columns_ref)
    share = numerators_ref[...].astype(jnp.float32) / 256.0
    shares = jnp.where(by_first, share[0:1], 0.0) + jnp.where(by_second, share[1:2], 0.0)
    shares = shares.astype(jnp.bfloat16)
    for quarter in range(Y):
        rows = jnp.concatenate([rows_ref[x * Y + quarter] for x in range(X)], axis=0)
        mixed = lax.dot_general(shares, rows, (((0,), (0,)), ((), ())), preferred_element_type=jnp.float32)
        mixed = mixed.astype(jnp.bfloat16)
        for member in range(MEMBERS):
            at = member * SHARD + quarter * 128
            out_ref[:, at : at + 128] = mixed[:, member * 128 : (member + 1) * 128]


def split_rows(block):
    wide = block.astype(jnp.float32)
    n = wide.shape[-1]
    mixed = wide[:, MAIN:LEAD].reshape(-1, 2, REST, n)
    even, odd = mixed[:, 0], mixed[:, 1]
    low = lax.broadcasted_iota(jnp.int32, even.shape, 1) < REST // 2
    rest = (jnp.where(low, even, swap_halves(odd)), jnp.where(low, swap_halves(even), odd))
    return [
        (wide[:, e * LEAD : e * LEAD + MAIN].reshape(-1, n).astype(jnp.bfloat16), rest[e].reshape(-1, n).astype(jnp.bfloat16))
        for e in range(2)
    ]


def swap_halves(rows):
    return jnp.concatenate([rows[:, REST // 2 :], rows[:, : REST // 2]], axis=1)


def join_rows(first, second):
    main = SRC * MAIN
    n = first.shape[-1]
    one, two = (rows[main:].reshape(-1, REST, n) for rows in (first, second))
    low = lax.broadcasted_iota(jnp.int32, one.shape, 1) < REST // 2
    even, odd = jnp.where(low, one, swap_halves(two)), jnp.where(low, swap_halves(one), two)
    mixed = jnp.stack([even, odd], axis=1).reshape(SRC, REST, n)
    runs = [rows[:main].reshape(SRC, MAIN, n) for rows in (first, second)]
    return jnp.concatenate([runs[0], mixed, runs[1]], axis=1).astype(jnp.bfloat16)


def swish(total):
    gate = total[:, :FQ]
    return gate / (1.0 + jnp.exp(-gate)) * total[:, FQ:]


def hidden_kernel(place_ref, *refs):
    rows, weights_ref, out_ref, held, here, sems, row_sems = refs[: 2 * Y], *refs[2 * Y : 2 * Y + 6]
    sums = refs[2 * Y + 6 :]
    groups = MEMBERS // DEEP
    copies = [
        pltpu.make_async_copy(
            weights_ref.at[:, (i % groups) * DEEP : (i % groups + 1) * DEEP, i // groups, :HALF], held.at[i], sems.at[i]
        )
        for i in range(C * groups)
    ]
    moves = [pltpu.make_async_copy(ref, here.at[i], row_sems.at[i]) for i, ref in enumerate(rows)]
    for move in moves[0::2]:
        move.start()
    copies[0].start()
    for move in moves[1::2]:
        move.start()
    copies[1].start()
    for i, copy in enumerate(copies):
        half, group = i // groups, i % groups
        at = slice(group * DEEP * HALF, (group + 1) * DEEP * HALF)
        if group == 0:
            for move in moves[half::2]:
                move.wait()
        blocks = [split_rows(here[2 * offset + half, :, :, at]) for offset in range(Y)]
        copy.wait()
        if i + 2 < len(copies):
            copies[i + 2].start()
        for expert, total in enumerate(sums):
            block = jnp.concatenate([b[expert][part] for part in range(2) for b in blocks], axis=0)
            weights = held[i, expert].reshape(DEEP * HALF, 2 * FQ)
            product = jnp.dot(block, weights, preferred_element_type=jnp.float32)
            total[...] = product if i == 0 else total[...] + product
    joined = join_rows(*(swish(total[...]) for total in sums))
    for offset in range(Y):
        source = lax.rem(place_ref[0] + offset, Y)
        block = joined[offset * X : (offset + 1) * X]
        for copy in range(Y):
            out_ref[copy, pl.ds(source * X, X)] = block


def down_kernel(hidden_ref, weights_ref, out_ref, held, sems, *rows):
    main = SRC * MAIN
    starts = range(0, MEMBERS, WIDE)
    copies = [
        pltpu.make_async_copy(weights_ref.at[:, start : start + WIDE, :, HALF:], held.at[i], sems.at[i])
        for i, start in enumerate(starts)
    ]
    for copy in copies:
        copy.start()
    for quarter in range(Y):
        at = slice(quarter * FQ, (quarter + 1) * FQ)
        for ref, (run, rest) in zip(rows, split_rows(hidden_ref[quarter])):
            ref[:main, at] = run
            ref[main:, at] = rest

    def result(i, expert):
        weights = jnp.concatenate(
            [
                jnp.concatenate([held[i, expert, m, half, :, q * 128 : (q + 1) * 128] for m in range(WIDE)], axis=1)
                for q in range(Y)
                for half in range(C)
            ],
            axis=0,
        )
        return jnp.dot(rows[expert][...], weights, preferred_element_type=jnp.float32)

    for i, start in enumerate(starts):
        copies[i].wait()
        joined = join_rows(result(i, 0), result(i, 1))
        for x in range(X):
            for y in range(Y):
                out_ref[x * Y + y, :, start * 128 : (start + WIDE) * 128] = joined[y * X + x]


SCALAR = pl.BlockSpec(memory_space=pltpu.SMEM)
WHOLE = pl.BlockSpec(memory_space=pltpu.VMEM)
ANY = pl.BlockSpec(memory_space=pl.ANY)


def shape(dims):
    return jax.ShapeDtypeStruct(dims, jnp.bfloat16)


def params(mebibytes):
    return pltpu.CompilerParams(vmem_limit_bytes=mebibytes << 20)


def encode(counts, routes, tokens):
    return pl.pallas_call(
        encode_kernel,
        out_shape=[shape((ALL_SLOTS, D // 2))] * 2,
        in_specs=[SCALAR, WHOLE, WHOLE],
        out_specs=[WHOLE] * 2,
        compiler_params=params(8),
        cost_estimate=pl.CostEstimate(flops=2 * ALL_SLOTS * TOK * D, bytes_accessed=2 * (TOK + ALL_SLOTS) * D, transcendentals=0),
    )(counts, routes.T, tokens)


def pack(w_gate, w_up, w_down):
    return pl.pallas_call(
        pack_kernel,
        out_shape=shape((HALF + 128, SHARD)),
        in_specs=[ANY] * 3,
        out_specs=ANY,
        scratch_shapes=[pltpu.VMEM((HALF + 128, SHARD), jnp.bfloat16), pltpu.SemaphoreType.DMA((3 + Y,))],
    )(w_gate, w_up, w_down)


def hidden_rows(place, rows, weights):
    pieces = C * MEMBERS // DEEP
    return pl.pallas_call(
        hidden_kernel,
        out_shape=shape((Y, SRC, SLOTS, FQ)),
        in_specs=[SCALAR, *[ANY] * (2 * Y), ANY],
        out_specs=WHOLE,
        scratch_shapes=[
            pltpu.VMEM((pieces, 2, DEEP, HALF, 2 * FQ), jnp.bfloat16),
            pltpu.VMEM((2 * Y, X, SLOTS, D // 2), jnp.bfloat16),
            pltpu.SemaphoreType.DMA((pieces,)),
            pltpu.SemaphoreType.DMA((2 * Y,)),
            *[pltpu.VMEM((SRC * SLOTS // 2, 2 * FQ), jnp.float32)] * 2,
        ],
        compiler_params=params(36),
        cost_estimate=pl.CostEstimate(flops=2 * ROWS * D * 2 * FQ, bytes_accessed=2 * ROWS * D + 8 * D * FQ, transcendentals=0),
    )(place, *rows, weights)


def down_rows(hidden, weights):
    pieces = MEMBERS // WIDE
    return pl.pallas_call(
        down_kernel,
        out_shape=shape((SRC, SLOTS, MEMBERS * 128)),
        in_specs=[WHOLE, ANY],
        out_specs=WHOLE,
        scratch_shapes=[
            pltpu.VMEM((pieces, 2, WIDE, C, 128, SHARD), jnp.bfloat16),
            pltpu.SemaphoreType.DMA((pieces,)),
            *[pltpu.VMEM((SRC * SLOTS // 2, F), jnp.bfloat16)] * 2,
        ],
        compiler_params=params(50),
        cost_estimate=pl.CostEstimate(flops=2 * ROWS * F * F, bytes_accessed=4 * ROWS * F + 4 * F * F, transcendentals=0),
    )(hidden, weights)


def mix(counts, routes, numerators, rows):
    return pl.pallas_call(
        mix_kernel,
        out_shape=shape((TOK, D)),
        in_specs=[SCALAR] + [WHOLE] * 3,
        out_specs=WHOLE,
        compiler_params=params(8),
    )(counts, routes.T, numerators.T, rows)


def shift(block, by):
    return lax.ppermute(block, "y", [(i, (i + by) % Y) for i in range(Y)])


def local(tokens, routes, numerators, counts, w_gate, w_up, w_down):
    place = lax.axis_index("y").astype(jnp.int32).reshape(1)
    weights = pack(w_gate, w_up, w_down)
    weights = lax.all_gather(weights, ("z", "c")).reshape(2, MEMBERS, C, HALF + 128, SHARD)
    first, second = encode(counts, routes, tokens)
    first = lax.all_to_all(first.reshape(X, SLOTS, D // 2), "x", 0, 0, tiled=True)
    second = lax.all_to_all(second.reshape(X, SLOTS, D // 2), "x", 0, 0, tiled=True)
    first_3, second_1 = shift(first, 1), shift(second, -1)
    second_3, first_1 = shift(second, 1), shift(first, -1)
    first_2, second_2 = shift(first_3, 1), shift(second_1, -1)
    rows = (first, second, first_1, second_1, first_2, second_2, first_3, second_3)
    hidden = lax.all_to_all(hidden_rows(place, rows, weights), "y", 0, 0, tiled=True)
    result = lax.all_to_all(down_rows(hidden, weights), ("x", "y"), 0, 0, tiled=True)
    return mix(counts, routes, numerators, result)


def solution(mesh):
    grid = Mesh(mesh.devices.reshape(Y, C, X, Z), ("y", "c", "x", "z"))
    tokens = ("y", "c", "x", "z")
    group = ("x", "z")
    placed = (
        P(tokens, None),
        P(tokens, None),
        P(tokens, None),
        P(tokens),
        P(group, None),
        P(group, None),
        P(None, group),
    )
    return jax.shard_map(local, mesh=grid, in_specs=placed, out_specs=P(tokens, None), check_vma=False)
```

```python
import jax
import jax.numpy as jnp
from jax import lax
from jax.experimental import pallas as pl
from jax.experimental.pallas import tpu as pltpu
from jax.sharding import Mesh
from jax.sharding import PartitionSpec as P

Y, C, X, Z = 4, 2, 4, 16
D, F, TOK = 4096, 1024, 64
SHARD = 512
MEMBERS = 8
CAP = 20
SLOTS = 2 * CAP
MAIN = 16
REST = SLOTS - 2 * MAIN
LEAD = MAIN + REST
SRC = Y * X
ROWS = SRC * SLOTS
ALL_SLOTS = X * SLOTS
FQ = F // Y
HALF = SHARD // 2
DEEP = 2
WIDE = 2


def slot_at(at):
    second = (at >= MAIN + REST // 2).astype(jnp.int32)
    slot = jnp.where(at < MAIN + REST // 2, at, jnp.where(at < LEAD, at - REST // 2, at - LEAD))
    return second, slot


def pack_kernel(gate_ref, up_ref, down_ref, out_ref, packed, sems):
    y, c = lax.axis_index("y"), lax.axis_index("c")
    rows = pl.ds(pl.multiple_of(c * HALF, HALF), HALF)
    columns = pl.ds(pl.multiple_of(y * FQ, FQ), FQ)
    copies = [
        pltpu.make_async_copy(gate_ref.at[rows, columns], packed.at[:HALF, :FQ], sems.at[0]),
        pltpu.make_async_copy(up_ref.at[rows, columns], packed.at[:HALF, FQ:], sems.at[1]),
    ]
    columns = pl.ds(pl.multiple_of(y * 128, 128), 128)
    for quarter in range(Y):
        rows = pl.ds(pl.multiple_of(quarter * FQ + c * 128, 128), 128)
        to = packed.at[HALF:, quarter * 128 : (quarter + 1) * 128]
        copies.append(pltpu.make_async_copy(down_ref.at[rows, columns], to, sems.at[2 + quarter]))
    for copy in copies:
        copy.start()
    for copy in copies:
        copy.wait()
    copy = pltpu.make_async_copy(packed, out_ref, sems.at[2 + Y])
    copy.start()
    copy.wait()


def restore(v):
    scale = (jnp.max(jnp.abs(v), axis=1, keepdims=True) + 1e-06) / 448.0
    scaled = v / scale
    x = jnp.abs(scaled)
    spacing = jnp.full_like(x, 2.0**-9)
    for shift, least in ((8, 2.0**2), (4, 2.0**-2), (2, 2.0**-4), (1, 2.0**-5)):
        big = x >= least
        x = jnp.where(big, x * 2.0**-shift, x)
        spacing = jnp.where(big, spacing * 2.0**shift, spacing)
    snapped = jnp.floor(x * 512.0 + 0.5) * spacing
    coded = jnp.where(scaled < 0.0, -snapped, snapped)
    return (coded * scale).astype(jnp.bfloat16)


def placements(count_ref, columns_ref):
    dims = (ALL_SLOTS, TOK)
    place = lax.broadcasted_iota(jnp.int32, dims, 0)
    row = lax.broadcasted_iota(jnp.int32, dims, 1)
    column = (place * 1639) >> 16
    second, slot = slot_at(place - column * SLOTS)
    expert = 2 * column + second
    live = row < count_ref[0]
    by_first, by_second = ((columns_ref[i : i + 1, :] == expert) & live for i in range(2))
    named = (by_first | by_second).astype(jnp.float32).astype(jnp.bfloat16)
    earlier = (lax.broadcasted_iota(jnp.int32, (TOK, TOK), 0) < lax.broadcasted_iota(jnp.int32, (TOK, TOK), 1))
    rank = jnp.dot(named, earlier.astype(jnp.float32).astype(jnp.bfloat16), preferred_element_type=jnp.float32)
    here = rank.astype(jnp.int32) == slot
    return by_first & here, by_second & here


def encode_kernel(count_ref, columns_ref, tokens_ref, first_ref, second_ref):
    by_first, by_second = placements(count_ref, columns_ref)
    chosen = (by_first | by_second).astype(jnp.float32).astype(jnp.bfloat16)

    def step(member, carry):
        for half, out_ref in enumerate((first_ref, second_ref)):
            start = pl.multiple_of(member * SHARD + half * HALF, HALF)
            values = tokens_ref[:, pl.ds(start, HALF)].astype(jnp.float32)
            restored = jnp.concatenate([restore(values[:, b * 128 : (b + 1) * 128]) for b in range(HALF // 128)], axis=1)
            rows = jnp.dot(chosen, restored, preferred_element_type=jnp.float32)
            out_ref[:, pl.ds(pl.multiple_of(member * HALF, HALF), HALF)] = rows.astype(jnp.bfloat16)
        return carry

    lax.fori_loop(0, MEMBERS, step, 0)


def mix_kernel(count_ref, columns_ref, numerators_ref, rows_ref, out_ref):
    by_first, by_second = placements(count_ref, columns_ref)
    share = numerators_ref[...].astype(jnp.float32) / 256.0
    shares = jnp.where(by_first, share[0:1], 0.0) + jnp.where(by_second, share[1:2], 0.0)
    shares = shares.astype(jnp.bfloat16)
    for quarter in range(Y):
        rows = jnp.concatenate([rows_ref[x * Y + quarter] for x in range(X)], axis=0)
        mixed = lax.dot_general(shares, rows, (((0,), (0,)), ((), ())), preferred_element_type=jnp.float32)
        mixed = mixed.astype(jnp.bfloat16)
        for member in range(MEMBERS):
            at = member * SHARD + quarter * 128
            out_ref[:, at : at + 128] = mixed[:, member * 128 : (member + 1) * 128]


def split_rows(block):
    wide = block.astype(jnp.float32)
    n = wide.shape[-1]
    mixed = wide[:, MAIN:LEAD].reshape(-1, 2, REST, n)
    even, odd = mixed[:, 0], mixed[:, 1]
    low = lax.broadcasted_iota(jnp.int32, even.shape, 1) < REST // 2
    rest = (jnp.where(low, even, swap_halves(odd)), jnp.where(low, swap_halves(even), odd))
    return [
        (wide[:, e * LEAD : e * LEAD + MAIN].reshape(-1, n).astype(jnp.bfloat16), rest[e].reshape(-1, n).astype(jnp.bfloat16))
        for e in range(2)
    ]


def swap_halves(rows):
    return jnp.concatenate([rows[:, REST // 2 :], rows[:, : REST // 2]], axis=1)


def join_rows(first, second):
    main = SRC * MAIN
    n = first.shape[-1]
    one, two = (rows[main:].reshape(-1, REST, n) for rows in (first, second))
    low = lax.broadcasted_iota(jnp.int32, one.shape, 1) < REST // 2
    even, odd = jnp.where(low, one, swap_halves(two)), jnp.where(low, swap_halves(one), two)
    mixed = jnp.stack([even, odd], axis=1).reshape(SRC, REST, n)
    runs = [rows[:main].reshape(SRC, MAIN, n) for rows in (first, second)]
    return jnp.concatenate([runs[0], mixed, runs[1]], axis=1).astype(jnp.bfloat16)


def swish(total):
    gate = total[:, :FQ]
    return gate / (1.0 + jnp.exp(-gate)) * total[:, FQ:]


def hidden_kernel(place_ref, *refs):
    rows, weights_ref, out_ref, held, here, sems, row_sems = refs[: 2 * Y], *refs[2 * Y : 2 * Y + 6]
    sums = refs[2 * Y + 6 :]
    groups = MEMBERS // DEEP
    copies = [
        pltpu.make_async_copy(
            weights_ref.at[:, (i % groups) * DEEP : (i % groups + 1) * DEEP, i // groups, :HALF], held.at[i], sems.at[i]
        )
        for i in range(C * groups)
    ]
    moves = [pltpu.make_async_copy(ref, here.at[i], row_sems.at[i]) for i, ref in enumerate(rows)]
    copies[0].start()
    for move in moves[0::2]:
        move.start()
    copies[1].start()
    for move in moves[1::2]:
        move.start()
    copies[2].start()
    for i, copy in enumerate(copies):
        half, group = i // groups, i % groups
        at = slice(group * DEEP * HALF, (group + 1) * DEEP * HALF)
        if group == 0:
            for move in moves[half::2]:
                move.wait()
        blocks = [split_rows(here[2 * offset + half, :, :, at]) for offset in range(Y)]
        copy.wait()
        if i + 3 < len(copies):
            copies[i + 3].start()
        for expert, total in enumerate(sums):
            block = jnp.concatenate([b[expert][part] for part in range(2) for b in blocks], axis=0)
            weights = held[i, expert].reshape(DEEP * HALF, 2 * FQ)
            product = jnp.dot(block, weights, preferred_element_type=jnp.float32)
            total[...] = product if i == 0 else total[...] + product
    joined = join_rows(*(swish(total[...]) for total in sums))
    for offset in range(Y):
        source = lax.rem(place_ref[0] + offset, Y)
        block = joined[offset * X : (offset + 1) * X]
        for copy in range(Y):
            out_ref[copy, pl.ds(source * X, X)] = block


def down_kernel(hidden_ref, weights_ref, out_ref, held, sems, *rows):
    main = SRC * MAIN
    starts = range(0, MEMBERS, WIDE)
    copies = [
        pltpu.make_async_copy(weights_ref.at[:, start : start + WIDE, :, HALF:], held.at[i], sems.at[i])
        for i, start in enumerate(starts)
    ]
    for copy in copies:
        copy.start()
    for quarter in range(Y):
        at = slice(quarter * FQ, (quarter + 1) * FQ)
        for ref, (run, rest) in zip(rows, split_rows(hidden_ref[quarter])):
            ref[:main, at] = run
            ref[main:, at] = rest

    def result(i, expert):
        weights = jnp.concatenate(
            [
                jnp.concatenate([held[i, expert, m, half, :, q * 128 : (q + 1) * 128] for m in range(WIDE)], axis=1)
                for q in range(Y)
                for half in range(C)
            ],
            axis=0,
        )
        return jnp.dot(rows[expert][...], weights, preferred_element_type=jnp.float32)

    for i, start in enumerate(starts):
        copies[i].wait()
        joined = join_rows(result(i, 0), result(i, 1))
        for x in range(X):
            for y in range(Y):
                out_ref[x * Y + y, :, start * 128 : (start + WIDE) * 128] = joined[y * X + x]


SCALAR = pl.BlockSpec(memory_space=pltpu.SMEM)
WHOLE = pl.BlockSpec(memory_space=pltpu.VMEM)
ANY = pl.BlockSpec(memory_space=pl.ANY)


def shape(dims):
    return jax.ShapeDtypeStruct(dims, jnp.bfloat16)


def params(mebibytes):
    return pltpu.CompilerParams(vmem_limit_bytes=mebibytes << 20)


def encode(counts, routes, tokens):
    return pl.pallas_call(
        encode_kernel,
        out_shape=[shape((ALL_SLOTS, D // 2))] * 2,
        in_specs=[SCALAR, WHOLE, WHOLE],
        out_specs=[WHOLE] * 2,
        compiler_params=params(8),
        cost_estimate=pl.CostEstimate(flops=2 * ALL_SLOTS * TOK * D, bytes_accessed=2 * (TOK + ALL_SLOTS) * D, transcendentals=0),
    )(counts, routes.T, tokens)


def pack(w_gate, w_up, w_down):
    return pl.pallas_call(
        pack_kernel,
        out_shape=shape((HALF + 128, SHARD)),
        in_specs=[ANY] * 3,
        out_specs=ANY,
        scratch_shapes=[pltpu.VMEM((HALF + 128, SHARD), jnp.bfloat16), pltpu.SemaphoreType.DMA((3 + Y,))],
    )(w_gate, w_up, w_down)


def hidden_rows(place, rows, weights):
    pieces = C * MEMBERS // DEEP
    return pl.pallas_call(
        hidden_kernel,
        out_shape=shape((Y, SRC, SLOTS, FQ)),
        in_specs=[SCALAR, *[ANY] * (2 * Y), ANY],
        out_specs=WHOLE,
        scratch_shapes=[
            pltpu.VMEM((pieces, 2, DEEP, HALF, 2 * FQ), jnp.bfloat16),
            pltpu.VMEM((2 * Y, X, SLOTS, D // 2), jnp.bfloat16),
            pltpu.SemaphoreType.DMA((pieces,)),
            pltpu.SemaphoreType.DMA((2 * Y,)),
            *[pltpu.VMEM((SRC * SLOTS // 2, 2 * FQ), jnp.float32)] * 2,
        ],
        compiler_params=params(36),
        cost_estimate=pl.CostEstimate(flops=2 * ROWS * D * 2 * FQ, bytes_accessed=2 * ROWS * D + 8 * D * FQ, transcendentals=0),
    )(place, *rows, weights)


def down_rows(hidden, weights):
    pieces = MEMBERS // WIDE
    return pl.pallas_call(
        down_kernel,
        out_shape=shape((SRC, SLOTS, MEMBERS * 128)),
        in_specs=[WHOLE, ANY],
        out_specs=WHOLE,
        scratch_shapes=[
            pltpu.VMEM((pieces, 2, WIDE, C, 128, SHARD), jnp.bfloat16),
            pltpu.SemaphoreType.DMA((pieces,)),
            *[pltpu.VMEM((SRC * SLOTS // 2, F), jnp.bfloat16)] * 2,
        ],
        compiler_params=params(50),
        cost_estimate=pl.CostEstimate(flops=2 * ROWS * F * F, bytes_accessed=4 * ROWS * F + 4 * F * F, transcendentals=0),
    )(hidden, weights)


def mix(counts, routes, numerators, rows):
    return pl.pallas_call(
        mix_kernel,
        out_shape=shape((TOK, D)),
        in_specs=[SCALAR] + [WHOLE] * 3,
        out_specs=WHOLE,
        compiler_params=params(8),
    )(counts, routes.T, numerators.T, rows)


def shift(block, by):
    return lax.ppermute(block, "y", [(i, (i + by) % Y) for i in range(Y)])


def local(tokens, routes, numerators, counts, w_gate, w_up, w_down):
    place = lax.axis_index("y").astype(jnp.int32).reshape(1)
    weights = pack(w_gate, w_up, w_down)
    weights = lax.all_gather(weights, ("z", "c")).reshape(2, MEMBERS, C, HALF + 128, SHARD)
    first, second = encode(counts, routes, tokens)
    first = lax.all_to_all(first.reshape(X, SLOTS, D // 2), "x", 0, 0, tiled=True)
    second = lax.all_to_all(second.reshape(X, SLOTS, D // 2), "x", 0, 0, tiled=True)
    first_3, second_1 = shift(first, 1), shift(second, -1)
    second_3, first_1 = shift(second, 1), shift(first, -1)
    first_2, second_2 = shift(first_3, 1), shift(second_1, -1)
    rows = (first, second, first_1, second_1, first_2, second_2, first_3, second_3)
    hidden = lax.all_to_all(hidden_rows(place, rows, weights), "y", 0, 0, tiled=True)
    result = lax.all_to_all(down_rows(hidden, weights), ("x", "y"), 0, 0, tiled=True)
    return mix(counts, routes, numerators, result)


def solution(mesh):
    grid = Mesh(mesh.devices.reshape(Y, C, X, Z), ("y", "c", "x", "z"))
    tokens = ("y", "c", "x", "z")
    group = ("x", "z")
    placed = (
        P(tokens, None),
        P(tokens, None),
        P(tokens, None),
        P(tokens),
        P(group, None),
        P(group, None),
        P(None, group),
    )
    return jax.shard_map(local, mesh=grid, in_specs=placed, out_specs=P(tokens, None), check_vma=False)
```

```python
import jax
import jax.numpy as jnp
from jax import lax
from jax.experimental import pallas as pl
from jax.experimental.pallas import tpu as pltpu
from jax.sharding import Mesh
from jax.sharding import PartitionSpec as P

Y, C, X, Z = 4, 2, 4, 16
D, F, TOK = 4096, 1024, 64
SHARD = 512
MEMBERS = 8
CAP = 20
SLOTS = 2 * CAP
MAIN = 16
REST = SLOTS - 2 * MAIN
LEAD = MAIN + REST
SRC = Y * X
ROWS = SRC * SLOTS
ALL_SLOTS = X * SLOTS
FQ = F // Y
HALF = SHARD // 2
DEEP = 2
WIDE = 2


def slot_at(at):
    second = (at >= MAIN + REST // 2).astype(jnp.int32)
    slot = jnp.where(at < MAIN + REST // 2, at, jnp.where(at < LEAD, at - REST // 2, at - LEAD))
    return second, slot


def pack_kernel(gate_ref, up_ref, down_ref, out_ref, packed, sems):
    y, c = lax.axis_index("y"), lax.axis_index("c")
    rows = pl.ds(pl.multiple_of(c * HALF, HALF), HALF)
    columns = pl.ds(pl.multiple_of(y * FQ, FQ), FQ)
    copies = [
        pltpu.make_async_copy(gate_ref.at[rows, columns], packed.at[:HALF, :FQ], sems.at[0]),
        pltpu.make_async_copy(up_ref.at[rows, columns], packed.at[:HALF, FQ:], sems.at[1]),
    ]
    columns = pl.ds(pl.multiple_of(y * 128, 128), 128)
    for quarter in range(Y):
        rows = pl.ds(pl.multiple_of(quarter * FQ + c * 128, 128), 128)
        to = packed.at[HALF:, quarter * 128 : (quarter + 1) * 128]
        copies.append(pltpu.make_async_copy(down_ref.at[rows, columns], to, sems.at[2 + quarter]))
    for copy in copies:
        copy.start()
    for copy in copies:
        copy.wait()
    copy = pltpu.make_async_copy(packed, out_ref, sems.at[2 + Y])
    copy.start()
    copy.wait()


def restore(v):
    scale = (jnp.max(jnp.abs(v), axis=1, keepdims=True) + 1e-06) / 448.0
    scaled = v / scale
    x = jnp.abs(scaled)
    spacing = jnp.full_like(x, 2.0**-9)
    for shift, least in ((8, 2.0**2), (4, 2.0**-2), (2, 2.0**-4), (1, 2.0**-5)):
        big = x >= least
        x = jnp.where(big, x * 2.0**-shift, x)
        spacing = jnp.where(big, spacing * 2.0**shift, spacing)
    snapped = jnp.floor(x * 512.0 + 0.5) * spacing
    coded = jnp.where(scaled < 0.0, -snapped, snapped)
    return (coded * scale).astype(jnp.bfloat16)


def placements(count_ref, columns_ref):
    dims = (ALL_SLOTS, TOK)
    place = lax.broadcasted_iota(jnp.int32, dims, 0)
    row = lax.broadcasted_iota(jnp.int32, dims, 1)
    column = (place * 1639) >> 16
    second, slot = slot_at(place - column * SLOTS)
    expert = 2 * column + second
    live = row < count_ref[0]
    by_first, by_second = ((columns_ref[i : i + 1, :] == expert) & live for i in range(2))
    named = (by_first | by_second).astype(jnp.float32).astype(jnp.bfloat16)
    earlier = (lax.broadcasted_iota(jnp.int32, (TOK, TOK), 0) < lax.broadcasted_iota(jnp.int32, (TOK, TOK), 1))
    rank = jnp.dot(named, earlier.astype(jnp.float32).astype(jnp.bfloat16), preferred_element_type=jnp.float32)
    here = rank.astype(jnp.int32) == slot
    return by_first & here, by_second & here


def encode_kernel(count_ref, columns_ref, tokens_ref, first_ref, second_ref):
    by_first, by_second = placements(count_ref, columns_ref)
    chosen = (by_first | by_second).astype(jnp.float32).astype(jnp.bfloat16)

    def step(member, carry):
        for half, out_ref in enumerate((first_ref, second_ref)):
            start = pl.multiple_of(member * SHARD + half * HALF, HALF)
            values = tokens_ref[:, pl.ds(start, HALF)].astype(jnp.float32)
            restored = jnp.concatenate([restore(values[:, b * 128 : (b + 1) * 128]) for b in range(HALF // 128)], axis=1)
            rows = jnp.dot(chosen, restored, preferred_element_type=jnp.float32)
            out_ref[:, pl.ds(pl.multiple_of(member * HALF, HALF), HALF)] = rows.astype(jnp.bfloat16)
        return carry

    lax.fori_loop(0, MEMBERS, step, 0)


def mix_kernel(count_ref, columns_ref, numerators_ref, rows_ref, out_ref):
    by_first, by_second = placements(count_ref, columns_ref)
    share = numerators_ref[...].astype(jnp.float32) / 256.0
    shares = jnp.where(by_first, share[0:1], 0.0) + jnp.where(by_second, share[1:2], 0.0)
    shares = shares.astype(jnp.bfloat16)
    for quarter in range(Y):
        rows = jnp.concatenate([rows_ref[x * Y + quarter] for x in range(X)], axis=0)
        mixed = lax.dot_general(shares, rows, (((0,), (0,)), ((), ())), preferred_element_type=jnp.float32)
        mixed = mixed.astype(jnp.bfloat16)
        for member in range(MEMBERS):
            at = member * SHARD + quarter * 128
            out_ref[:, at : at + 128] = mixed[:, member * 128 : (member + 1) * 128]


def split_rows(block):
    wide = block.astype(jnp.float32)
    n = wide.shape[-1]
    mixed = wide[:, MAIN:LEAD].reshape(-1, 2, REST, n)
    even, odd = mixed[:, 0], mixed[:, 1]
    low = lax.broadcasted_iota(jnp.int32, even.shape, 1) < REST // 2
    rest = (jnp.where(low, even, swap_halves(odd)), jnp.where(low, swap_halves(even), odd))
    return [
        (wide[:, e * LEAD : e * LEAD + MAIN].reshape(-1, n).astype(jnp.bfloat16), rest[e].reshape(-1, n).astype(jnp.bfloat16))
        for e in range(2)
    ]


def swap_halves(rows):
    return jnp.concatenate([rows[:, REST // 2 :], rows[:, : REST // 2]], axis=1)


def join_rows(first, second):
    main = SRC * MAIN
    n = first.shape[-1]
    one, two = (rows[main:].reshape(-1, REST, n) for rows in (first, second))
    low = lax.broadcasted_iota(jnp.int32, one.shape, 1) < REST // 2
    even, odd = jnp.where(low, one, swap_halves(two)), jnp.where(low, swap_halves(one), two)
    mixed = jnp.stack([even, odd], axis=1).reshape(SRC, REST, n)
    runs = [rows[:main].reshape(SRC, MAIN, n) for rows in (first, second)]
    return jnp.concatenate([runs[0], mixed, runs[1]], axis=1).astype(jnp.bfloat16)


def swish(total):
    gate = total[:, :FQ]
    return gate / (1.0 + jnp.exp(-gate)) * total[:, FQ:]


def hidden_kernel(place_ref, *refs):
    rows, weights_ref, out_ref, held, here, sems, row_sems = refs[: 2 * Y], *refs[2 * Y : 2 * Y + 6]
    sums = refs[2 * Y + 6 :]
    groups = MEMBERS // DEEP
    copies = [
        pltpu.make_async_copy(
            weights_ref.at[:, (i % groups) * DEEP : (i % groups + 1) * DEEP, i // groups, :HALF], held.at[i], sems.at[i]
        )
        for i in range(C * groups)
    ]
    moves = [pltpu.make_async_copy(ref, here.at[i], row_sems.at[i]) for i, ref in enumerate(rows)]
    copies[0].start()
    for move in moves[0::2]:
        move.start()
    copies[1].start()
    for move in moves[1::2]:
        move.start()
    copies[2].start()
    for i, copy in enumerate(copies):
        half, group = i // groups, i % groups
        at = slice(group * DEEP * HALF, (group + 1) * DEEP * HALF)
        if group == 0:
            for move in moves[half::2]:
                move.wait()
        blocks = [split_rows(here[2 * offset + half, :, :, at]) for offset in range(Y)]
        copy.wait()
        if i + 3 < len(copies):
            copies[i + 3].start()
        for expert, total in enumerate(sums):
            block = jnp.concatenate([b[expert][part] for part in range(2) for b in blocks], axis=0)
            weights = held[i, expert].reshape(DEEP * HALF, 2 * FQ)
            product = jnp.dot(block, weights, preferred_element_type=jnp.float32)
            total[...] = product if i == 0 else total[...] + product
    joined = join_rows(*(swish(total[...]) for total in sums))
    for offset in range(Y):
        source = lax.rem(place_ref[0] + offset, Y)
        out_ref[pl.ds(source * X, X)] = joined[offset * X : (offset + 1) * X]


def down_kernel(place_ref, *refs):
    hidden, weights_ref, out_ref, held, sems = refs[:Y], *refs[Y : Y + 4]
    rows = refs[Y + 4 :]
    main = SRC * MAIN
    starts = range(0, MEMBERS, WIDE)
    copies = [
        pltpu.make_async_copy(weights_ref.at[:, start : start + WIDE, :, HALF:], held.at[i], sems.at[i])
        for i, start in enumerate(starts)
    ]
    for copy in copies:
        copy.start()
    for offset in range(Y):
        at = pl.ds(pl.multiple_of(lax.rem(place_ref[0] + offset, Y) * FQ, FQ), FQ)
        for ref, (run, rest) in zip(rows, split_rows(hidden[offset][...])):
            ref[:main, at] = run
            ref[main:, at] = rest

    def result(i, expert):
        weights = jnp.concatenate(
            [
                jnp.concatenate([held[i, expert, m, half, :, q * 128 : (q + 1) * 128] for m in range(WIDE)], axis=1)
                for q in range(Y)
                for half in range(C)
            ],
            axis=0,
        )
        return jnp.dot(rows[expert][...], weights, preferred_element_type=jnp.float32)

    for i, start in enumerate(starts):
        copies[i].wait()
        joined = join_rows(result(i, 0), result(i, 1))
        for x in range(X):
            for y in range(Y):
                out_ref[x * Y + y, :, start * 128 : (start + WIDE) * 128] = joined[y * X + x]


SCALAR = pl.BlockSpec(memory_space=pltpu.SMEM)
WHOLE = pl.BlockSpec(memory_space=pltpu.VMEM)
ANY = pl.BlockSpec(memory_space=pl.ANY)


def shape(dims):
    return jax.ShapeDtypeStruct(dims, jnp.bfloat16)


def params(mebibytes):
    return pltpu.CompilerParams(vmem_limit_bytes=mebibytes << 20)


def encode(counts, routes, tokens):
    return pl.pallas_call(
        encode_kernel,
        out_shape=[shape((ALL_SLOTS, D // 2))] * 2,
        in_specs=[SCALAR, WHOLE, WHOLE],
        out_specs=[WHOLE] * 2,
        compiler_params=params(8),
        cost_estimate=pl.CostEstimate(flops=2 * ALL_SLOTS * TOK * D, bytes_accessed=2 * (TOK + ALL_SLOTS) * D, transcendentals=0),
    )(counts, routes.T, tokens)


def pack(w_gate, w_up, w_down):
    return pl.pallas_call(
        pack_kernel,
        out_shape=shape((HALF + 128, SHARD)),
        in_specs=[ANY] * 3,
        out_specs=ANY,
        scratch_shapes=[pltpu.VMEM((HALF + 128, SHARD), jnp.bfloat16), pltpu.SemaphoreType.DMA((3 + Y,))],
    )(w_gate, w_up, w_down)


def hidden_rows(place, rows, weights):
    pieces = C * MEMBERS // DEEP
    return pl.pallas_call(
        hidden_kernel,
        out_shape=shape((SRC, SLOTS, FQ)),
        in_specs=[SCALAR, *[ANY] * (2 * Y), ANY],
        out_specs=WHOLE,
        scratch_shapes=[
            pltpu.VMEM((pieces, 2, DEEP, HALF, 2 * FQ), jnp.bfloat16),
            pltpu.VMEM((2 * Y, X, SLOTS, D // 2), jnp.bfloat16),
            pltpu.SemaphoreType.DMA((pieces,)),
            pltpu.SemaphoreType.DMA((2 * Y,)),
            *[pltpu.VMEM((SRC * SLOTS // 2, 2 * FQ), jnp.float32)] * 2,
        ],
        compiler_params=params(36),
        cost_estimate=pl.CostEstimate(flops=2 * ROWS * D * 2 * FQ, bytes_accessed=2 * ROWS * D + 8 * D * FQ, transcendentals=0),
    )(place, *rows, weights)


def down_rows(place, hidden, weights):
    pieces = MEMBERS // WIDE
    return pl.pallas_call(
        down_kernel,
        out_shape=shape((SRC, SLOTS, MEMBERS * 128)),
        in_specs=[SCALAR, *[WHOLE] * Y, ANY],
        out_specs=WHOLE,
        scratch_shapes=[
            pltpu.VMEM((pieces, 2, WIDE, C, 128, SHARD), jnp.bfloat16),
            pltpu.SemaphoreType.DMA((pieces,)),
            *[pltpu.VMEM((SRC * SLOTS // 2, F), jnp.bfloat16)] * 2,
        ],
        compiler_params=params(50),
        cost_estimate=pl.CostEstimate(flops=2 * ROWS * F * F, bytes_accessed=4 * ROWS * F + 4 * F * F, transcendentals=0),
    )(place, *hidden, weights)


def mix(counts, routes, numerators, rows):
    return pl.pallas_call(
        mix_kernel,
        out_shape=shape((TOK, D)),
        in_specs=[SCALAR] + [WHOLE] * 3,
        out_specs=WHOLE,
        compiler_params=params(8),
    )(counts, routes.T, numerators.T, rows)


def shift(block, by):
    return lax.ppermute(block, "y", [(i, (i + by) % Y) for i in range(Y)])


def local(tokens, routes, numerators, counts, w_gate, w_up, w_down):
    place = lax.axis_index("y").astype(jnp.int32).reshape(1)
    weights = pack(w_gate, w_up, w_down)
    weights = lax.all_gather(weights, ("z", "c")).reshape(2, MEMBERS, C, HALF + 128, SHARD)
    first, second = encode(counts, routes, tokens)
    first = lax.all_to_all(first.reshape(X, SLOTS, D // 2), "x", 0, 0, tiled=True)
    second = lax.all_to_all(second.reshape(X, SLOTS, D // 2), "x", 0, 0, tiled=True)
    first_3, second_1 = shift(first, 1), shift(second, -1)
    second_3, first_1 = shift(second, 1), shift(first, -1)
    first_2, second_2 = shift(first_3, 1), shift(second_1, -1)
    rows = (first, second, first_1, second_1, first_2, second_2, first_3, second_3)
    own = hidden_rows(place, rows, weights)
    hidden = (own, shift(own, -1), shift(own, 2), shift(own, 1))
    result = lax.all_to_all(down_rows(place, hidden, weights), ("x", "y"), 0, 0, tiled=True)
    return mix(counts, routes, numerators, result)


def solution(mesh):
    grid = Mesh(mesh.devices.reshape(Y, C, X, Z), ("y", "c", "x", "z"))
    tokens = ("y", "c", "x", "z")
    group = ("x", "z")
    placed = (
        P(tokens, None),
        P(tokens, None),
        P(tokens, None),
        P(tokens),
        P(group, None),
        P(group, None),
        P(None, group),
    )
    return jax.shard_map(local, mesh=grid, in_specs=placed, out_specs=P(tokens, None), check_vma=False)
```

```python
import jax
import jax.numpy as jnp
from jax import lax
from jax.experimental import pallas as pl
from jax.experimental.pallas import tpu as pltpu
from jax.sharding import Mesh
from jax.sharding import PartitionSpec as P

Y, C, X, Z = 4, 2, 4, 16
D, F, TOK = 4096, 1024, 64
SHARD = 512
MEMBERS = 8
CAP = 20
SLOTS = 2 * CAP
MAIN = 16
REST = SLOTS - 2 * MAIN
LEAD = MAIN + REST
SRC = Y * X
ROWS = SRC * SLOTS
ALL_SLOTS = X * SLOTS
FQ = F // Y
HALF = SHARD // 2
DEEP = 2
WIDE = 2


def slot_at(at):
    second = (at >= MAIN + REST // 2).astype(jnp.int32)
    slot = jnp.where(at < MAIN + REST // 2, at, jnp.where(at < LEAD, at - REST // 2, at - LEAD))
    return second, slot


def pack_kernel(gate_ref, up_ref, down_ref, out_ref, packed, sems):
    y, c = lax.axis_index("y"), lax.axis_index("c")
    rows = pl.ds(pl.multiple_of(c * HALF, HALF), HALF)
    columns = pl.ds(pl.multiple_of(y * FQ, FQ), FQ)
    copies = [
        pltpu.make_async_copy(gate_ref.at[rows, columns], packed.at[:HALF, :FQ], sems.at[0]),
        pltpu.make_async_copy(up_ref.at[rows, columns], packed.at[:HALF, FQ:], sems.at[1]),
    ]
    columns = pl.ds(pl.multiple_of(y * 128, 128), 128)
    for quarter in range(Y):
        rows = pl.ds(pl.multiple_of(quarter * FQ + c * 128, 128), 128)
        to = packed.at[HALF:, quarter * 128 : (quarter + 1) * 128]
        copies.append(pltpu.make_async_copy(down_ref.at[rows, columns], to, sems.at[2 + quarter]))
    for copy in copies:
        copy.start()
    for copy in copies:
        copy.wait()
    copy = pltpu.make_async_copy(packed, out_ref, sems.at[2 + Y])
    copy.start()
    copy.wait()


def restore(v):
    scale = (jnp.max(jnp.abs(v), axis=1, keepdims=True) + 1e-06) / 448.0
    scaled = v / scale
    x = jnp.abs(scaled)
    spacing = jnp.full_like(x, 2.0**-9)
    for shift, least in ((8, 2.0**2), (4, 2.0**-2), (2, 2.0**-4), (1, 2.0**-5)):
        big = x >= least
        x = jnp.where(big, x * 2.0**-shift, x)
        spacing = jnp.where(big, spacing * 2.0**shift, spacing)
    snapped = jnp.floor(x * 512.0 + 0.5) * spacing
    coded = jnp.where(scaled < 0.0, -snapped, snapped)
    return (coded * scale).astype(jnp.bfloat16)


def placements(count_ref, columns_ref):
    dims = (ALL_SLOTS, TOK)
    place = lax.broadcasted_iota(jnp.int32, dims, 0)
    row = lax.broadcasted_iota(jnp.int32, dims, 1)
    column = (place * 1639) >> 16
    second, slot = slot_at(place - column * SLOTS)
    expert = 2 * column + second
    live = row < count_ref[0]
    by_first, by_second = ((columns_ref[i : i + 1, :] == expert) & live for i in range(2))
    named = (by_first | by_second).astype(jnp.float32).astype(jnp.bfloat16)
    earlier = (lax.broadcasted_iota(jnp.int32, (TOK, TOK), 0) < lax.broadcasted_iota(jnp.int32, (TOK, TOK), 1))
    rank = jnp.dot(named, earlier.astype(jnp.float32).astype(jnp.bfloat16), preferred_element_type=jnp.float32)
    here = rank.astype(jnp.int32) == slot
    return by_first & here, by_second & here


def encode_kernel(count_ref, columns_ref, numerators_ref, tokens_ref, first_ref, second_ref, shares_ref):
    by_first, by_second = placements(count_ref, columns_ref)
    chosen = (by_first | by_second).astype(jnp.float32).astype(jnp.bfloat16)
    share = numerators_ref[...].astype(jnp.float32) / 256.0
    shares = jnp.where(by_first, share[0:1], 0.0) + jnp.where(by_second, share[1:2], 0.0)
    shares_ref[...] = shares.astype(jnp.bfloat16)

    def step(member, carry):
        for half, out_ref in enumerate((first_ref, second_ref)):
            start = pl.multiple_of(member * SHARD + half * HALF, HALF)
            values = tokens_ref[:, pl.ds(start, HALF)].astype(jnp.float32)
            restored = jnp.concatenate([restore(values[:, b * 128 : (b + 1) * 128]) for b in range(HALF // 128)], axis=1)
            rows = jnp.dot(chosen, restored, preferred_element_type=jnp.float32)
            out_ref[:, pl.ds(pl.multiple_of(member * HALF, HALF), HALF)] = rows.astype(jnp.bfloat16)
        return carry

    lax.fori_loop(0, MEMBERS, step, 0)


def mix_kernel(shares_ref, rows_ref, out_ref):
    shares = shares_ref[...]
    for quarter in range(Y):
        rows = jnp.concatenate([rows_ref[x * Y + quarter] for x in range(X)], axis=0)
        mixed = lax.dot_general(shares, rows, (((0,), (0,)), ((), ())), preferred_element_type=jnp.float32)
        mixed = mixed.astype(jnp.bfloat16)
        for member in range(MEMBERS):
            at = member * SHARD + quarter * 128
            out_ref[:, at : at + 128] = mixed[:, member * 128 : (member + 1) * 128]


def split_rows(block):
    wide = block.astype(jnp.float32)
    n = wide.shape[-1]
    mixed = wide[:, MAIN:LEAD].reshape(-1, 2, REST, n)
    even, odd = mixed[:, 0], mixed[:, 1]
    low = lax.broadcasted_iota(jnp.int32, even.shape, 1) < REST // 2
    rest = (jnp.where(low, even, swap_halves(odd)), jnp.where(low, swap_halves(even), odd))
    return [
        (wide[:, e * LEAD : e * LEAD + MAIN].reshape(-1, n).astype(jnp.bfloat16), rest[e].reshape(-1, n).astype(jnp.bfloat16))
        for e in range(2)
    ]


def swap_halves(rows):
    return jnp.concatenate([rows[:, REST // 2 :], rows[:, : REST // 2]], axis=1)


def join_rows(first, second):
    main = SRC * MAIN
    n = first.shape[-1]
    one, two = (rows[main:].reshape(-1, REST, n) for rows in (first, second))
    low = lax.broadcasted_iota(jnp.int32, one.shape, 1) < REST // 2
    even, odd = jnp.where(low, one, swap_halves(two)), jnp.where(low, swap_halves(one), two)
    mixed = jnp.stack([even, odd], axis=1).reshape(SRC, REST, n)
    runs = [rows[:main].reshape(SRC, MAIN, n) for rows in (first, second)]
    return jnp.concatenate([runs[0], mixed, runs[1]], axis=1).astype(jnp.bfloat16)


def swish(total):
    gate = total[:, :FQ]
    return gate / (1.0 + jnp.exp(-gate)) * total[:, FQ:]


def hidden_kernel(place_ref, *refs):
    rows, weights_ref, out_ref, held, here, sems, row_sems = refs[: 2 * Y], *refs[2 * Y : 2 * Y + 6]
    sums = refs[2 * Y + 6 :]
    groups = MEMBERS // DEEP
    copies = [
        pltpu.make_async_copy(
            weights_ref.at[:, (i % groups) * DEEP : (i % groups + 1) * DEEP, i // groups, :HALF], held.at[i], sems.at[i]
        )
        for i in range(C * groups)
    ]
    moves = [pltpu.make_async_copy(ref, here.at[i], row_sems.at[i]) for i, ref in enumerate(rows)]
    copies[0].start()
    for move in moves[0::2]:
        move.start()
    copies[1].start()
    for move in moves[1::2]:
        move.start()
    copies[2].start()
    for i, copy in enumerate(copies):
        half, group = i // groups, i % groups
        at = slice(group * DEEP * HALF, (group + 1) * DEEP * HALF)
        if group == 0:
            for move in moves[half::2]:
                move.wait()
        blocks = [split_rows(here[2 * offset + half, :, :, at]) for offset in range(Y)]
        copy.wait()
        if i + 3 < len(copies):
            copies[i + 3].start()
        for expert, total in enumerate(sums):
            block = jnp.concatenate([b[expert][part] for part in range(2) for b in blocks], axis=0)
            weights = held[i, expert].reshape(DEEP * HALF, 2 * FQ)
            product = jnp.dot(block, weights, preferred_element_type=jnp.float32)
            total[...] = product if i == 0 else total[...] + product
    joined = join_rows(*(swish(total[...]) for total in sums))
    for offset in range(Y):
        source = lax.rem(place_ref[0] + offset, Y)
        block = joined[offset * X : (offset + 1) * X]
        for copy in range(Y):
            out_ref[copy, pl.ds(source * X, X)] = block


def down_kernel(hidden_ref, weights_ref, out_ref, held, sems, *rows):
    main = SRC * MAIN
    starts = range(0, MEMBERS, WIDE)
    copies = [
        pltpu.make_async_copy(weights_ref.at[:, start : start + WIDE, :, HALF:], held.at[i], sems.at[i])
        for i, start in enumerate(starts)
    ]
    for copy in copies:
        copy.start()
    for quarter in range(Y):
        at = slice(quarter * FQ, (quarter + 1) * FQ)
        for ref, (run, rest) in zip(rows, split_rows(hidden_ref[quarter])):
            ref[:main, at] = run
            ref[main:, at] = rest

    def result(i, expert):
        weights = jnp.concatenate(
            [
                jnp.concatenate([held[i, expert, m, half, :, q * 128 : (q + 1) * 128] for m in range(WIDE)], axis=1)
                for q in range(Y)
                for half in range(C)
            ],
            axis=0,
        )
        return jnp.dot(rows[expert][...], weights, preferred_element_type=jnp.float32)

    for i, start in enumerate(starts):
        copies[i].wait()
        joined = join_rows(result(i, 0), result(i, 1))
        for x in range(X):
            for y in range(Y):
                out_ref[x * Y + y, :, start * 128 : (start + WIDE) * 128] = joined[y * X + x]


SCALAR = pl.BlockSpec(memory_space=pltpu.SMEM)
WHOLE = pl.BlockSpec(memory_space=pltpu.VMEM)
ANY = pl.BlockSpec(memory_space=pl.ANY)


def shape(dims):
    return jax.ShapeDtypeStruct(dims, jnp.bfloat16)


def params(mebibytes):
    return pltpu.CompilerParams(vmem_limit_bytes=mebibytes << 20)


def encode(counts, routes, numerators, tokens):
    return pl.pallas_call(
        encode_kernel,
        out_shape=[*[shape((ALL_SLOTS, D // 2))] * 2, shape((ALL_SLOTS, TOK))],
        in_specs=[SCALAR, *[WHOLE] * 3],
        out_specs=[WHOLE] * 3,
        compiler_params=params(8),
        cost_estimate=pl.CostEstimate(flops=2 * ALL_SLOTS * TOK * D, bytes_accessed=2 * (TOK + ALL_SLOTS) * D, transcendentals=0),
    )(counts, routes.T, numerators.T, tokens)


def pack(w_gate, w_up, w_down):
    return pl.pallas_call(
        pack_kernel,
        out_shape=shape((HALF + 128, SHARD)),
        in_specs=[ANY] * 3,
        out_specs=ANY,
        scratch_shapes=[pltpu.VMEM((HALF + 128, SHARD), jnp.bfloat16), pltpu.SemaphoreType.DMA((3 + Y,))],
    )(w_gate, w_up, w_down)


def hidden_rows(place, rows, weights):
    pieces = C * MEMBERS // DEEP
    return pl.pallas_call(
        hidden_kernel,
        out_shape=shape((Y, SRC, SLOTS, FQ)),
        in_specs=[SCALAR, *[ANY] * (2 * Y), ANY],
        out_specs=WHOLE,
        scratch_shapes=[
            pltpu.VMEM((pieces, 2, DEEP, HALF, 2 * FQ), jnp.bfloat16),
            pltpu.VMEM((2 * Y, X, SLOTS, D // 2), jnp.bfloat16),
            pltpu.SemaphoreType.DMA((pieces,)),
            pltpu.SemaphoreType.DMA((2 * Y,)),
            *[pltpu.VMEM((SRC * SLOTS // 2, 2 * FQ), jnp.float32)] * 2,
        ],
        compiler_params=params(36),
        cost_estimate=pl.CostEstimate(flops=2 * ROWS * D * 2 * FQ, bytes_accessed=2 * ROWS * D + 8 * D * FQ, transcendentals=0),
    )(place, *rows, weights)


def down_rows(hidden, weights):
    pieces = MEMBERS // WIDE
    return pl.pallas_call(
        down_kernel,
        out_shape=shape((SRC, SLOTS, MEMBERS * 128)),
        in_specs=[WHOLE, ANY],
        out_specs=WHOLE,
        scratch_shapes=[
            pltpu.VMEM((pieces, 2, WIDE, C, 128, SHARD), jnp.bfloat16),
            pltpu.SemaphoreType.DMA((pieces,)),
            *[pltpu.VMEM((SRC * SLOTS // 2, F), jnp.bfloat16)] * 2,
        ],
        compiler_params=params(50),
        cost_estimate=pl.CostEstimate(flops=2 * ROWS * F * F, bytes_accessed=4 * ROWS * F + 4 * F * F, transcendentals=0),
    )(hidden, weights)


def mix(shares, rows):
    return pl.pallas_call(
        mix_kernel,
        out_shape=shape((TOK, D)),
        in_specs=[WHOLE] * 2,
        out_specs=WHOLE,
        compiler_params=params(8),
    )(shares, rows)


def shift(block, by):
    return lax.ppermute(block, "y", [(i, (i + by) % Y) for i in range(Y)])


def local(tokens, routes, numerators, counts, w_gate, w_up, w_down):
    place = lax.axis_index("y").astype(jnp.int32).reshape(1)
    weights = pack(w_gate, w_up, w_down)
    weights = lax.all_gather(weights, ("z", "c")).reshape(2, MEMBERS, C, HALF + 128, SHARD)
    first, second, shares = encode(counts, routes, numerators, tokens)
    first = lax.all_to_all(first.reshape(X, SLOTS, D // 2), "x", 0, 0, tiled=True)
    second = lax.all_to_all(second.reshape(X, SLOTS, D // 2), "x", 0, 0, tiled=True)
    first_3, second_1 = shift(first, 1), shift(second, -1)
    second_3, first_1 = shift(second, 1), shift(first, -1)
    first_2, second_2 = shift(first_3, 1), shift(second_1, -1)
    rows = (first, second, first_1, second_1, first_2, second_2, first_3, second_3)
    hidden = lax.all_to_all(hidden_rows(place, rows, weights), "y", 0, 0, tiled=True)
    result = lax.all_to_all(down_rows(hidden, weights), ("x", "y"), 0, 0, tiled=True)
    return mix(shares, result)


def solution(mesh):
    grid = Mesh(mesh.devices.reshape(Y, C, X, Z), ("y", "c", "x", "z"))
    tokens = ("y", "c", "x", "z")
    group = ("x", "z")
    placed = (
        P(tokens, None),
        P(tokens, None),
        P(tokens, None),
        P(tokens),
        P(group, None),
        P(group, None),
        P(None, group),
    )
    return jax.shard_map(local, mesh=grid, in_specs=placed, out_specs=P(tokens, None), check_vma=False)
```

```python
import jax
import jax.numpy as jnp
from jax import lax
from jax.experimental import pallas as pl
from jax.experimental.pallas import tpu as pltpu
from jax.sharding import Mesh
from jax.sharding import PartitionSpec as P

Y, C, X, Z = 4, 2, 4, 16
D, F, TOK = 4096, 1024, 64
SHARD = 512
MEMBERS = 8
CAP = 20
SLOTS = 2 * CAP
MAIN = 16
REST = SLOTS - 2 * MAIN
LEAD = MAIN + REST
SRC = Y * X
ROWS = SRC * SLOTS
ALL_SLOTS = X * SLOTS
FQ = F // Y
HALF = SHARD // 2
DEEP = 2
WIDE = 2


def slot_at(at):
    second = (at >= MAIN + REST // 2).astype(jnp.int32)
    slot = jnp.where(at < MAIN + REST // 2, at, jnp.where(at < LEAD, at - REST // 2, at - LEAD))
    return second, slot


def pack_kernel(gate_ref, up_ref, down_ref, out_ref, packed, sems):
    y, c = lax.axis_index("y"), lax.axis_index("c")
    rows = pl.ds(pl.multiple_of(c * HALF, HALF), HALF)
    columns = pl.ds(pl.multiple_of(y * FQ, FQ), FQ)
    copies = [
        pltpu.make_async_copy(gate_ref.at[rows, columns], packed.at[:HALF, :FQ], sems.at[0]),
        pltpu.make_async_copy(up_ref.at[rows, columns], packed.at[:HALF, FQ:], sems.at[1]),
    ]
    columns = pl.ds(pl.multiple_of(y * 128, 128), 128)
    for quarter in range(Y):
        rows = pl.ds(pl.multiple_of(quarter * FQ + c * 128, 128), 128)
        to = packed.at[HALF:, quarter * 128 : (quarter + 1) * 128]
        copies.append(pltpu.make_async_copy(down_ref.at[rows, columns], to, sems.at[2 + quarter]))
    for copy in copies:
        copy.start()
    for copy in copies:
        copy.wait()
    copy = pltpu.make_async_copy(packed, out_ref, sems.at[2 + Y])
    copy.start()
    copy.wait()


def restore(v):
    scale = (jnp.max(jnp.abs(v), axis=1, keepdims=True) + 1e-06) / 448.0
    scaled = v / scale
    x = jnp.abs(scaled)
    spacing = jnp.full_like(x, 2.0**-9)
    for shift, least in ((8, 2.0**2), (4, 2.0**-2), (2, 2.0**-4), (1, 2.0**-5)):
        big = x >= least
        x = jnp.where(big, x * 2.0**-shift, x)
        spacing = jnp.where(big, spacing * 2.0**shift, spacing)
    snapped = jnp.floor(x * 512.0 + 0.5) * spacing
    coded = jnp.where(scaled < 0.0, -snapped, snapped)
    return (coded * scale).astype(jnp.bfloat16)


def placements(count_ref, columns_ref):
    dims = (ALL_SLOTS, TOK)
    place = lax.broadcasted_iota(jnp.int32, dims, 0)
    row = lax.broadcasted_iota(jnp.int32, dims, 1)
    column = (place * 1639) >> 16
    second, slot = slot_at(place - column * SLOTS)
    expert = 2 * column + second
    live = row < count_ref[0]
    by_first, by_second = ((columns_ref[i : i + 1, :] == expert) & live for i in range(2))
    named = (by_first | by_second).astype(jnp.float32).astype(jnp.bfloat16)
    earlier = (lax.broadcasted_iota(jnp.int32, (TOK, TOK), 0) < lax.broadcasted_iota(jnp.int32, (TOK, TOK), 1))
    rank = jnp.dot(named, earlier.astype(jnp.float32).astype(jnp.bfloat16), preferred_element_type=jnp.float32)
    here = rank.astype(jnp.int32) == slot
    return by_first & here, by_second & here


def encode_kernel(count_ref, columns_ref, numerators_ref, tokens_ref, first_ref, second_ref, shares_ref):
    by_first, by_second = placements(count_ref, columns_ref)
    chosen = (by_first | by_second).astype(jnp.float32).astype(jnp.bfloat16)
    share = numerators_ref[...].astype(jnp.float32) / 256.0
    shares = jnp.where(by_first, share[0:1], 0.0) + jnp.where(by_second, share[1:2], 0.0)
    shares_ref[...] = shares.astype(jnp.bfloat16)

    def step(member, carry):
        for half, out_ref in enumerate((first_ref, second_ref)):
            start = pl.multiple_of(member * SHARD + half * HALF, HALF)
            values = tokens_ref[:, pl.ds(start, HALF)].astype(jnp.float32)
            restored = jnp.concatenate([restore(values[:, b * 128 : (b + 1) * 128]) for b in range(HALF // 128)], axis=1)
            rows = jnp.dot(chosen, restored, preferred_element_type=jnp.float32)
            out_ref[:, pl.ds(pl.multiple_of(member * HALF, HALF), HALF)] = rows.astype(jnp.bfloat16)
        return carry

    lax.fori_loop(0, MEMBERS, step, 0)


def mix_kernel(shares_ref, rows_ref, out_ref):
    shares = shares_ref[...]
    for quarter in range(Y):
        rows = jnp.concatenate([rows_ref[x * Y + quarter] for x in range(X)], axis=0)
        mixed = lax.dot_general(shares, rows, (((0,), (0,)), ((), ())), preferred_element_type=jnp.float32)
        mixed = mixed.astype(jnp.bfloat16)
        for member in range(MEMBERS):
            at = member * SHARD + quarter * 128
            out_ref[:, at : at + 128] = mixed[:, member * 128 : (member + 1) * 128]


def split_rows(block):
    wide = block.astype(jnp.float32)
    n = wide.shape[-1]
    mixed = wide[:, MAIN:LEAD].reshape(-1, 2, REST, n)
    even, odd = mixed[:, 0], mixed[:, 1]
    low = lax.broadcasted_iota(jnp.int32, even.shape, 1) < REST // 2
    rest = (jnp.where(low, even, swap_halves(odd)), jnp.where(low, swap_halves(even), odd))
    return [
        (wide[:, e * LEAD : e * LEAD + MAIN].reshape(-1, n).astype(jnp.bfloat16), rest[e].reshape(-1, n).astype(jnp.bfloat16))
        for e in range(2)
    ]


def swap_halves(rows):
    return jnp.concatenate([rows[:, REST // 2 :], rows[:, : REST // 2]], axis=1)


def join_rows(first, second):
    main = SRC * MAIN
    n = first.shape[-1]
    one, two = (rows[main:].reshape(-1, REST, n) for rows in (first, second))
    low = lax.broadcasted_iota(jnp.int32, one.shape, 1) < REST // 2
    even, odd = jnp.where(low, one, swap_halves(two)), jnp.where(low, swap_halves(one), two)
    mixed = jnp.stack([even, odd], axis=1).reshape(SRC, REST, n)
    runs = [rows[:main].reshape(SRC, MAIN, n) for rows in (first, second)]
    return jnp.concatenate([runs[0], mixed, runs[1]], axis=1).astype(jnp.bfloat16)


def swish(total):
    gate = total[:, :FQ]
    return gate / (1.0 + jnp.exp(-gate)) * total[:, FQ:]


def hidden_kernel(place_ref, *refs):
    rows, weights_ref, out_ref, held, here, sems, row_sems = refs[: 2 * Y], *refs[2 * Y : 2 * Y + 6]
    sums = refs[2 * Y + 6 :]
    groups = MEMBERS // DEEP
    copies = [
        pltpu.make_async_copy(
            weights_ref.at[:, (i % groups) * DEEP : (i % groups + 1) * DEEP, i // groups, :HALF], held.at[i], sems.at[i]
        )
        for i in range(C * groups)
    ]
    moves = [pltpu.make_async_copy(ref, here.at[i], row_sems.at[i]) for i, ref in enumerate(rows)]
    copies[0].start()
    for move in moves[0::2]:
        move.start()
    copies[1].start()
    for move in moves[1::2]:
        move.start()
    copies[2].start()
    for i, copy in enumerate(copies):
        half, group = i // groups, i % groups
        at = slice(group * DEEP * HALF, (group + 1) * DEEP * HALF)
        if group == 0:
            for move in moves[half::2]:
                move.wait()
        blocks = [split_rows(here[2 * offset + half, :, :, at]) for offset in range(Y)]
        copy.wait()
        if i + 3 < len(copies):
            copies[i + 3].start()
        for expert, total in enumerate(sums):
            block = jnp.concatenate([b[expert][part] for part in range(2) for b in blocks], axis=0)
            weights = held[i, expert].reshape(DEEP * HALF, 2 * FQ)
            product = jnp.dot(block, weights, preferred_element_type=jnp.float32)
            total[...] = product if i == 0 else total[...] + product
    for expert, total in enumerate(sums):
        hidden = swish(total[...]).astype(jnp.bfloat16)
        for start, length in ((0, X * MAIN), (SRC * MAIN, X * REST // 2)):
            for offset in range(Y):
                source = lax.rem(place_ref[0] + offset, Y)
                to = pl.ds(pl.multiple_of(start + source * length, length), length)
                block = hidden[start + offset * length : start + (offset + 1) * length]
                for copy in range(Y):
                    out_ref[copy, expert, to] = block


def down_kernel(hidden_ref, weights_ref, out_ref, held, sems):
    starts = range(0, MEMBERS, WIDE)
    copies = [
        pltpu.make_async_copy(weights_ref.at[:, start : start + WIDE, :, HALF:], held.at[i], sems.at[i])
        for i, start in enumerate(starts)
    ]
    for copy in copies:
        copy.start()
    rows = [jnp.concatenate([hidden_ref[q, expert] for q in range(Y)], axis=1) for expert in range(2)]

    def result(i, expert):
        weights = jnp.concatenate(
            [
                jnp.concatenate([held[i, expert, m, half, :, q * 128 : (q + 1) * 128] for m in range(WIDE)], axis=1)
                for q in range(Y)
                for half in range(C)
            ],
            axis=0,
        )
        return jnp.dot(rows[expert], weights, preferred_element_type=jnp.float32)

    for i, start in enumerate(starts):
        copies[i].wait()
        joined = join_rows(result(i, 0), result(i, 1))
        for x in range(X):
            for y in range(Y):
                out_ref[x * Y + y, :, start * 128 : (start + WIDE) * 128] = joined[y * X + x]


SCALAR = pl.BlockSpec(memory_space=pltpu.SMEM)
WHOLE = pl.BlockSpec(memory_space=pltpu.VMEM)
ANY = pl.BlockSpec(memory_space=pl.ANY)


def shape(dims):
    return jax.ShapeDtypeStruct(dims, jnp.bfloat16)


def params(mebibytes):
    return pltpu.CompilerParams(vmem_limit_bytes=mebibytes << 20)


def encode(counts, routes, numerators, tokens):
    return pl.pallas_call(
        encode_kernel,
        out_shape=[*[shape((ALL_SLOTS, D // 2))] * 2, shape((ALL_SLOTS, TOK))],
        in_specs=[SCALAR, *[WHOLE] * 3],
        out_specs=[WHOLE] * 3,
        compiler_params=params(8),
        cost_estimate=pl.CostEstimate(flops=2 * ALL_SLOTS * TOK * D, bytes_accessed=2 * (TOK + ALL_SLOTS) * D, transcendentals=0),
    )(counts, routes.T, numerators.T, tokens)


def pack(w_gate, w_up, w_down):
    return pl.pallas_call(
        pack_kernel,
        out_shape=shape((HALF + 128, SHARD)),
        in_specs=[ANY] * 3,
        out_specs=ANY,
        scratch_shapes=[pltpu.VMEM((HALF + 128, SHARD), jnp.bfloat16), pltpu.SemaphoreType.DMA((3 + Y,))],
    )(w_gate, w_up, w_down)


def hidden_rows(place, rows, weights):
    pieces = C * MEMBERS // DEEP
    return pl.pallas_call(
        hidden_kernel,
        out_shape=shape((Y, 2, ROWS // 2, FQ)),
        in_specs=[SCALAR, *[ANY] * (2 * Y), ANY],
        out_specs=WHOLE,
        scratch_shapes=[
            pltpu.VMEM((pieces, 2, DEEP, HALF, 2 * FQ), jnp.bfloat16),
            pltpu.VMEM((2 * Y, X, SLOTS, D // 2), jnp.bfloat16),
            pltpu.SemaphoreType.DMA((pieces,)),
            pltpu.SemaphoreType.DMA((2 * Y,)),
            *[pltpu.VMEM((SRC * SLOTS // 2, 2 * FQ), jnp.float32)] * 2,
        ],
        compiler_params=params(36),
        cost_estimate=pl.CostEstimate(flops=2 * ROWS * D * 2 * FQ, bytes_accessed=2 * ROWS * D + 8 * D * FQ, transcendentals=0),
    )(place, *rows, weights)


def down_rows(hidden, weights):
    pieces = MEMBERS // WIDE
    return pl.pallas_call(
        down_kernel,
        out_shape=shape((SRC, SLOTS, MEMBERS * 128)),
        in_specs=[WHOLE, ANY],
        out_specs=WHOLE,
        scratch_shapes=[
            pltpu.VMEM((pieces, 2, WIDE, C, 128, SHARD), jnp.bfloat16),
            pltpu.SemaphoreType.DMA((pieces,)),
        ],
        compiler_params=params(50),
        cost_estimate=pl.CostEstimate(flops=2 * ROWS * F * F, bytes_accessed=4 * ROWS * F + 4 * F * F, transcendentals=0),
    )(hidden, weights)


def mix(shares, rows):
    return pl.pallas_call(
        mix_kernel,
        out_shape=shape((TOK, D)),
        in_specs=[WHOLE] * 2,
        out_specs=WHOLE,
        compiler_params=params(8),
    )(shares, rows)


def shift(block, by):
    return lax.ppermute(block, "y", [(i, (i + by) % Y) for i in range(Y)])


def local(tokens, routes, numerators, counts, w_gate, w_up, w_down):
    place = lax.axis_index("y").astype(jnp.int32).reshape(1)
    weights = pack(w_gate, w_up, w_down)
    weights = lax.all_gather(weights, ("z", "c")).reshape(2, MEMBERS, C, HALF + 128, SHARD)
    first, second, shares = encode(counts, routes, numerators, tokens)
    first = lax.all_to_all(first.reshape(X, SLOTS, D // 2), "x", 0, 0, tiled=True)
    second = lax.all_to_all(second.reshape(X, SLOTS, D // 2), "x", 0, 0, tiled=True)
    first_3, second_1 = shift(first, 1), shift(second, -1)
    second_3, first_1 = shift(second, 1), shift(first, -1)
    first_2, second_2 = shift(first_3, 1), shift(second_1, -1)
    rows = (first, second, first_1, second_1, first_2, second_2, first_3, second_3)
    hidden = lax.all_to_all(hidden_rows(place, rows, weights), "y", 0, 0, tiled=True)
    result = lax.all_to_all(down_rows(hidden, weights), ("x", "y"), 0, 0, tiled=True)
    return mix(shares, result)


def solution(mesh):
    grid = Mesh(mesh.devices.reshape(Y, C, X, Z), ("y", "c", "x", "z"))
    tokens = ("y", "c", "x", "z")
    group = ("x", "z")
    placed = (
        P(tokens, None),
        P(tokens, None),
        P(tokens, None),
        P(tokens),
        P(group, None),
        P(group, None),
        P(None, group),
    )
    return jax.shard_map(local, mesh=grid, in_specs=placed, out_specs=P(tokens, None), check_vma=False)
```

```python
import jax
import jax.numpy as jnp
from jax import lax
from jax.experimental import pallas as pl
from jax.experimental.pallas import tpu as pltpu
from jax.sharding import Mesh
from jax.sharding import PartitionSpec as P

Y, C, X, Z = 4, 2, 4, 16
D, F, TOK = 4096, 1024, 64
SHARD = 512
MEMBERS = 8
CAP = 20
SLOTS = 2 * CAP
MAIN = 16
REST = SLOTS - 2 * MAIN
LEAD = MAIN + REST
SRC = Y * X
ROWS = SRC * SLOTS
ALL_SLOTS = X * SLOTS
FQ = F // Y
HALF = SHARD // 2
DEEP = 2
WIDE = 2


def slot_at(at):
    second = (at >= MAIN + REST // 2).astype(jnp.int32)
    slot = jnp.where(at < MAIN + REST // 2, at, jnp.where(at < LEAD, at - REST // 2, at - LEAD))
    return second, slot


def pack_kernel(gate_ref, up_ref, down_ref, out_ref, packed, sems):
    y, c = lax.axis_index("y"), lax.axis_index("c")
    rows = pl.ds(pl.multiple_of(c * HALF, HALF), HALF)
    columns = pl.ds(pl.multiple_of(y * FQ, FQ), FQ)
    copies = [
        pltpu.make_async_copy(gate_ref.at[rows, columns], packed.at[:HALF, :FQ], sems.at[0]),
        pltpu.make_async_copy(up_ref.at[rows, columns], packed.at[:HALF, FQ:], sems.at[1]),
    ]
    columns = pl.ds(pl.multiple_of(y * 128, 128), 128)
    for quarter in range(Y):
        rows = pl.ds(pl.multiple_of(quarter * FQ + c * 128, 128), 128)
        to = packed.at[HALF:, quarter * 128 : (quarter + 1) * 128]
        copies.append(pltpu.make_async_copy(down_ref.at[rows, columns], to, sems.at[2 + quarter]))
    for copy in copies:
        copy.start()
    for copy in copies:
        copy.wait()
    copy = pltpu.make_async_copy(packed, out_ref, sems.at[2 + Y])
    copy.start()
    copy.wait()


def restore(v):
    scale = (jnp.max(jnp.abs(v), axis=1, keepdims=True) + 1e-06) / 448.0
    scaled = v / scale
    x = jnp.abs(scaled)
    spacing = jnp.full_like(x, 2.0**-9)
    for shift, least in ((8, 2.0**2), (4, 2.0**-2), (2, 2.0**-4), (1, 2.0**-5)):
        big = x >= least
        x = jnp.where(big, x * 2.0**-shift, x)
        spacing = jnp.where(big, spacing * 2.0**shift, spacing)
    snapped = jnp.floor(x * 512.0 + 0.5) * spacing
    coded = jnp.where(scaled < 0.0, -snapped, snapped)
    return (coded * scale).astype(jnp.bfloat16)


def placements(count_ref, columns_ref):
    dims = (ALL_SLOTS, TOK)
    place = lax.broadcasted_iota(jnp.int32, dims, 0)
    row = lax.broadcasted_iota(jnp.int32, dims, 1)
    column = (place * 1639) >> 16
    second, slot = slot_at(place - column * SLOTS)
    expert = 2 * column + second
    live = row < count_ref[0]
    by_first, by_second = ((columns_ref[i : i + 1, :] == expert) & live for i in range(2))
    named = (by_first | by_second).astype(jnp.float32).astype(jnp.bfloat16)
    earlier = (lax.broadcasted_iota(jnp.int32, (TOK, TOK), 0) < lax.broadcasted_iota(jnp.int32, (TOK, TOK), 1))
    rank = jnp.dot(named, earlier.astype(jnp.float32).astype(jnp.bfloat16), preferred_element_type=jnp.float32)
    here = rank.astype(jnp.int32) == slot
    return by_first & here, by_second & here


def encode_kernel(count_ref, columns_ref, numerators_ref, tokens_ref, first_ref, second_ref, shares_ref):
    by_first, by_second = placements(count_ref, columns_ref)
    chosen = (by_first | by_second).astype(jnp.float32).astype(jnp.bfloat16)
    share = numerators_ref[...].astype(jnp.float32) / 256.0
    shares = jnp.where(by_first, share[0:1], 0.0) + jnp.where(by_second, share[1:2], 0.0)
    shares_ref[...] = shares.astype(jnp.bfloat16)

    def step(member, carry):
        for half, out_ref in enumerate((first_ref, second_ref)):
            start = pl.multiple_of(member * SHARD + half * HALF, HALF)
            values = tokens_ref[:, pl.ds(start, HALF)].astype(jnp.float32)
            restored = jnp.concatenate([restore(values[:, b * 128 : (b + 1) * 128]) for b in range(HALF // 128)], axis=1)
            rows = jnp.dot(chosen, restored, preferred_element_type=jnp.float32)
            out_ref[:, pl.ds(pl.multiple_of(member * HALF, HALF), HALF)] = rows.astype(jnp.bfloat16)
        return carry

    lax.fori_loop(0, MEMBERS, step, 0)


def mix_kernel(shares_ref, rows_ref, out_ref, held, sems):
    shares = shares_ref[...]
    copies = []
    for i, start in enumerate(range(0, MEMBERS, WIDE)):
        for quarter in range(Y):
            rows = [rows_ref[x * Y + quarter, :, start * 128 : (start + WIDE) * 128] for x in range(X)]
            rows = jnp.concatenate(rows, axis=0)
            mixed = lax.dot_general(shares, rows, (((0,), (0,)), ((), ())), preferred_element_type=jnp.float32)
            mixed = mixed.astype(jnp.bfloat16)
            for m in range(WIDE):
                at = (start + m) * SHARD + quarter * 128
                held[:, at : at + 128] = mixed[:, m * 128 : (m + 1) * 128]
        done = slice(start * SHARD, (start + WIDE) * SHARD)
        copies.append(pltpu.make_async_copy(held.at[:, done], out_ref.at[:, done], sems.at[i]))
        copies[-1].start()
    for copy in copies:
        copy.wait()


def split_rows(block):
    wide = block.astype(jnp.float32)
    n = wide.shape[-1]
    mixed = wide[:, MAIN:LEAD].reshape(-1, 2, REST, n)
    even, odd = mixed[:, 0], mixed[:, 1]
    low = lax.broadcasted_iota(jnp.int32, even.shape, 1) < REST // 2
    rest = (jnp.where(low, even, swap_halves(odd)), jnp.where(low, swap_halves(even), odd))
    return [
        (wide[:, e * LEAD : e * LEAD + MAIN].reshape(-1, n).astype(jnp.bfloat16), rest[e].reshape(-1, n).astype(jnp.bfloat16))
        for e in range(2)
    ]


def swap_halves(rows):
    return jnp.concatenate([rows[:, REST // 2 :], rows[:, : REST // 2]], axis=1)


def join_rows(first, second):
    main = SRC * MAIN
    n = first.shape[-1]
    one, two = (rows[main:].reshape(-1, REST, n) for rows in (first, second))
    low = lax.broadcasted_iota(jnp.int32, one.shape, 1) < REST // 2
    even, odd = jnp.where(low, one, swap_halves(two)), jnp.where(low, swap_halves(one), two)
    mixed = jnp.stack([even, odd], axis=1).reshape(SRC, REST, n)
    runs = [rows[:main].reshape(SRC, MAIN, n) for rows in (first, second)]
    return jnp.concatenate([runs[0], mixed, runs[1]], axis=1).astype(jnp.bfloat16)


def swish(total):
    gate = total[:, :FQ]
    return gate / (1.0 + jnp.exp(-gate)) * total[:, FQ:]


def hidden_kernel(place_ref, *refs):
    rows, weights_ref, out_ref, held, here, sems, row_sems = refs[: 2 * Y], *refs[2 * Y : 2 * Y + 6]
    sums = refs[2 * Y + 6 :]
    groups = MEMBERS // DEEP
    copies = [
        pltpu.make_async_copy(
            weights_ref.at[:, (i % groups) * DEEP : (i % groups + 1) * DEEP, i // groups, :HALF], held.at[i], sems.at[i]
        )
        for i in range(C * groups)
    ]
    moves = [pltpu.make_async_copy(ref, here.at[i], row_sems.at[i]) for i, ref in enumerate(rows)]
    copies[0].start()
    for move in moves[0::2]:
        move.start()
    copies[1].start()
    for move in moves[1::2]:
        move.start()
    copies[2].start()
    for i, copy in enumerate(copies):
        half, group = i // groups, i % groups
        at = slice(group * DEEP * HALF, (group + 1) * DEEP * HALF)
        if group == 0:
            for move in moves[half::2]:
                move.wait()
        blocks = [split_rows(here[2 * offset + half, :, :, at]) for offset in range(Y)]
        copy.wait()
        if i + 3 < len(copies):
            copies[i + 3].start()
        for expert, total in enumerate(sums):
            block = jnp.concatenate([b[expert][part] for part in range(2) for b in blocks], axis=0)
            weights = held[i, expert].reshape(DEEP * HALF, 2 * FQ)
            product = jnp.dot(block, weights, preferred_element_type=jnp.float32)
            total[...] = product if i == 0 else total[...] + product
    for expert, total in enumerate(sums):
        hidden = swish(total[...]).astype(jnp.bfloat16)
        for start, length in ((0, X * MAIN), (SRC * MAIN, X * REST // 2)):
            for offset in range(Y):
                source = lax.rem(place_ref[0] + offset, Y)
                to = pl.ds(pl.multiple_of(start + source * length, length), length)
                block = hidden[start + offset * length : start + (offset + 1) * length]
                for copy in range(Y):
                    out_ref[copy, expert, to] = block


def down_kernel(hidden_ref, weights_ref, out_ref, held, sems):
    starts = range(0, MEMBERS, WIDE)
    copies = [
        pltpu.make_async_copy(weights_ref.at[:, start : start + WIDE, :, HALF:], held.at[i], sems.at[i])
        for i, start in enumerate(starts)
    ]
    for copy in copies:
        copy.start()
    rows = [jnp.concatenate([hidden_ref[q, expert] for q in range(Y)], axis=1) for expert in range(2)]

    def result(i, expert):
        weights = jnp.concatenate(
            [
                jnp.concatenate([held[i, expert, m, half, :, q * 128 : (q + 1) * 128] for m in range(WIDE)], axis=1)
                for q in range(Y)
                for half in range(C)
            ],
            axis=0,
        )
        return jnp.dot(rows[expert], weights, preferred_element_type=jnp.float32)

    for i, start in enumerate(starts):
        copies[i].wait()
        joined = join_rows(result(i, 0), result(i, 1))
        for x in range(X):
            for y in range(Y):
                out_ref[x * Y + y, :, start * 128 : (start + WIDE) * 128] = joined[y * X + x]


SCALAR = pl.BlockSpec(memory_space=pltpu.SMEM)
WHOLE = pl.BlockSpec(memory_space=pltpu.VMEM)
ANY = pl.BlockSpec(memory_space=pl.ANY)


def shape(dims):
    return jax.ShapeDtypeStruct(dims, jnp.bfloat16)


def params(mebibytes):
    return pltpu.CompilerParams(vmem_limit_bytes=mebibytes << 20)


def encode(counts, routes, numerators, tokens):
    return pl.pallas_call(
        encode_kernel,
        out_shape=[*[shape((ALL_SLOTS, D // 2))] * 2, shape((ALL_SLOTS, TOK))],
        in_specs=[SCALAR, *[WHOLE] * 3],
        out_specs=[WHOLE] * 3,
        compiler_params=params(8),
        cost_estimate=pl.CostEstimate(flops=2 * ALL_SLOTS * TOK * D, bytes_accessed=2 * (TOK + ALL_SLOTS) * D, transcendentals=0),
    )(counts, routes.T, numerators.T, tokens)


def pack(w_gate, w_up, w_down):
    return pl.pallas_call(
        pack_kernel,
        out_shape=shape((HALF + 128, SHARD)),
        in_specs=[ANY] * 3,
        out_specs=ANY,
        scratch_shapes=[pltpu.VMEM((HALF + 128, SHARD), jnp.bfloat16), pltpu.SemaphoreType.DMA((3 + Y,))],
    )(w_gate, w_up, w_down)


def hidden_rows(place, rows, weights):
    pieces = C * MEMBERS // DEEP
    return pl.pallas_call(
        hidden_kernel,
        out_shape=shape((Y, 2, ROWS // 2, FQ)),
        in_specs=[SCALAR, *[ANY] * (2 * Y), ANY],
        out_specs=WHOLE,
        scratch_shapes=[
            pltpu.VMEM((pieces, 2, DEEP, HALF, 2 * FQ), jnp.bfloat16),
            pltpu.VMEM((2 * Y, X, SLOTS, D // 2), jnp.bfloat16),
            pltpu.SemaphoreType.DMA((pieces,)),
            pltpu.SemaphoreType.DMA((2 * Y,)),
            *[pltpu.VMEM((SRC * SLOTS // 2, 2 * FQ), jnp.float32)] * 2,
        ],
        compiler_params=params(36),
        cost_estimate=pl.CostEstimate(flops=2 * ROWS * D * 2 * FQ, bytes_accessed=2 * ROWS * D + 8 * D * FQ, transcendentals=0),
    )(place, *rows, weights)


def down_rows(hidden, weights):
    pieces = MEMBERS // WIDE
    return pl.pallas_call(
        down_kernel,
        out_shape=shape((SRC, SLOTS, MEMBERS * 128)),
        in_specs=[WHOLE, ANY],
        out_specs=WHOLE,
        scratch_shapes=[
            pltpu.VMEM((pieces, 2, WIDE, C, 128, SHARD), jnp.bfloat16),
            pltpu.SemaphoreType.DMA((pieces,)),
        ],
        compiler_params=params(50),
        cost_estimate=pl.CostEstimate(flops=2 * ROWS * F * F, bytes_accessed=4 * ROWS * F + 4 * F * F, transcendentals=0),
    )(hidden, weights)


def mix(shares, rows):
    return pl.pallas_call(
        mix_kernel,
        out_shape=shape((TOK, D)),
        in_specs=[WHOLE] * 2,
        out_specs=ANY,
        scratch_shapes=[pltpu.VMEM((TOK, D), jnp.bfloat16), pltpu.SemaphoreType.DMA((MEMBERS // WIDE,))],
        compiler_params=params(8),
    )(shares, rows)


def shift(block, by):
    return lax.ppermute(block, "y", [(i, (i + by) % Y) for i in range(Y)])


def local(tokens, routes, numerators, counts, w_gate, w_up, w_down):
    place = lax.axis_index("y").astype(jnp.int32).reshape(1)
    weights = pack(w_gate, w_up, w_down)
    weights = lax.all_gather(weights, ("z", "c")).reshape(2, MEMBERS, C, HALF + 128, SHARD)
    first, second, shares = encode(counts, routes, numerators, tokens)
    first = lax.all_to_all(first.reshape(X, SLOTS, D // 2), "x", 0, 0, tiled=True)
    second = lax.all_to_all(second.reshape(X, SLOTS, D // 2), "x", 0, 0, tiled=True)
    first_3, second_1 = shift(first, 1), shift(second, -1)
    second_3, first_1 = shift(second, 1), shift(first, -1)
    first_2, second_2 = shift(first_3, 1), shift(second_1, -1)
    rows = (first, second, first_1, second_1, first_2, second_2, first_3, second_3)
    hidden = lax.all_to_all(hidden_rows(place, rows, weights), "y", 0, 0, tiled=True)
    result = lax.all_to_all(down_rows(hidden, weights), ("x", "y"), 0, 0, tiled=True)
    return mix(shares, result)


def solution(mesh):
    grid = Mesh(mesh.devices.reshape(Y, C, X, Z), ("y", "c", "x", "z"))
    tokens = ("y", "c", "x", "z")
    group = ("x", "z")
    placed = (
        P(tokens, None),
        P(tokens, None),
        P(tokens, None),
        P(tokens),
        P(group, None),
        P(group, None),
        P(None, group),
    )
    return jax.shard_map(local, mesh=grid, in_specs=placed, out_specs=P(tokens, None), check_vma=False)
```

```python
import jax
import jax.numpy as jnp
from jax import lax
from jax.experimental import pallas as pl
from jax.experimental.pallas import tpu as pltpu
from jax.sharding import Mesh
from jax.sharding import PartitionSpec as P

Y, C, X, Z = 4, 2, 4, 16
D, F, TOK = 4096, 1024, 64
SHARD = 512
MEMBERS = 8
CAP = 20
SLOTS = 2 * CAP
MAIN = 16
REST = SLOTS - 2 * MAIN
LEAD = MAIN + REST
SRC = Y * X
ROWS = SRC * SLOTS
ALL_SLOTS = X * SLOTS
FQ = F // Y
HALF = SHARD // 2
DEEP = 2
WIDE = 2


def slot_at(at):
    second = (at >= MAIN + REST // 2).astype(jnp.int32)
    slot = jnp.where(at < MAIN + REST // 2, at, jnp.where(at < LEAD, at - REST // 2, at - LEAD))
    return second, slot


def pack_kernel(gate_ref, up_ref, down_ref, out_ref, packed, sems):
    y, c = lax.axis_index("y"), lax.axis_index("c")
    rows = pl.ds(pl.multiple_of(c * HALF, HALF), HALF)
    columns = pl.ds(pl.multiple_of(y * FQ, FQ), FQ)
    copies = [
        pltpu.make_async_copy(gate_ref.at[rows, columns], packed.at[:HALF, :FQ], sems.at[0]),
        pltpu.make_async_copy(up_ref.at[rows, columns], packed.at[:HALF, FQ:], sems.at[1]),
    ]
    columns = pl.ds(pl.multiple_of(y * 128, 128), 128)
    for quarter in range(Y):
        rows = pl.ds(pl.multiple_of(quarter * FQ + c * 128, 128), 128)
        to = packed.at[HALF:, quarter * 128 : (quarter + 1) * 128]
        copies.append(pltpu.make_async_copy(down_ref.at[rows, columns], to, sems.at[2 + quarter]))
    for copy in copies:
        copy.start()
    for copy in copies:
        copy.wait()
    copy = pltpu.make_async_copy(packed, out_ref, sems.at[2 + Y])
    copy.start()
    copy.wait()


def restore(v):
    scale = (jnp.max(jnp.abs(v), axis=1, keepdims=True) + 1e-06) / 448.0
    scaled = v / scale
    x = jnp.abs(scaled)
    spacing = jnp.full_like(x, 2.0**-9)
    for shift, least in ((8, 2.0**2), (4, 2.0**-2), (2, 2.0**-4), (1, 2.0**-5)):
        big = x >= least
        x = jnp.where(big, x * 2.0**-shift, x)
        spacing = jnp.where(big, spacing * 2.0**shift, spacing)
    snapped = jnp.floor(x * 512.0 + 0.5) * spacing
    coded = jnp.where(scaled < 0.0, -snapped, snapped)
    return (coded * scale).astype(jnp.bfloat16)


def placements(count_ref, columns_ref):
    dims = (ALL_SLOTS, TOK)
    place = lax.broadcasted_iota(jnp.int32, dims, 0)
    row = lax.broadcasted_iota(jnp.int32, dims, 1)
    column = (place * 1639) >> 16
    second, slot = slot_at(place - column * SLOTS)
    expert = 2 * column + second
    live = row < count_ref[0]
    by_first, by_second = ((columns_ref[i : i + 1, :] == expert) & live for i in range(2))
    named = (by_first | by_second).astype(jnp.float32).astype(jnp.bfloat16)
    earlier = (lax.broadcasted_iota(jnp.int32, (TOK, TOK), 0) < lax.broadcasted_iota(jnp.int32, (TOK, TOK), 1))
    rank = jnp.dot(named, earlier.astype(jnp.float32).astype(jnp.bfloat16), preferred_element_type=jnp.float32)
    here = rank.astype(jnp.int32) == slot
    return by_first & here, by_second & here


def encode_kernel(count_ref, columns_ref, numerators_ref, tokens_ref, first_ref, second_ref, shares_ref):
    by_first, by_second = placements(count_ref, columns_ref)
    chosen = (by_first | by_second).astype(jnp.float32).astype(jnp.bfloat16)
    share = numerators_ref[...].astype(jnp.float32) / 256.0
    shares = jnp.where(by_first, share[0:1], 0.0) + jnp.where(by_second, share[1:2], 0.0)
    shares_ref[...] = shares.astype(jnp.bfloat16)

    def step(member, carry):
        for half, out_ref in enumerate((first_ref, second_ref)):
            start = pl.multiple_of(member * SHARD + half * HALF, HALF)
            values = tokens_ref[:, pl.ds(start, HALF)].astype(jnp.float32)
            restored = jnp.concatenate([restore(values[:, b * 128 : (b + 1) * 128]) for b in range(HALF // 128)], axis=1)
            rows = jnp.dot(chosen, restored, preferred_element_type=jnp.float32)
            out_ref[:, pl.ds(pl.multiple_of(member * HALF, HALF), HALF)] = rows.astype(jnp.bfloat16)
        return carry

    lax.fori_loop(0, MEMBERS, step, 0)


def mix_kernel(shares_ref, rows_ref, out_ref, held, sems):
    shares = shares_ref[...]
    copies = []
    for i, start in enumerate(range(0, MEMBERS, WIDE)):
        for quarter in range(Y):
            rows = [rows_ref[x * Y + quarter, :, start * 128 : (start + WIDE) * 128] for x in range(X)]
            rows = jnp.concatenate(rows, axis=0)
            mixed = lax.dot_general(shares, rows, (((0,), (0,)), ((), ())), preferred_element_type=jnp.float32)
            mixed = mixed.astype(jnp.bfloat16)
            for m in range(WIDE):
                at = (start + m) * SHARD + quarter * 128
                held[:, at : at + 128] = mixed[:, m * 128 : (m + 1) * 128]
        done = slice(start * SHARD, (start + WIDE) * SHARD)
        copies.append(pltpu.make_async_copy(held.at[:, done], out_ref.at[:, done], sems.at[i]))
        copies[-1].start()
    for copy in copies:
        copy.wait()


def split_rows(block):
    wide = block.astype(jnp.float32)
    n = wide.shape[-1]
    mixed = wide[:, MAIN:LEAD].reshape(-1, 2, REST, n)
    even, odd = mixed[:, 0], mixed[:, 1]
    low = lax.broadcasted_iota(jnp.int32, even.shape, 1) < REST // 2
    rest = (jnp.where(low, even, swap_halves(odd)), jnp.where(low, swap_halves(even), odd))
    return [
        (wide[:, e * LEAD : e * LEAD + MAIN].reshape(-1, n).astype(jnp.bfloat16), rest[e].reshape(-1, n).astype(jnp.bfloat16))
        for e in range(2)
    ]


def swap_halves(rows):
    return jnp.concatenate([rows[:, REST // 2 :], rows[:, : REST // 2]], axis=1)


def join_rows(first, second):
    main = SRC * MAIN
    n = first.shape[-1]
    one, two = (rows[main:].reshape(-1, REST, n) for rows in (first, second))
    low = lax.broadcasted_iota(jnp.int32, one.shape, 1) < REST // 2
    even, odd = jnp.where(low, one, swap_halves(two)), jnp.where(low, swap_halves(one), two)
    mixed = jnp.stack([even, odd], axis=1).reshape(SRC, REST, n)
    runs = [rows[:main].reshape(SRC, MAIN, n) for rows in (first, second)]
    return jnp.concatenate([runs[0], mixed, runs[1]], axis=1).astype(jnp.bfloat16)


def swish(total):
    gate = total[:, :FQ]
    return gate / (1.0 + jnp.exp(-gate)) * total[:, FQ:]


def hidden_kernel(place_ref, *refs):
    rows, weights_ref, out_ref, down_ref, held, here, sems, row_sems = refs[: 2 * Y], *refs[2 * Y : 2 * Y + 7]
    sums = refs[2 * Y + 7 :]
    groups = MEMBERS // DEEP
    copies = [
        pltpu.make_async_copy(
            weights_ref.at[:, (i % groups) * DEEP : (i % groups + 1) * DEEP, i // groups, :HALF], held.at[i], sems.at[i]
        )
        for i in range(C * groups)
    ]
    moves = [pltpu.make_async_copy(ref, here.at[i], row_sems.at[i]) for i, ref in enumerate(rows)]
    copies[0].start()
    for move in moves[0::2]:
        move.start()
    copies[1].start()
    for move in moves[1::2]:
        move.start()
    copies[2].start()
    for i, copy in enumerate(copies):
        half, group = i // groups, i % groups
        at = slice(group * DEEP * HALF, (group + 1) * DEEP * HALF)
        if group == 0:
            for move in moves[half::2]:
                move.wait()
        blocks = [split_rows(here[2 * offset + half, :, :, at]) for offset in range(Y)]
        copy.wait()
        if i + 3 < len(copies):
            copies[i + 3].start()
        elif i + 3 == len(copies):
            down_copy = pltpu.make_async_copy(weights_ref.at[:, :WIDE, :, HALF:], down_ref, sems.at[len(copies)])
            down_copy.start()
        for expert, total in enumerate(sums):
            block = jnp.concatenate([b[expert][part] for part in range(2) for b in blocks], axis=0)
            weights = held[i, expert].reshape(DEEP * HALF, 2 * FQ)
            product = jnp.dot(block, weights, preferred_element_type=jnp.float32)
            total[...] = product if i == 0 else total[...] + product
    for expert, total in enumerate(sums):
        hidden = swish(total[...]).astype(jnp.bfloat16)
        for start, length in ((0, X * MAIN), (SRC * MAIN, X * REST // 2)):
            for offset in range(Y):
                source = lax.rem(place_ref[0] + offset, Y)
                to = pl.ds(pl.multiple_of(start + source * length, length), length)
                block = hidden[start + offset * length : start + (offset + 1) * length]
                for copy in range(Y):
                    out_ref[copy, expert, to] = block
    down_copy.wait()


def down_kernel(hidden_ref, piece_ref, weights_ref, out_ref, held, sems):
    starts = range(0, MEMBERS, WIDE)
    copies = [
        pltpu.make_async_copy(weights_ref.at[:, start : start + WIDE, :, HALF:], held.at[i], sems.at[i])
        for i, start in enumerate(starts[1:])
    ]
    for copy in copies:
        copy.start()
    rows = [jnp.concatenate([hidden_ref[q, expert] for q in range(Y)], axis=1) for expert in range(2)]

    def result(i, expert):
        piece = held.at[i - 1] if i else piece_ref
        weights = jnp.concatenate(
            [
                jnp.concatenate([piece[expert, m, half, :, q * 128 : (q + 1) * 128] for m in range(WIDE)], axis=1)
                for q in range(Y)
                for half in range(C)
            ],
            axis=0,
        )
        return jnp.dot(rows[expert], weights, preferred_element_type=jnp.float32)

    for i, start in enumerate(starts):
        if i:
            copies[i - 1].wait()
        joined = join_rows(result(i, 0), result(i, 1))
        for x in range(X):
            for y in range(Y):
                out_ref[x * Y + y, :, start * 128 : (start + WIDE) * 128] = joined[y * X + x]


SCALAR = pl.BlockSpec(memory_space=pltpu.SMEM)
WHOLE = pl.BlockSpec(memory_space=pltpu.VMEM)
ANY = pl.BlockSpec(memory_space=pl.ANY)


def shape(dims):
    return jax.ShapeDtypeStruct(dims, jnp.bfloat16)


def params(mebibytes):
    return pltpu.CompilerParams(vmem_limit_bytes=mebibytes << 20)


def encode(counts, routes, numerators, tokens):
    return pl.pallas_call(
        encode_kernel,
        out_shape=[*[shape((ALL_SLOTS, D // 2))] * 2, shape((ALL_SLOTS, TOK))],
        in_specs=[SCALAR, *[WHOLE] * 3],
        out_specs=[WHOLE] * 3,
        compiler_params=params(8),
        cost_estimate=pl.CostEstimate(flops=2 * ALL_SLOTS * TOK * D, bytes_accessed=2 * (TOK + ALL_SLOTS) * D, transcendentals=0),
    )(counts, routes.T, numerators.T, tokens)


def pack(w_gate, w_up, w_down):
    return pl.pallas_call(
        pack_kernel,
        out_shape=shape((HALF + 128, SHARD)),
        in_specs=[ANY] * 3,
        out_specs=ANY,
        scratch_shapes=[pltpu.VMEM((HALF + 128, SHARD), jnp.bfloat16), pltpu.SemaphoreType.DMA((3 + Y,))],
    )(w_gate, w_up, w_down)


def hidden_rows(place, rows, weights):
    pieces = C * MEMBERS // DEEP
    return pl.pallas_call(
        hidden_kernel,
        out_shape=[shape((Y, 2, ROWS // 2, FQ)), shape((2, WIDE, C, 128, SHARD))],
        in_specs=[SCALAR, *[ANY] * (2 * Y), ANY],
        out_specs=[WHOLE] * 2,
        scratch_shapes=[
            pltpu.VMEM((pieces, 2, DEEP, HALF, 2 * FQ), jnp.bfloat16),
            pltpu.VMEM((2 * Y, X, SLOTS, D // 2), jnp.bfloat16),
            pltpu.SemaphoreType.DMA((pieces + 1,)),
            pltpu.SemaphoreType.DMA((2 * Y,)),
            *[pltpu.VMEM((SRC * SLOTS // 2, 2 * FQ), jnp.float32)] * 2,
        ],
        compiler_params=params(36),
        cost_estimate=pl.CostEstimate(flops=2 * ROWS * D * 2 * FQ, bytes_accessed=2 * ROWS * D + 8 * D * FQ, transcendentals=0),
    )(place, *rows, weights)


def down_rows(hidden, piece, weights):
    pieces = MEMBERS // WIDE - 1
    return pl.pallas_call(
        down_kernel,
        out_shape=shape((SRC, SLOTS, MEMBERS * 128)),
        in_specs=[WHOLE, WHOLE, ANY],
        out_specs=WHOLE,
        scratch_shapes=[
            pltpu.VMEM((pieces, 2, WIDE, C, 128, SHARD), jnp.bfloat16),
            pltpu.SemaphoreType.DMA((pieces,)),
        ],
        compiler_params=params(50),
        cost_estimate=pl.CostEstimate(flops=2 * ROWS * F * F, bytes_accessed=4 * ROWS * F + 4 * F * F, transcendentals=0),
    )(hidden, piece, weights)


def mix(shares, rows):
    return pl.pallas_call(
        mix_kernel,
        out_shape=shape((TOK, D)),
        in_specs=[WHOLE] * 2,
        out_specs=ANY,
        scratch_shapes=[pltpu.VMEM((TOK, D), jnp.bfloat16), pltpu.SemaphoreType.DMA((MEMBERS // WIDE,))],
        compiler_params=params(8),
    )(shares, rows)


def shift(block, by):
    return lax.ppermute(block, "y", [(i, (i + by) % Y) for i in range(Y)])


def local(tokens, routes, numerators, counts, w_gate, w_up, w_down):
    place = lax.axis_index("y").astype(jnp.int32).reshape(1)
    weights = pack(w_gate, w_up, w_down)
    weights = lax.all_gather(weights, ("z", "c")).reshape(2, MEMBERS, C, HALF + 128, SHARD)
    first, second, shares = encode(counts, routes, numerators, tokens)
    first = lax.all_to_all(first.reshape(X, SLOTS, D // 2), "x", 0, 0, tiled=True)
    second = lax.all_to_all(second.reshape(X, SLOTS, D // 2), "x", 0, 0, tiled=True)
    first_3, second_1 = shift(first, 1), shift(second, -1)
    second_3, first_1 = shift(second, 1), shift(first, -1)
    first_2, second_2 = shift(first_3, 1), shift(second_1, -1)
    rows = (first, second, first_1, second_1, first_2, second_2, first_3, second_3)
    hidden, piece = hidden_rows(place, rows, weights)
    hidden = lax.all_to_all(hidden, "y", 0, 0, tiled=True)
    result = lax.all_to_all(down_rows(hidden, piece, weights), ("x", "y"), 0, 0, tiled=True)
    return mix(shares, result)


def solution(mesh):
    grid = Mesh(mesh.devices.reshape(Y, C, X, Z), ("y", "c", "x", "z"))
    tokens = ("y", "c", "x", "z")
    group = ("x", "z")
    placed = (
        P(tokens, None),
        P(tokens, None),
        P(tokens, None),
        P(tokens),
        P(group, None),
        P(group, None),
        P(None, group),
    )
    return jax.shard_map(local, mesh=grid, in_specs=placed, out_specs=P(tokens, None), check_vma=False)
```

```python
import jax
import jax.numpy as jnp
from jax import lax
from jax.experimental import pallas as pl
from jax.experimental.pallas import tpu as pltpu
from jax.sharding import Mesh
from jax.sharding import PartitionSpec as P

Y, C, X, Z = 4, 2, 4, 16
D, F, TOK = 4096, 1024, 64
SHARD = 512
MEMBERS = 8
CAP = 20
SLOTS = 2 * CAP
MAIN = 16
REST = SLOTS - 2 * MAIN
LEAD = MAIN + REST
SRC = Y * X
ROWS = SRC * SLOTS
ALL_SLOTS = X * SLOTS
FQ = F // Y
HALF = SHARD // 2
DEEP = 2
WIDE = 4


def slot_at(at):
    second = (at >= MAIN + REST // 2).astype(jnp.int32)
    slot = jnp.where(at < MAIN + REST // 2, at, jnp.where(at < LEAD, at - REST // 2, at - LEAD))
    return second, slot


def pack_kernel(gate_ref, up_ref, down_ref, out_ref, packed, sems):
    y, c = lax.axis_index("y"), lax.axis_index("c")
    rows = pl.ds(pl.multiple_of(c * HALF, HALF), HALF)
    columns = pl.ds(pl.multiple_of(y * FQ, FQ), FQ)
    copies = [
        pltpu.make_async_copy(gate_ref.at[rows, columns], packed.at[:HALF, :FQ], sems.at[0]),
        pltpu.make_async_copy(up_ref.at[rows, columns], packed.at[:HALF, FQ:], sems.at[1]),
    ]
    columns = pl.ds(pl.multiple_of(y * 128, 128), 128)
    for quarter in range(Y):
        rows = pl.ds(pl.multiple_of(quarter * FQ + c * 128, 128), 128)
        to = packed.at[HALF:, quarter * 128 : (quarter + 1) * 128]
        copies.append(pltpu.make_async_copy(down_ref.at[rows, columns], to, sems.at[2 + quarter]))
    for copy in copies:
        copy.start()
    for copy in copies:
        copy.wait()
    copy = pltpu.make_async_copy(packed, out_ref, sems.at[2 + Y])
    copy.start()
    copy.wait()


def restore(v):
    scale = (jnp.max(jnp.abs(v), axis=1, keepdims=True) + 1e-06) / 448.0
    scaled = v / scale
    x = jnp.abs(scaled)
    spacing = jnp.full_like(x, 2.0**-9)
    for shift, least in ((8, 2.0**2), (4, 2.0**-2), (2, 2.0**-4), (1, 2.0**-5)):
        big = x >= least
        x = jnp.where(big, x * 2.0**-shift, x)
        spacing = jnp.where(big, spacing * 2.0**shift, spacing)
    snapped = jnp.floor(x * 512.0 + 0.5) * spacing
    coded = jnp.where(scaled < 0.0, -snapped, snapped)
    return (coded * scale).astype(jnp.bfloat16)


def placements(count_ref, columns_ref):
    dims = (ALL_SLOTS, TOK)
    place = lax.broadcasted_iota(jnp.int32, dims, 0)
    row = lax.broadcasted_iota(jnp.int32, dims, 1)
    column = (place * 1639) >> 16
    second, slot = slot_at(place - column * SLOTS)
    expert = 2 * column + second
    live = row < count_ref[0]
    by_first, by_second = ((columns_ref[i : i + 1, :] == expert) & live for i in range(2))
    named = (by_first | by_second).astype(jnp.float32).astype(jnp.bfloat16)
    earlier = (lax.broadcasted_iota(jnp.int32, (TOK, TOK), 0) < lax.broadcasted_iota(jnp.int32, (TOK, TOK), 1))
    rank = jnp.dot(named, earlier.astype(jnp.float32).astype(jnp.bfloat16), preferred_element_type=jnp.float32)
    here = rank.astype(jnp.int32) == slot
    return by_first & here, by_second & here


def encode_kernel(count_ref, columns_ref, numerators_ref, tokens_ref, first_ref, second_ref, shares_ref):
    by_first, by_second = placements(count_ref, columns_ref)
    chosen = (by_first | by_second).astype(jnp.float32).astype(jnp.bfloat16)
    share = numerators_ref[...].astype(jnp.float32) / 256.0
    shares = jnp.where(by_first, share[0:1], 0.0) + jnp.where(by_second, share[1:2], 0.0)
    shares_ref[...] = shares.astype(jnp.bfloat16)

    def step(member, carry):
        for half, out_ref in enumerate((first_ref, second_ref)):
            start = pl.multiple_of(member * SHARD + half * HALF, HALF)
            values = tokens_ref[:, pl.ds(start, HALF)].astype(jnp.float32)
            restored = jnp.concatenate([restore(values[:, b * 128 : (b + 1) * 128]) for b in range(HALF // 128)], axis=1)
            rows = jnp.dot(chosen, restored, preferred_element_type=jnp.float32)
            out_ref[:, pl.ds(pl.multiple_of(member * HALF, HALF), HALF)] = rows.astype(jnp.bfloat16)
        return carry

    lax.fori_loop(0, MEMBERS, step, 0)


def mix_kernel(shares_ref, rows_ref, out_ref, held, sems):
    shares = shares_ref[...]
    copies = []
    for i, start in enumerate(range(0, MEMBERS, WIDE)):
        for quarter in range(Y):
            rows = [rows_ref[x * Y + quarter, :, start * 128 : (start + WIDE) * 128] for x in range(X)]
            rows = jnp.concatenate(rows, axis=0)
            mixed = lax.dot_general(shares, rows, (((0,), (0,)), ((), ())), preferred_element_type=jnp.float32)
            mixed = mixed.astype(jnp.bfloat16)
            for m in range(WIDE):
                at = (start + m) * SHARD + quarter * 128
                held[:, at : at + 128] = mixed[:, m * 128 : (m + 1) * 128]
        done = slice(start * SHARD, (start + WIDE) * SHARD)
        copies.append(pltpu.make_async_copy(held.at[:, done], out_ref.at[:, done], sems.at[i]))
        copies[-1].start()
    for copy in copies:
        copy.wait()


def split_rows(block):
    wide = block.astype(jnp.float32)
    n = wide.shape[-1]
    mixed = wide[:, MAIN:LEAD].reshape(-1, 2, REST, n)
    even, odd = mixed[:, 0], mixed[:, 1]
    low = lax.broadcasted_iota(jnp.int32, even.shape, 1) < REST // 2
    rest = (jnp.where(low, even, swap_halves(odd)), jnp.where(low, swap_halves(even), odd))
    return [
        (wide[:, e * LEAD : e * LEAD + MAIN].reshape(-1, n).astype(jnp.bfloat16), rest[e].reshape(-1, n).astype(jnp.bfloat16))
        for e in range(2)
    ]


def swap_halves(rows):
    return jnp.concatenate([rows[:, REST // 2 :], rows[:, : REST // 2]], axis=1)


def join_rows(first, second):
    main = SRC * MAIN
    n = first.shape[-1]
    one, two = (rows[main:].reshape(-1, REST, n) for rows in (first, second))
    low = lax.broadcasted_iota(jnp.int32, one.shape, 1) < REST // 2
    even, odd = jnp.where(low, one, swap_halves(two)), jnp.where(low, swap_halves(one), two)
    mixed = jnp.stack([even, odd], axis=1).reshape(SRC, REST, n)
    runs = [rows[:main].reshape(SRC, MAIN, n) for rows in (first, second)]
    return jnp.concatenate([runs[0], mixed, runs[1]], axis=1).astype(jnp.bfloat16)


def swish(total):
    gate = total[:, :FQ]
    return gate / (1.0 + jnp.exp(-gate)) * total[:, FQ:]


def hidden_kernel(place_ref, *refs):
    rows, weights_ref, out_ref, down_ref, held, here, sems, row_sems = refs[: 2 * Y], *refs[2 * Y : 2 * Y + 7]
    sums = refs[2 * Y + 7 :]
    groups = MEMBERS // DEEP
    copies = [
        pltpu.make_async_copy(
            weights_ref.at[:, (i % groups) * DEEP : (i % groups + 1) * DEEP, i // groups, :HALF], held.at[i], sems.at[i]
        )
        for i in range(C * groups)
    ]
    moves = [pltpu.make_async_copy(ref, here.at[i], row_sems.at[i]) for i, ref in enumerate(rows)]
    copies[0].start()
    for move in moves[0::2]:
        move.start()
    copies[1].start()
    for move in moves[1::2]:
        move.start()
    copies[2].start()
    for i, copy in enumerate(copies):
        half, group = i // groups, i % groups
        at = slice(group * DEEP * HALF, (group + 1) * DEEP * HALF)
        if group == 0:
            for move in moves[half::2]:
                move.wait()
        blocks = [split_rows(here[2 * offset + half, :, :, at]) for offset in range(Y)]
        copy.wait()
        if i + 3 < len(copies):
            copies[i + 3].start()
        elif i + 3 == len(copies):
            down_copy = pltpu.make_async_copy(weights_ref.at[:, :WIDE, :, HALF:], down_ref, sems.at[len(copies)])
            down_copy.start()
        for expert, total in enumerate(sums):
            block = jnp.concatenate([b[expert][part] for part in range(2) for b in blocks], axis=0)
            weights = held[i, expert].reshape(DEEP * HALF, 2 * FQ)
            product = jnp.dot(block, weights, preferred_element_type=jnp.float32)
            total[...] = product if i == 0 else total[...] + product
    for expert, total in enumerate(sums):
        hidden = swish(total[...]).astype(jnp.bfloat16)
        for start, length in ((0, X * MAIN), (SRC * MAIN, X * REST // 2)):
            for offset in range(Y):
                source = lax.rem(place_ref[0] + offset, Y)
                to = pl.ds(pl.multiple_of(start + source * length, length), length)
                block = hidden[start + offset * length : start + (offset + 1) * length]
                for copy in range(Y):
                    out_ref[copy, expert, to] = block
    down_copy.wait()


def down_kernel(hidden_ref, piece_ref, weights_ref, out_ref, held, sems):
    starts = range(0, MEMBERS, WIDE)
    copies = [
        pltpu.make_async_copy(weights_ref.at[:, start : start + WIDE, :, HALF:], held.at[i], sems.at[i])
        for i, start in enumerate(starts[1:])
    ]
    for copy in copies:
        copy.start()
    rows = [jnp.concatenate([hidden_ref[q, expert] for q in range(Y)], axis=1) for expert in range(2)]

    def result(i, expert):
        piece = held.at[i - 1] if i else piece_ref
        weights = jnp.concatenate(
            [
                jnp.concatenate([piece[expert, m, half, :, q * 128 : (q + 1) * 128] for m in range(WIDE)], axis=1)
                for q in range(Y)
                for half in range(C)
            ],
            axis=0,
        )
        return jnp.dot(rows[expert], weights, preferred_element_type=jnp.float32)

    for i, start in enumerate(starts):
        if i:
            copies[i - 1].wait()
        joined = join_rows(result(i, 0), result(i, 1))
        for x in range(X):
            for y in range(Y):
                out_ref[x * Y + y, :, start * 128 : (start + WIDE) * 128] = joined[y * X + x]


SCALAR = pl.BlockSpec(memory_space=pltpu.SMEM)
WHOLE = pl.BlockSpec(memory_space=pltpu.VMEM)
ANY = pl.BlockSpec(memory_space=pl.ANY)


def shape(dims):
    return jax.ShapeDtypeStruct(dims, jnp.bfloat16)


def params(mebibytes):
    return pltpu.CompilerParams(vmem_limit_bytes=mebibytes << 20)


def encode(counts, routes, numerators, tokens):
    return pl.pallas_call(
        encode_kernel,
        out_shape=[*[shape((ALL_SLOTS, D // 2))] * 2, shape((ALL_SLOTS, TOK))],
        in_specs=[SCALAR, *[WHOLE] * 3],
        out_specs=[WHOLE] * 3,
        compiler_params=params(8),
        cost_estimate=pl.CostEstimate(flops=2 * ALL_SLOTS * TOK * D, bytes_accessed=2 * (TOK + ALL_SLOTS) * D, transcendentals=0),
    )(counts, routes.T, numerators.T, tokens)


def pack(w_gate, w_up, w_down):
    return pl.pallas_call(
        pack_kernel,
        out_shape=shape((HALF + 128, SHARD)),
        in_specs=[ANY] * 3,
        out_specs=ANY,
        scratch_shapes=[pltpu.VMEM((HALF + 128, SHARD), jnp.bfloat16), pltpu.SemaphoreType.DMA((3 + Y,))],
    )(w_gate, w_up, w_down)


def hidden_rows(place, rows, weights):
    pieces = C * MEMBERS // DEEP
    return pl.pallas_call(
        hidden_kernel,
        out_shape=[shape((Y, 2, ROWS // 2, FQ)), shape((2, WIDE, C, 128, SHARD))],
        in_specs=[SCALAR, *[ANY] * (2 * Y), ANY],
        out_specs=[WHOLE] * 2,
        scratch_shapes=[
            pltpu.VMEM((pieces, 2, DEEP, HALF, 2 * FQ), jnp.bfloat16),
            pltpu.VMEM((2 * Y, X, SLOTS, D // 2), jnp.bfloat16),
            pltpu.SemaphoreType.DMA((pieces + 1,)),
            pltpu.SemaphoreType.DMA((2 * Y,)),
            *[pltpu.VMEM((SRC * SLOTS // 2, 2 * FQ), jnp.float32)] * 2,
        ],
        compiler_params=params(36),
        cost_estimate=pl.CostEstimate(flops=2 * ROWS * D * 2 * FQ, bytes_accessed=2 * ROWS * D + 8 * D * FQ, transcendentals=0),
    )(place, *rows, weights)


def down_rows(hidden, piece, weights):
    pieces = MEMBERS // WIDE - 1
    return pl.pallas_call(
        down_kernel,
        out_shape=shape((SRC, SLOTS, MEMBERS * 128)),
        in_specs=[WHOLE, WHOLE, ANY],
        out_specs=WHOLE,
        scratch_shapes=[
            pltpu.VMEM((pieces, 2, WIDE, C, 128, SHARD), jnp.bfloat16),
            pltpu.SemaphoreType.DMA((pieces,)),
        ],
        compiler_params=params(50),
        cost_estimate=pl.CostEstimate(flops=2 * ROWS * F * F, bytes_accessed=4 * ROWS * F + 4 * F * F, transcendentals=0),
    )(hidden, piece, weights)


def mix(shares, rows):
    return pl.pallas_call(
        mix_kernel,
        out_shape=shape((TOK, D)),
        in_specs=[WHOLE] * 2,
        out_specs=ANY,
        scratch_shapes=[pltpu.VMEM((TOK, D), jnp.bfloat16), pltpu.SemaphoreType.DMA((MEMBERS // WIDE,))],
        compiler_params=params(8),
    )(shares, rows)


def shift(block, by):
    return lax.ppermute(block, "y", [(i, (i + by) % Y) for i in range(Y)])


def local(tokens, routes, numerators, counts, w_gate, w_up, w_down):
    place = lax.axis_index("y").astype(jnp.int32).reshape(1)
    weights = pack(w_gate, w_up, w_down)
    weights = lax.all_gather(weights, ("z", "c")).reshape(2, MEMBERS, C, HALF + 128, SHARD)
    first, second, shares = encode(counts, routes, numerators, tokens)
    first = lax.all_to_all(first.reshape(X, SLOTS, D // 2), "x", 0, 0, tiled=True)
    second = lax.all_to_all(second.reshape(X, SLOTS, D // 2), "x", 0, 0, tiled=True)
    first_3, second_1 = shift(first, 1), shift(second, -1)
    second_3, first_1 = shift(second, 1), shift(first, -1)
    first_2, second_2 = shift(first_3, 1), shift(second_1, -1)
    rows = (first, second, first_1, second_1, first_2, second_2, first_3, second_3)
    hidden, piece = hidden_rows(place, rows, weights)
    hidden = lax.all_to_all(hidden, "y", 0, 0, tiled=True)
    result = lax.all_to_all(down_rows(hidden, piece, weights), ("x", "y"), 0, 0, tiled=True)
    return mix(shares, result)


def solution(mesh):
    grid = Mesh(mesh.devices.reshape(Y, C, X, Z), ("y", "c", "x", "z"))
    tokens = ("y", "c", "x", "z")
    group = ("x", "z")
    placed = (
        P(tokens, None),
        P(tokens, None),
        P(tokens, None),
        P(tokens),
        P(group, None),
        P(group, None),
        P(None, group),
    )
    return jax.shard_map(local, mesh=grid, in_specs=placed, out_specs=P(tokens, None), check_vma=False)
```
